512 devices in a mesh: shard: 128 (over y, z, core), lane: 4 (over x).
Axes of the slice: x: 4, y: 4, z: 16, core: 2. Of those that a mesh axis runs over, the one named last changes fastest.
Arguments:
- descriptors: bfloat16 [16384, 2048], P('shard', 'lane'), may hold values from -8 to 8
- neighbours: int32 [16384, 10], P('shard'), may hold values from 0 to 16383, as said below
- owned: int32 [16384, 10], P('shard'), may hold values 0 or 1
- queries: bfloat16 [1024, 2048], P('lane'), may hold values from -6 to 6
- candidates: int32 [1024, 2], P('lane'), may hold values from 0 to 127, as said below
Outputs:
- augmented: bfloat16 [16384, 2048], P('shard', 'lane')
- scores: float32 [1024, 256], P('lane')
The draws below stay inside these ranges and needn't reach their ends.
Inputs may be any that keep to these rules, and one draw needn't show every extreme that they name: `neighbours`: of the 1280 slots of the images of one index of shard, exactly 15 name images of each of half of the shards and 5 name images of each other shard; which shards, slots and images is drawn. `candidates`: every block number is named by exactly 16 of the 2048 entries; which ones is drawn, and a query may name one block twice.
All inputs are finite; a program needn't handle non-finite values. No bound on the sum of `owned` on one device may be relied on, other than what follows from the above.
Results may differ from the reference program's by a relative error of at most 0.0028.
Values may be sent and summed in bfloat16 or wider, within the bound.
No kernel may reach another device: no remote copies, remote signals or barrier semaphores. Data moves between devices by JAX's collectives and lax.ppermute only.
A program may use at most 64 MiB of HBM per device.

```python
import math
import jax
import jax.numpy as jnp
import numpy as np
from jax import lax

D = 2048
NBRS = 10
BLOCK = 128
ROWS_DEV = 128
CANDS = 2
IMAGES = 16384
QUERIES = 1024
CAPACITY = 15
N_SHARD = 128


def common_direction(key):
    return jnp.clip(jax.random.normal(jax.random.fold_in(key, 91), (D,), jnp.float32), -4.0, 4.0)


def draw_descriptors(key, part):
    direction = common_direction(key)
    key = jax.random.fold_in(key, 3)
    key_gain, key_noise = jax.random.split(key)
    gains = jax.random.uniform(key_gain, (IMAGES, 1), jnp.float32, 0.5, 1.0)
    noise = 0.6 * jnp.clip(jax.random.normal(key_noise, (IMAGES, D), jnp.float32), -4.0, 4.0)
    return (gains * direction[None, :] + noise).astype(jnp.bfloat16)


def draw_queries(key, part):
    direction = common_direction(key)
    key = jax.random.fold_in(key, 5)
    key_gain, key_noise = jax.random.split(key)
    gains = jax.random.uniform(key_gain, (QUERIES, 1), jnp.float32, -1.0, 1.0)
    noise = jnp.clip(jax.random.normal(key_noise, (QUERIES, D), jnp.float32), -4.0, 4.0)
    return (0.03 * gains * direction[None, :] + noise).astype(jnp.bfloat16)


def draw_neighbours(key, part):
    key = jax.random.fold_in(key, 11)
    slot_count = ROWS_DEV * NBRS
    counts = np.where(np.arange(N_SHARD) < N_SHARD // 2, CAPACITY, CAPACITY // 3)
    bounds = jnp.asarray(np.cumsum(counts)[:-1], dtype=jnp.int32)

    def one_shard(shard_key):
        key_label, key_order, key_row = jax.random.split(shard_key, 3)
        positions = jnp.arange(slot_count, dtype=jnp.int32)
        ranked = jnp.sum((positions[:, None] >= bounds[None, :]).astype(jnp.int32), axis=1)
        labels = jax.random.permutation(key_label, N_SHARD).astype(jnp.int32)
        target = jnp.take(labels, ranked)
        order = jax.random.permutation(key_order, slot_count)
        target = jnp.take(target, order)
        row_pick = jax.random.randint(key_row, (slot_count,), 0, ROWS_DEV, jnp.int32)
        return (target * ROWS_DEV + row_pick).reshape(ROWS_DEV, NBRS)
    shard_keys = jax.random.split(key, N_SHARD)
    return jax.vmap(one_shard)(shard_keys).reshape(IMAGES, NBRS)


def draw_candidates(key, part):
    key = jax.random.fold_in(key, 17)
    block_total = IMAGES // BLOCK
    labels = jnp.arange(QUERIES * CANDS, dtype=jnp.int32) % block_total
    shuffled = jax.random.permutation(key, labels)
    return shuffled.astype(jnp.int32).reshape(QUERIES, CANDS)


def plant(entries, rng, smallest, largest):
    place = [jax.random.randint(jax.random.fold_in(rng, axis), (), 0, length) for axis, length in enumerate(entries.shape)]
    longest = entries.shape.index(max(entries.shape))
    next_to = place[:longest] + [(place[longest] + 1) % entries.shape[longest]] + place[longest + 1:]
    return entries.at[tuple(place)].set(smallest).at[tuple(next_to)].set(largest)


def setup_inputs(seed: int = 0) -> dict:
    key_list = jax.random.split(jax.random.key(seed), 6)
    descriptors = draw_descriptors(jax.random.fold_in(key_list[5], 71), 0)
    neighbours = draw_neighbours(jax.random.fold_in(key_list[5], 71), 0)
    owned = plant((jax.random.randint(key_list[2], (IMAGES, NBRS), 0, 2) < 1).astype(jnp.int32), jax.random.fold_in(key_list[2], 1), 0, 1)
    queries = draw_queries(jax.random.fold_in(key_list[5], 71), 0)
    candidates = draw_candidates(jax.random.fold_in(key_list[5], 71), 0)
    return dict(descriptors=descriptors, neighbours=neighbours, owned=owned, queries=queries, candidates=candidates)


def reference(descriptors, neighbours, owned, queries, candidates):
    images, width = descriptors.shape
    block_count = images // BLOCK
    base = descriptors.astype(jnp.float32)

    def step(accum, block_index):
        start = block_index * BLOCK
        own_rows = lax.dynamic_slice_in_dim(descriptors, start, BLOCK, 0).astype(jnp.float32)
        listed = lax.dynamic_slice_in_dim(neighbours, start, BLOCK, 0)
        flags = lax.dynamic_slice_in_dim(owned, start, BLOCK, 0).astype(jnp.float32)
        nearby = jnp.take(descriptors, listed, axis=0).astype(jnp.float32)
        similar = jnp.einsum('rd,rkd->rk', own_rows, nearby, precision=lax.Precision.HIGHEST) / D
        weight = similar ** 3
        forward = lax.optimization_barrier(jnp.sum(weight[..., None] * nearby, axis=1))
        reverse_terms = ((weight * flags)[..., None] * own_rows[:, None, :]).astype(jnp.bfloat16)
        reverse_terms = lax.optimization_barrier(reverse_terms).astype(jnp.float32)
        current = lax.dynamic_slice_in_dim(accum, start, BLOCK, 0)
        accum = lax.dynamic_update_slice_in_dim(accum, current + forward, start, 0)
        accum = accum.at[listed.reshape(-1)].add(reverse_terms.reshape(-1, width))
        return (accum, None)
    summed, _ = lax.scan(step, base, jnp.arange(block_count, dtype=jnp.int32))
    energy = lax.optimization_barrier(jnp.mean(summed * summed, axis=1))
    augmented = (summed * lax.rsqrt(energy + 1e-06)[:, None]).astype(jnp.bfloat16)
    tiled = augmented.reshape(block_count, BLOCK, width)

    def score_one(pair):
        query_row, cand_row = pair
        chosen = jnp.take(tiled, cand_row, axis=0).astype(jnp.float32)
        values = jnp.einsum('d,cbd->cb', query_row.astype(jnp.float32), chosen, precision=lax.Precision.HIGHEST)
        return values.reshape(-1)
    scores = lax.map(score_one, (queries, candidates)) / math.sqrt(D)
    return (augmented, scores)
```

```python
import functools
import math

import jax
import jax.numpy as jnp
from jax import lax
from jax.experimental import pallas as pl
from jax.experimental.pallas import tpu as pltpu
from jax.sharding import Mesh
from jax.sharding import PartitionSpec as P

D = 2048
BLOCK = 128
PLACES = 16
GROUP = 8
CORES = 2
LANES = 128
VMEM = 48 * 1024 * 1024
INTERPRET = False
f32 = jnp.float32
bf16 = jnp.bfloat16
i32 = jnp.int32
NT = (((1,), (1,)), ((), ()))
TN = (((0,), (0,)), ((), ()))


def exchange(parts, axis):
    return lax.all_to_all(parts, axis, split_axis=0, concat_axis=0, tiled=True)


def spread(part, axis, count):
    return exchange(jnp.broadcast_to(part[None], (count,) + part.shape), axis)


def params(**more):
    return pltpu.CompilerParams(vmem_limit_bytes=VMEM, **more)


def table_kernel(sizes, listed_ref, owned_ref, table_ref):
    ys, zs = sizes
    rows = listed_ref.shape[0]
    row = lax.broadcasted_iota(i32, (rows, LANES), 0)
    lane = lax.broadcasted_iota(i32, (rows, LANES), 1)
    lower = (row > lane).astype(bf16)
    own_mark = (row + 1).astype(f32)
    before = jnp.zeros((1, LANES), f32)
    high = jnp.zeros((LANES, LANES), f32)
    low = jnp.zeros((LANES, LANES), f32)
    for slot in range(listed_ref.shape[1]):
        listed = listed_ref[:, slot : slot + 1]
        shard = lax.shift_right_logical(listed, 7)
        y = shard // (zs * CORES)
        zc = shard - y * (zs * CORES)
        column = zc * ys + y
        match = lane == column
        ones = match.astype(bf16)
        counted = jnp.dot(lower, ones, preferred_element_type=f32) + before
        before = before + jnp.sum(ones.astype(f32), axis=0, keepdims=True)
        rank = jnp.sum(jnp.where(match, counted, 0.0), axis=1, keepdims=True).astype(i32)
        group = lax.shift_right_logical(column, 3)
        place = (column - group * GROUP) * PLACES + rank
        left = (lane == group).astype(bf16)
        here = lane == place
        source = ((listed & (BLOCK - 1)) * 2 + owned_ref[:, slot : slot + 1]).astype(f32)
        high += lax.dot_general(left, jnp.where(here, own_mark, 0.0).astype(bf16), TN, preferred_element_type=f32)
        low += lax.dot_general(left, jnp.where(here, source, 0.0).astype(bf16), TN, preferred_element_type=f32)
    high = high[:zs].astype(i32)
    low = low[:zs].astype(i32)
    table_ref[...] = jnp.where(high > 0, (high - 1) * 256 + low, -1)


def build_table(neighbours, owned, ys, zs):
    return pl.pallas_call(
        functools.partial(table_kernel, (ys, zs)),
        out_shape=jax.ShapeDtypeStruct((zs, LANES), i32),
        compiler_params=params(),
        interpret=INTERPRET,
        name="slot_table",
    )(neighbours, owned)


def similar_kernel(groups, all_ref, own_ref, src_ref, at_ref, got_ref, sims_ref):
    row = lax.broadcasted_iota(i32, (BLOCK, LANES), 0)
    shards = own_ref.shape[0] // BLOCK

    def step(group, carry):
        first = pl.multiple_of(group * GROUP, GROUP)
        source = src_ref[pl.ds(first, GROUP), :]
        at = at_ref[pl.ds(first, GROUP), :]
        parts = []
        for one in range(GROUP):
            pick = (row == source[one : one + 1]).astype(bf16)
            block = all_ref[pl.ds(pl.multiple_of((first + one) * BLOCK, BLOCK), BLOCK), :]
            parts.append(lax.dot_general(pick, block, TN, preferred_element_type=f32).astype(bf16))
        sims = []
        for shard in range(shards):
            own = own_ref[shard * BLOCK : (shard + 1) * BLOCK, :]
            for kind in range(2):
                k = 2 * shard + kind
                chunk = jnp.concatenate([part[k * PLACES : (k + 1) * PLACES] for part in parts], axis=0)
                got_ref[k, pl.ds(pl.multiple_of(group * LANES, LANES), LANES), :] = chunk
                dots = lax.dot_general(own, chunk, NT, preferred_element_type=f32)
                sims.append(jnp.sum(jnp.where(row == at[k : k + 1], dots, 0.0), axis=0, keepdims=True))
        sims_ref[pl.ds(first, GROUP), :] = jnp.concatenate(sims, axis=0)
        return carry

    lax.fori_loop(0, groups, step, 0)


def similar_parts(everything, own, source, at):
    blocks = everything.shape[0] // BLOCK
    groups = blocks // GROUP
    steps = 4
    per = groups // steps
    kinds = 2 * own.shape[0] // BLOCK
    return pl.pallas_call(
        functools.partial(similar_kernel, per),
        grid=(steps,),
        in_specs=[
            pl.BlockSpec((per * GROUP * BLOCK, LANES), lambda i: (i, 0)),
            pl.BlockSpec(own.shape, lambda i: (0, 0)),
            pl.BlockSpec((per * GROUP, LANES), lambda i: (i, 0)),
            pl.BlockSpec((per * GROUP, LANES), lambda i: (i, 0)),
        ],
        out_specs=[
            pl.BlockSpec((kinds, per * LANES, LANES), lambda i: (0, i, 0)),
            pl.BlockSpec((per * GROUP, LANES), lambda i: (i, 0)),
        ],
        out_shape=[
            jax.ShapeDtypeStruct((kinds, groups * LANES, LANES), bf16),
            jax.ShapeDtypeStruct((groups * GROUP, LANES), f32),
        ],
        compiler_params=params(),
        interpret=INTERPRET,
        name="similar_parts",
    )(everything, own, source, at)


def sum_kernel(groups, got_ref, sims_ref, own_ref, at_ref, sum_ref):
    row = lax.broadcasted_iota(i32, (BLOCK, LANES), 0)
    shards = own_ref.shape[0] // BLOCK

    @pl.when(pl.program_id(0) == 0)
    def _():
        sum_ref[...] = own_ref[...].astype(f32)

    similar = sims_ref[...] / D
    weight = similar * similar * similar
    high = weight.astype(bf16).astype(f32)
    low = weight - high
    for shard in range(shards):
        total = sum_ref[shard * BLOCK : (shard + 1) * BLOCK, :]
        for kind in range(2):
            k = 2 * shard + kind
            left_high, left_low = [], []
            for group in range(groups):
                n = group * GROUP + k
                here = row == at_ref[n : n + 1, :]
                left_high.append(jnp.where(here, high[n : n + 1], 0.0).astype(bf16))
                left_low.append(jnp.where(here, low[n : n + 1], 0.0).astype(bf16))
            got = got_ref[k]
            total += jnp.dot(jnp.concatenate(left_high, axis=1), got, preferred_element_type=f32)
            total += jnp.dot(jnp.concatenate(left_low, axis=1), got, preferred_element_type=f32)
        sum_ref[shard * BLOCK : (shard + 1) * BLOCK, :] = total


def weighted_sum(got, sims, own, at):
    kinds, slots, _ = got.shape
    groups = slots // LANES
    steps = 4
    per = groups // steps
    return pl.pallas_call(
        functools.partial(sum_kernel, per),
        grid=(steps,),
        in_specs=[
            pl.BlockSpec((kinds, per * LANES, LANES), lambda i: (0, i, 0)),
            pl.BlockSpec((per * GROUP, LANES), lambda i: (i, 0)),
            pl.BlockSpec(own.shape, lambda i: (0, 0)),
            pl.BlockSpec((per * GROUP, LANES), lambda i: (i, 0)),
        ],
        out_specs=pl.BlockSpec(own.shape, lambda i: (0, 0)),
        out_shape=jax.ShapeDtypeStruct(own.shape, f32),
        compiler_params=params(),
        interpret=INTERPRET,
        name="weighted_sum",
    )(got, sims, own, at)


def pick_kernel(rows_ref, table_ref, out_ref):
    def step(i, carry):
        for cand in range(2):
            picked = []
            for one in range(GROUP):
                r = rows_ref[i * (2 * GROUP) + 2 * one + cand]
                picked.append(table_ref[pl.ds(r, 1), :])
            at = pl.ds(pl.multiple_of(i * GROUP, GROUP), GROUP)
            out_ref[at, cand * LANES : (cand + 1) * LANES] = jnp.concatenate(picked, axis=0)
        return carry

    lax.fori_loop(0, out_ref.shape[0] // GROUP, step, 0)


def pick_scores(rows, table):
    queries = rows.shape[0] // 2
    return pl.pallas_call(
        pick_kernel,
        in_specs=[pl.BlockSpec(memory_space=pltpu.SMEM), pl.BlockSpec(memory_space=pltpu.VMEM)],
        out_specs=pl.BlockSpec(memory_space=pltpu.VMEM),
        out_shape=jax.ShapeDtypeStruct((queries, 2 * LANES), f32),
        compiler_params=params(),
        interpret=INTERPRET,
        name="pick_scores",
    )(rows, table)


def slot_orders(table, ys, zs):
    toward = exchange(table.reshape(zs, 1, LANES), "z").reshape(zs, LANES)
    both = spread(jnp.stack([table, toward]), ("y", "core"), GROUP)
    both = both.reshape(ys, CORES, 2, zs, LANES)
    core = lax.axis_index("core")
    ahead = lax.dynamic_index_in_dim(both[:, :, 0], core, 1, keepdims=False)
    ahead = ahead.reshape(ys, zs * GROUP, PLACES)
    back = both[:, :, 1].reshape(ys, CORES, zs, CORES, ys * PLACES)
    back = lax.dynamic_index_in_dim(back, core, 3, keepdims=False)
    back = back.reshape(ys, CORES, zs, ys, PLACES).transpose(2, 1, 0, 3, 4)
    back = back.reshape(zs * GROUP, ys, PLACES)
    ahead_own = jnp.where(ahead >= 0, lax.shift_right_logical(ahead, 8), -1)
    ahead_src = jnp.where(ahead >= 0, lax.shift_right_logical(ahead, 1) & (BLOCK - 1), -1)
    held = (back >= 0) & ((back & 1) == 1)
    back_src = jnp.where(held, lax.shift_right_logical(back, 8), -1)
    back_own = jnp.where(held, lax.shift_right_logical(back, 1) & (BLOCK - 1), -1)
    source = jnp.stack([ahead_src.transpose(1, 0, 2), back_src], axis=2).reshape(zs * GROUP, LANES)
    at = jnp.stack([ahead_own, back_own.transpose(1, 0, 2)], axis=1)
    at = at.reshape(2 * ys, zs, LANES).transpose(1, 0, 2).reshape(zs * GROUP, LANES)
    return source, at


def query_entries(queries, candidates, xs, zs):
    flat = candidates.reshape(-1)
    order = jnp.arange(flat.shape[0], dtype=i32)
    earlier = (flat[:, None] == flat[None, :]) & (order[:, None] > order[None, :])
    rank = jnp.sum(earlier.astype(i32), axis=1)
    here = lax.axis_index(("y", "z", "core"))
    hits = (flat == here)[None, :] & (rank[None, :] == jnp.arange(PLACES, dtype=i32)[:, None])
    hits = jnp.sum(hits.reshape(PLACES, -1, 2).astype(f32), axis=2).astype(bf16)
    chosen = jnp.dot(hits, queries, preferred_element_type=f32).astype(bf16)
    chosen = chosen.reshape(PLACES, xs, -1).transpose(1, 0, 2)
    chosen = exchange(chosen, "x").reshape(xs * PLACES, -1)
    y = flat // (zs * CORES)
    z = flat // CORES - y * zs
    core = flat - (flat // CORES) * CORES
    rows = ((y * CORES + core) * zs + z) * PLACES + rank
    return chosen, rows


def per_device(descriptors, neighbours, owned, queries, candidates):
    ys, zs, xs = lax.axis_size("y"), lax.axis_size("z"), lax.axis_size("x")
    rows, width = descriptors.shape
    pieces = descriptors.reshape(rows, ys, LANES).transpose(1, 0, 2)
    own = exchange(pieces, "y").reshape(ys * rows, LANES)
    everything = lax.all_gather(own, ("z", "core"), axis=0, tiled=True)
    table = build_table(neighbours, owned, ys, zs)
    source, at = slot_orders(table, ys, zs)
    chosen, score_rows = query_entries(queries, candidates, xs, zs)
    got, sims = similar_parts(everything, own, source, at)
    share = jnp.sum(exchange(sims.reshape(ys * xs, -1, LANES), ("y", "x")), axis=0)
    sims = spread(share, ("y", "x"), ys * xs).reshape(sims.shape)
    summed = weighted_sum(got, sims, own, at)
    summed = exchange(summed.reshape(ys, rows, LANES), "y").transpose(1, 0, 2).reshape(rows, width)
    energy = jnp.sum(summed * summed, axis=1)
    scores = lax.dot_general(chosen.astype(f32), summed, NT, precision=lax.Precision.HIGHEST)
    parts = jnp.concatenate(
        [scores.reshape(xs, PLACES, rows), jnp.broadcast_to(energy[None, None, :], (xs, 8, rows))], axis=1
    )
    whole = jnp.sum(exchange(parts, "x"), axis=0)
    scale = lax.rsqrt(whole[PLACES] / (xs * width) + 1e-06)
    augmented = (summed * scale[:, None]).astype(bf16)
    mine = whole[:PLACES] * (scale / math.sqrt(xs * width))[None, :]
    plane = spread(mine, "z", zs)
    table = spread(plane, ("y", "core"), GROUP).reshape(-1, rows)
    return augmented, pick_scores(score_rows, table)


def solution(mesh):
    shards, lanes = mesh.devices.shape
    ys = GROUP // CORES
    split = Mesh(mesh.devices.reshape(ys, shards // GROUP, CORES, lanes), ("y", "z", "core", "x"))
    shard = ("y", "z", "core")
    return jax.shard_map(
        per_device,
        mesh=split,
        in_specs=(P(shard, "x"), P(shard, None), P(shard, None), P("x", None), P("x", None)),
        out_specs=(P(shard, "x"), P("x", None)),
        check_vma=False,
    )
```

```python
import functools
import math

import jax
import jax.numpy as jnp
from jax import lax
from jax.experimental import pallas as pl
from jax.experimental.pallas import tpu as pltpu
from jax.sharding import Mesh
from jax.sharding import PartitionSpec as P

D = 2048
BLOCK = 128
PLACES = 16
GROUP = 8
CORES = 2
LANES = 128
VMEM = 48 * 1024 * 1024
INTERPRET = False
STEPS = 4
HBM = pltpu.HBM
f32 = jnp.float32
bf16 = jnp.bfloat16
i32 = jnp.int32
NT = (((1,), (1,)), ((), ()))
TN = (((0,), (0,)), ((), ()))


def exchange(parts, axis):
    return lax.all_to_all(parts, axis, split_axis=0, concat_axis=0, tiled=True)


def spread(part, axis, count):
    return exchange(jnp.broadcast_to(part[None], (count,) + part.shape), axis)


def hbm(shape, dtype):
    return jax.ShapeDtypeStruct(shape, dtype) if INTERPRET else pltpu.HBM(shape, dtype)


def params(**more):
    return pltpu.CompilerParams(vmem_limit_bytes=VMEM, **more)


def table_kernel(listed_ref, owned_ref, table_ref):
    rows = listed_ref.shape[0]
    row = lax.broadcasted_iota(i32, (rows, LANES), 0)
    lane = lax.broadcasted_iota(i32, (rows, LANES), 1)
    lower = (row > lane).astype(bf16)
    own_mark = (row + 1).astype(f32)
    before = jnp.zeros((1, LANES), f32)
    high = jnp.zeros((LANES, LANES), f32)
    low = jnp.zeros((LANES, LANES), f32)
    for slot in range(listed_ref.shape[1]):
        listed = listed_ref[:, slot : slot + 1]
        shard = lax.shift_right_logical(listed, 7)
        match = lane == shard
        ones = jnp.where(match, 1.0, 0.0)
        counted = jnp.dot(lower, ones.astype(bf16), preferred_element_type=f32) + before
        before = before + jnp.sum(ones, axis=0, keepdims=True)
        rank = jnp.sum(jnp.where(match, counted, 0.0), axis=1, keepdims=True).astype(i32)
        left = jnp.where(lane == lax.shift_right_logical(shard, 3), 1.0, 0.0).astype(bf16)
        here = lane == (shard & (GROUP - 1)) * PLACES + rank
        source = ((listed & (BLOCK - 1)) * 2 + owned_ref[:, slot : slot + 1]).astype(f32)
        high += lax.dot_general(left, jnp.where(here, own_mark, 0.0).astype(bf16), TN, preferred_element_type=f32)
        low += lax.dot_general(left, jnp.where(here, source, 0.0).astype(bf16), TN, preferred_element_type=f32)
    count = table_ref.shape[0]
    high = high[:count].astype(i32)
    low = low[:count].astype(i32)
    table_ref[...] = jnp.where(high > 0, (high - 1) * 256 + low, -1)


def build_table(neighbours, owned, shards):
    return pl.pallas_call(
        table_kernel,
        out_shape=jax.ShapeDtypeStruct((shards // GROUP, LANES), i32),
        compiler_params=params(),
        interpret=INTERPRET,
        name="slot_table",
    )(neighbours, owned)


def similar_kernel(groups, all_ref, own_ref, src_ref, at_ref, got_ref, sims_ref):
    row = lax.broadcasted_iota(i32, (BLOCK, LANES), 0)
    shards = own_ref.shape[0] // BLOCK
    for group in range(groups):
        parts = []
        for one in range(group * GROUP, (group + 1) * GROUP):
            pick = jnp.where(row == src_ref[one : one + 1, :], 1.0, 0.0).astype(bf16)
            block = all_ref[one * BLOCK : (one + 1) * BLOCK, :]
            parts.append(lax.dot_general(pick, block, TN, preferred_element_type=f32).astype(bf16))
        sims = []
        for shard in range(shards):
            chunks = []
            for k in (2 * shard, 2 * shard + 1):
                chunk = jnp.concatenate([part[k * PLACES : (k + 1) * PLACES] for part in parts], axis=0)
                got_ref[k, group * LANES : (group + 1) * LANES, :] = chunk
                chunks.append(chunk)
            own = own_ref[shard * BLOCK : (shard + 1) * BLOCK, :]
            dots = lax.dot_general(own, jnp.concatenate(chunks, axis=0), NT, preferred_element_type=f32)
            for kind in range(2):
                n = group * GROUP + 2 * shard + kind
                held = jnp.where(row == at_ref[n : n + 1, :], dots[:, kind * LANES : (kind + 1) * LANES], 0.0)
                sims.append(jnp.sum(held, axis=0, keepdims=True))
        sims_ref[group * GROUP : (group + 1) * GROUP, :] = jnp.concatenate(sims, axis=0)


def similar_parts(everything, own, source, at, steps=STEPS):
    width = own.shape[1]
    groups = everything.shape[0] // BLOCK // GROUP
    per = max(groups // steps, 1)
    kinds = 2 * own.shape[0] // BLOCK
    return pl.pallas_call(
        functools.partial(similar_kernel, per),
        grid=(groups // per,),
        in_specs=[
            pl.BlockSpec((per * GROUP * BLOCK, width), lambda i: (i, 0)),
            pl.BlockSpec(own.shape, lambda i: (0, 0)),
            pl.BlockSpec((per * GROUP, LANES), lambda i: (i, 0)),
            pl.BlockSpec((per * GROUP, LANES), lambda i: (i, 0)),
        ],
        out_specs=[
            pl.BlockSpec((kinds, per * LANES, width), lambda i: (0, i, 0)),
            pl.BlockSpec((per * GROUP, LANES), lambda i: (i, 0)),
        ],
        out_shape=[
            hbm((kinds, groups * LANES, width), bf16),
            jax.ShapeDtypeStruct((groups * GROUP, LANES), f32),
        ],
        compiler_params=params(),
        interpret=INTERPRET,
        name="similar_parts",
    )(everything, own, source, at)


def sum_kernel(got_ref, sims_ref, at_ref, sum_ref, held_ref, sems):
    shards = sum_ref.shape[0]
    copies = []
    for shard in range(shards):
        pair = slice(2 * shard, 2 * shard + 2)
        copies.append(pltpu.make_async_copy(got_ref.at[pair], held_ref.at[pair], sems.at[shard]))
        copies[-1].start()
    row = lax.broadcasted_iota(i32, (BLOCK, LANES), 0)
    similar = jnp.sum(sims_ref[...], axis=0) / D
    weight = similar * similar * similar
    high = weight.astype(bf16).astype(f32)
    low = weight - high
    groups = at_ref.shape[0] // GROUP
    for shard in range(shards):
        left_high, left_low = [], []
        for k in (2 * shard, 2 * shard + 1):
            for group in range(groups):
                n = group * GROUP + k
                here = row == at_ref[n : n + 1, :]
                left_high.append(jnp.where(here, high[n : n + 1], 0.0).astype(bf16))
                left_low.append(jnp.where(here, low[n : n + 1], 0.0).astype(bf16))
        copies[shard].wait()
        right = jnp.concatenate([held_ref[2 * shard], held_ref[2 * shard + 1]], axis=0)
        total = jnp.dot(jnp.concatenate(left_high, axis=1), right, preferred_element_type=f32)
        total += jnp.dot(jnp.concatenate(left_low, axis=1), right, preferred_element_type=f32)
        sum_ref[shard] = total


def weighted_sums(got, sims, at):
    kinds, slots, width = got.shape
    vmem = pl.BlockSpec(memory_space=pltpu.VMEM)
    return pl.pallas_call(
        sum_kernel,
        in_specs=[pl.BlockSpec(memory_space=HBM), vmem, vmem],
        out_specs=vmem,
        out_shape=jax.ShapeDtypeStruct((kinds // 2, BLOCK, width), f32),
        scratch_shapes=[pltpu.VMEM(got.shape, bf16), pltpu.SemaphoreType.DMA((kinds // 2,))],
        compiler_params=params(),
        interpret=INTERPRET,
        name="weighted_sums",
    )(got, sims, at)


def score_kernel(parts_ref, own_ref, chosen_ref, sum_ref, out_ref):
    total = own_ref[...].astype(f32)
    for part in range(parts_ref.shape[0]):
        total += parts_ref[part]
    sum_ref[...] = total
    energy = jnp.sum(total * total, axis=1, keepdims=True)
    energy = jnp.broadcast_to(energy, (BLOCK, LANES)).T[:8]
    high = total.astype(bf16)
    low = (total - high.astype(f32)).astype(bf16)
    chosen = chosen_ref[...]
    scores = lax.dot_general(chosen, high, NT, preferred_element_type=f32)
    scores += lax.dot_general(chosen, low, NT, preferred_element_type=f32)
    for lane in range(out_ref.shape[0]):
        out_ref[lane, :PLACES, :] = scores[lane * PLACES : (lane + 1) * PLACES]
        out_ref[lane, PLACES:, :] = energy


def score_parts(parts, own, chosen, xs):
    return pl.pallas_call(
        score_kernel,
        out_shape=[
            jax.ShapeDtypeStruct(own.shape, f32),
            jax.ShapeDtypeStruct((xs, PLACES + 8, LANES), f32),
        ],
        compiler_params=params(),
        interpret=INTERPRET,
        name="score_parts",
    )(parts, own, chosen)


def pick_kernel(rows_ref, near_ref, far_ref, out_ref):
    count = near_ref.shape[0]

    def step(i, carry):
        for cand in range(2):
            picked = []
            for one in range(GROUP):
                r = rows_ref[i * (2 * GROUP) + 2 * one + cand]
                near = near_ref[pl.ds(lax.rem(r, count), 1), :]
                far = far_ref[pl.ds(lax.rem(r, count), 1), :]
                picked.append(jnp.where(r < count, near, far))
            at = pl.ds(pl.multiple_of(i * GROUP, GROUP), GROUP)
            out_ref[at, cand * LANES : (cand + 1) * LANES] = jnp.concatenate(picked, axis=0)
        return carry

    lax.fori_loop(0, out_ref.shape[0] // GROUP, step, 0)


def pick_scores(rows, near, far):
    queries = rows.shape[0] // 2
    vmem = pl.BlockSpec(memory_space=pltpu.VMEM)
    return pl.pallas_call(
        pick_kernel,
        in_specs=[pl.BlockSpec(memory_space=pltpu.SMEM), vmem, vmem],
        out_specs=vmem,
        out_shape=jax.ShapeDtypeStruct((queries, 2 * LANES), f32),
        compiler_params=params(),
        interpret=INTERPRET,
        name="pick_scores",
    )(rows, near, far)


def slot_orders(table, ys, zs):
    count = zs * CORES
    groups = count // GROUP
    ahead = exchange(table.reshape(ys, groups, LANES), "y")
    back = table.reshape(ys, count, PLACES).transpose(1, 0, 2).reshape(count, 1, ys * PLACES)
    back = exchange(back, ("z", "core")).reshape(count, ys, PLACES)
    ahead_own = jnp.where(ahead >= 0, lax.shift_right_logical(ahead, 8), -1)
    ahead_src = jnp.where(ahead >= 0, lax.shift_right_logical(ahead, 1) & (BLOCK - 1), -1)
    held = (back >= 0) & ((back & 1) == 1)
    back_src = jnp.where(held, lax.shift_right_logical(back, 8), -1)
    back_own = jnp.where(held, lax.shift_right_logical(back, 1) & (BLOCK - 1), -1)
    source = jnp.stack([ahead_src.reshape(ys, count, PLACES).transpose(1, 0, 2), back_src], axis=2)
    at = jnp.stack([ahead_own, back_own.transpose(1, 0, 2).reshape(ys, groups, LANES)], axis=1)
    at = at.reshape(2 * ys, groups, LANES).transpose(1, 0, 2).reshape(groups * GROUP, LANES)
    return source.reshape(count, LANES), at


def query_entries(queries, candidates, xs, zs):
    flat = candidates.reshape(-1)
    order = jnp.arange(flat.shape[0], dtype=i32)
    earlier = (flat[:, None] == flat[None, :]) & (order[:, None] > order[None, :])
    rank = jnp.sum(earlier.astype(i32), axis=1)
    here = lax.axis_index(("y", "z", "core"))
    hits = (flat == here)[None, :] & (rank[None, :] == jnp.arange(PLACES, dtype=i32)[:, None])
    hits = jnp.sum(hits.reshape(PLACES, -1, 2).astype(f32), axis=2).astype(bf16)
    chosen = jnp.dot(hits, queries, preferred_element_type=f32).astype(bf16)
    chosen = chosen.reshape(PLACES, xs, -1).transpose(1, 0, 2)
    chosen = exchange(chosen, "x").reshape(xs * PLACES, -1)
    plane = flat // CORES
    core = flat - plane * CORES
    far = (core != lax.axis_index("core")).astype(i32)
    rows = (far * (GROUP // CORES * zs) + plane) * PLACES + rank
    return chosen, rows


def per_device(descriptors, neighbours, owned, queries, candidates):
    ys, zs, xs = lax.axis_size("y"), lax.axis_size("z"), lax.axis_size("x")
    rows, width = descriptors.shape
    everything = lax.all_gather(descriptors, ("z", "core"), axis=0, tiled=True)
    table = build_table(neighbours, owned, ys * zs * CORES)
    source, at = slot_orders(table, ys, zs)
    own = spread(descriptors, "y", ys).reshape(ys * rows, width)
    chosen, score_rows = query_entries(queries, candidates, xs, zs)
    source, at, own, chosen, score_rows = lax.optimization_barrier((source, at, own, chosen, score_rows))
    got, sims = similar_parts(everything, own, source, at)
    sims = spread(sims, "x", xs)
    parts = exchange(weighted_sums(got, sims, at), "y")
    summed, parts = score_parts(parts, descriptors, chosen, xs)
    whole = jnp.sum(exchange(parts, "x"), axis=0)
    scale = lax.rsqrt(whole[PLACES] / (xs * width) + 1e-06)
    augmented = (summed * scale[:, None]).astype(bf16)
    mine = whole[:PLACES] * (scale / math.sqrt(xs * width))[None, :]
    near = spread(spread(mine, "z", zs), "y", ys).reshape(-1, rows)
    far = lax.ppermute(near, "core", [(0, 1), (1, 0)])
    return augmented, pick_scores(score_rows, near, far)


def solution(mesh):
    shards, lanes = mesh.devices.shape
    ys = GROUP // CORES
    split = Mesh(mesh.devices.reshape(ys, shards // GROUP, CORES, lanes), ("y", "z", "core", "x"))
    shard = ("y", "z", "core")
    return jax.shard_map(
        per_device,
        mesh=split,
        in_specs=(P(shard, "x"), P(shard, None), P(shard, None), P("x", None), P("x", None)),
        out_specs=(P(shard, "x"), P("x", None)),
        check_vma=False,
    )
```

```python
import functools
import math

import jax
import jax.numpy as jnp
from jax import lax
from jax.experimental import pallas as pl
from jax.experimental.pallas import tpu as pltpu
from jax.sharding import Mesh
from jax.sharding import PartitionSpec as P

D = 2048
BLOCK = 128
PLACES = 16
GROUP = 8
CORES = 2
LANES = 128
VMEM = 48 * 1024 * 1024
INTERPRET = False
STEPS = 2
HBM = pltpu.HBM
f32 = jnp.float32
bf16 = jnp.bfloat16
i16 = jnp.int16
i32 = jnp.int32
LEVELS = 32512.0
STEPS_PER_OCTAVE = 64.0
NT = (((1,), (1,)), ((), ()))
TN = (((0,), (0,)), ((), ()))


def exchange(parts, axis):
    return lax.all_to_all(parts, axis, split_axis=0, concat_axis=0, tiled=True)


def spread(part, axis, count):
    return exchange(jnp.broadcast_to(part[None], (count,) + part.shape), axis)


def hbm(shape, dtype):
    return jax.ShapeDtypeStruct(shape, dtype) if INTERPRET else pltpu.HBM(shape, dtype)


def pinned(value):
    return value if INTERPRET else pltpu.with_memory_space_constraint(value, HBM)


def params(**more):
    return pltpu.CompilerParams(vmem_limit_bytes=VMEM, **more)


def table_kernel(listed_ref, owned_ref, table_ref):
    rows = listed_ref.shape[0]
    row = lax.broadcasted_iota(i32, (rows, LANES), 0)
    lane = lax.broadcasted_iota(i32, (rows, LANES), 1)
    lower = (row > lane).astype(bf16)
    own_mark = (row + 1).astype(f32)
    before = jnp.zeros((1, LANES), f32)
    high = jnp.zeros((LANES, LANES), f32)
    low = jnp.zeros((LANES, LANES), f32)
    for slot in range(listed_ref.shape[1]):
        listed = listed_ref[:, slot : slot + 1]
        shard = lax.shift_right_logical(listed, 7)
        match = lane == shard
        ones = jnp.where(match, 1.0, 0.0)
        counted = jnp.dot(lower, ones.astype(bf16), preferred_element_type=f32) + before
        before = before + jnp.sum(ones, axis=0, keepdims=True)
        rank = jnp.sum(jnp.where(match, counted, 0.0), axis=1, keepdims=True).astype(i32)
        left = jnp.where(lane == lax.shift_right_logical(shard, 3), 1.0, 0.0).astype(bf16)
        here = lane == (shard & (GROUP - 1)) * PLACES + rank
        source = ((listed & (BLOCK - 1)) * 2 + owned_ref[:, slot : slot + 1]).astype(f32)
        high += lax.dot_general(left, jnp.where(here, own_mark, 0.0).astype(bf16), TN, preferred_element_type=f32)
        low += lax.dot_general(left, jnp.where(here, source, 0.0).astype(bf16), TN, preferred_element_type=f32)
    count = table_ref.shape[0]
    high = high[:count].astype(i32)
    low = low[:count].astype(i32)
    table_ref[...] = jnp.where(high > 0, (high - 1) * 256 + low, -1)


def build_table(neighbours, owned, shards):
    return pl.pallas_call(
        table_kernel,
        out_shape=jax.ShapeDtypeStruct((shards // GROUP, LANES), i32),
        compiler_params=params(),
        interpret=INTERPRET,
        name="slot_table",
    )(neighbours, owned)


def similar_kernel(groups, all_ref, own_ref, src_ref, at_ref, got_ref, sims_ref):
    row = lax.broadcasted_iota(i32, (BLOCK, LANES), 0)
    shards = own_ref.shape[0] // BLOCK
    for group in range(groups):
        parts = []
        for one in range(group * GROUP, (group + 1) * GROUP):
            pick = jnp.where(row == src_ref[one : one + 1, :], 1.0, 0.0).astype(bf16)
            block = all_ref[one * BLOCK : (one + 1) * BLOCK, :]
            parts.append(lax.dot_general(pick, block, TN, preferred_element_type=f32).astype(bf16))
        sims = []
        for shard in range(shards):
            chunks = []
            for k in (2 * shard, 2 * shard + 1):
                chunk = jnp.concatenate([part[k * PLACES : (k + 1) * PLACES] for part in parts], axis=0)
                got_ref[k, group * LANES : (group + 1) * LANES, :] = chunk
                chunks.append(chunk)
            own = own_ref[shard * BLOCK : (shard + 1) * BLOCK, :]
            dots = lax.dot_general(own, jnp.concatenate(chunks, axis=0), NT, preferred_element_type=f32)
            for kind in range(2):
                n = group * GROUP + 2 * shard + kind
                held = jnp.where(row == at_ref[n : n + 1, :], dots[:, kind * LANES : (kind + 1) * LANES], 0.0)
                sims.append(jnp.sum(held, axis=0, keepdims=True))
        sims_ref[group * GROUP : (group + 1) * GROUP, :] = jnp.concatenate(sims, axis=0)


def similar_parts(everything, own, source, at, steps=STEPS):
    width = own.shape[1]
    groups = everything.shape[0] // BLOCK // GROUP
    per = max(groups // steps, 1)
    kinds = 2 * own.shape[0] // BLOCK
    return pl.pallas_call(
        functools.partial(similar_kernel, per),
        grid=(groups // per,),
        in_specs=[
            pl.BlockSpec((per * GROUP * BLOCK, width), lambda i: (i, 0)),
            pl.BlockSpec(own.shape, lambda i: (0, 0)),
            pl.BlockSpec((per * GROUP, LANES), lambda i: (i, 0)),
            pl.BlockSpec((per * GROUP, LANES), lambda i: (i, 0)),
        ],
        out_specs=[
            pl.BlockSpec((kinds, per * LANES, width), lambda i: (0, i, 0)),
            pl.BlockSpec((per * GROUP, LANES), lambda i: (i, 0)),
        ],
        out_shape=[
            hbm((kinds, groups * LANES, width), bf16),
            jax.ShapeDtypeStruct((groups * GROUP, LANES), f32),
        ],
        compiler_params=params(),
        interpret=INTERPRET,
        name="similar_parts",
    )(pinned(everything), own, source, at)


def sum_kernel(got_ref, sims_ref, at_ref, sum_ref, held_ref, sems):
    shards = sum_ref.shape[0]
    copies = []
    for shard in range(shards):
        pair = slice(2 * shard, 2 * shard + 2)
        copies.append(pltpu.make_async_copy(got_ref.at[pair], held_ref.at[pair], sems.at[shard]))
        copies[-1].start()
    row = lax.broadcasted_iota(i32, (BLOCK, LANES), 0)
    similar = jnp.sum(sims_ref[...], axis=0) / D
    weight = similar * similar * similar
    high = weight.astype(bf16).astype(f32)
    low = weight - high
    groups = at_ref.shape[0] // GROUP
    for shard in range(shards):
        left_high, left_low = [], []
        for k in (2 * shard, 2 * shard + 1):
            for group in range(groups):
                n = group * GROUP + k
                here = row == at_ref[n : n + 1, :]
                left_high.append(jnp.where(here, high[n : n + 1], 0.0).astype(bf16))
                left_low.append(jnp.where(here, low[n : n + 1], 0.0).astype(bf16))
        copies[shard].wait()
        right = jnp.concatenate([held_ref[2 * shard], held_ref[2 * shard + 1]], axis=0)
        total = jnp.dot(jnp.concatenate(left_high, axis=1), right, preferred_element_type=f32)
        total += jnp.dot(jnp.concatenate(left_low, axis=1), right, preferred_element_type=f32)
        peak = jnp.maximum(jnp.max(jnp.abs(total), axis=1, keepdims=True), 1e-30)
        level = jnp.floor(jnp.log2(peak) * STEPS_PER_OCTAVE) + 1.0
        scale = LEVELS / jnp.exp2(level / STEPS_PER_OCTAVE)
        sum_ref[shard, :BLOCK, :] = jnp.floor(total * scale + 0.5).astype(i32).astype(i16)
        level = jnp.broadcast_to(level, (BLOCK, LANES)).T[:PLACES].astype(i32).astype(i16)
        sum_ref[shard, BLOCK:, :] = jnp.concatenate([level] * (total.shape[1] // LANES), axis=1)


def weighted_sums(got, sims, at):
    kinds, slots, width = got.shape
    vmem = pl.BlockSpec(memory_space=pltpu.VMEM)
    return pl.pallas_call(
        sum_kernel,
        in_specs=[pl.BlockSpec(memory_space=HBM), vmem, vmem],
        out_specs=vmem,
        out_shape=jax.ShapeDtypeStruct((kinds // 2, BLOCK + PLACES, width), i16),
        scratch_shapes=[pltpu.VMEM(got.shape, bf16), pltpu.SemaphoreType.DMA((kinds // 2,))],
        compiler_params=params(),
        interpret=INTERPRET,
        name="weighted_sums",
    )(pinned(got), sims, at)


def score_kernel(parts_ref, own_ref, chosen_ref, sum_ref, out_ref):
    total = own_ref[...].astype(f32)
    for part in range(parts_ref.shape[0]):
        level = parts_ref[part, BLOCK:, :LANES].astype(i32).astype(f32)[:1]
        level = jnp.broadcast_to(level, (BLOCK, LANES)).T[:, :1]
        scale = jnp.exp2(level / STEPS_PER_OCTAVE) / LEVELS
        total += parts_ref[part, :BLOCK, :].astype(i32).astype(f32) * scale
    sum_ref[...] = total
    energy = jnp.sum(total * total, axis=1, keepdims=True)
    energy = jnp.broadcast_to(energy, (BLOCK, LANES)).T[:8]
    high = total.astype(bf16)
    low = (total - high.astype(f32)).astype(bf16)
    chosen = chosen_ref[...]
    scores = lax.dot_general(chosen, high, NT, preferred_element_type=f32)
    scores += lax.dot_general(chosen, low, NT, preferred_element_type=f32)
    for lane in range(out_ref.shape[0]):
        out_ref[lane, :PLACES, :] = scores[lane * PLACES : (lane + 1) * PLACES]
        out_ref[lane, PLACES:, :] = energy


def score_parts(parts, own, chosen, xs):
    return pl.pallas_call(
        score_kernel,
        out_shape=[
            jax.ShapeDtypeStruct(own.shape, f32),
            jax.ShapeDtypeStruct((xs, PLACES + 8, LANES), f32),
        ],
        compiler_params=params(),
        interpret=INTERPRET,
        name="score_parts",
    )(parts, own, chosen)


def pick_kernel(rows_ref, near_ref, far_ref, out_ref):
    count = near_ref.shape[0]

    def step(i, carry):
        for cand in range(2):
            picked = []
            for one in range(GROUP):
                r = rows_ref[i * (2 * GROUP) + 2 * one + cand]
                place = pl.ds(r & (count - 1), 1)
                picked.append(jnp.where(r < count, near_ref[place, :], far_ref[place, :]))
            at = pl.ds(pl.multiple_of(i * GROUP, GROUP), GROUP)
            out_ref[at, cand * LANES : (cand + 1) * LANES] = jnp.concatenate(picked, axis=0)
        return carry

    lax.fori_loop(0, out_ref.shape[0] // GROUP, step, 0, unroll=4)


def pick_scores(rows, near, far):
    queries = rows.shape[0] // 2
    vmem = pl.BlockSpec(memory_space=pltpu.VMEM)
    return pl.pallas_call(
        pick_kernel,
        in_specs=[pl.BlockSpec(memory_space=pltpu.SMEM), vmem, vmem],
        out_specs=vmem,
        out_shape=jax.ShapeDtypeStruct((queries, 2 * LANES), f32),
        compiler_params=params(),
        interpret=INTERPRET,
        name="pick_scores",
    )(rows, near, far)


def slot_orders(table, ys, zs):
    count = zs * CORES
    groups = count // GROUP
    ahead = exchange(table.reshape(ys, groups, LANES), "y")
    back = table.reshape(ys, count, PLACES).transpose(1, 0, 2).reshape(count, 1, ys * PLACES)
    back = exchange(back, ("z", "core")).reshape(count, ys, PLACES)
    ahead_own = jnp.where(ahead >= 0, lax.shift_right_logical(ahead, 8), -1)
    ahead_src = jnp.where(ahead >= 0, lax.shift_right_logical(ahead, 1) & (BLOCK - 1), -1)
    held = (back >= 0) & ((back & 1) == 1)
    back_src = jnp.where(held, lax.shift_right_logical(back, 8), -1)
    back_own = jnp.where(held, lax.shift_right_logical(back, 1) & (BLOCK - 1), -1)
    source = jnp.stack([ahead_src.reshape(ys, count, PLACES).transpose(1, 0, 2), back_src], axis=2)
    at = jnp.stack([ahead_own, back_own.transpose(1, 0, 2).reshape(ys, groups, LANES)], axis=1)
    at = at.reshape(2 * ys, groups, LANES).transpose(1, 0, 2).reshape(groups * GROUP, LANES)
    return source.reshape(count, LANES), at


def query_entries(queries, candidates, xs, zs):
    flat = candidates.reshape(-1)
    order = jnp.arange(flat.shape[0], dtype=i32)
    earlier = (flat[:, None] == flat[None, :]) & (order[:, None] > order[None, :])
    rank = jnp.sum(earlier.astype(i32), axis=1)
    here = lax.axis_index(("y", "z", "core"))
    hits = (flat == here)[None, :] & (rank[None, :] == jnp.arange(PLACES, dtype=i32)[:, None])
    hits = jnp.sum(hits.reshape(PLACES, -1, 2).astype(f32), axis=2).astype(bf16)
    chosen = jnp.dot(hits, queries, preferred_element_type=f32).astype(bf16)
    chosen = chosen.reshape(PLACES, xs, -1).transpose(1, 0, 2)
    chosen = exchange(chosen, "x").reshape(xs * PLACES, -1)
    plane = flat // CORES
    core = flat - plane * CORES
    far = (core != lax.axis_index("core")).astype(i32)
    rows = (far * (GROUP // CORES * zs) + plane) * PLACES + rank
    return chosen, rows


def per_device(descriptors, neighbours, owned, queries, candidates):
    ys, zs, xs = lax.axis_size("y"), lax.axis_size("z"), lax.axis_size("x")
    rows, width = descriptors.shape
    everything = lax.all_gather(descriptors, ("z", "core"), axis=0, tiled=True)
    table = build_table(neighbours, owned, ys * zs * CORES)
    source, at = slot_orders(table, ys, zs)
    own = spread(descriptors, "y", ys).reshape(ys * rows, width)
    chosen, score_rows = query_entries(queries, candidates, xs, zs)
    source, at, own, chosen, score_rows = lax.optimization_barrier((source, at, own, chosen, score_rows))
    got, sims = similar_parts(everything, own, source, at)
    sims = spread(sims, "x", xs)
    parts = exchange(weighted_sums(got, sims, at), "y")
    summed, parts = score_parts(parts, descriptors, chosen, xs)
    whole = jnp.sum(exchange(parts, "x"), axis=0)
    scale = lax.rsqrt(whole[PLACES] / (xs * width) + 1e-06)
    augmented = (summed * scale[:, None]).astype(bf16)
    mine = whole[:PLACES] * (scale / math.sqrt(xs * width))[None, :]
    near = spread(spread(mine, "z", zs), "y", ys).reshape(-1, rows)
    far = lax.ppermute(near, "core", [(0, 1), (1, 0)])
    return augmented, pick_scores(score_rows, near, far)


def solution(mesh):
    shards, lanes = mesh.devices.shape
    ys = GROUP // CORES
    split = Mesh(mesh.devices.reshape(ys, shards // GROUP, CORES, lanes), ("y", "z", "core", "x"))
    shard = ("y", "z", "core")
    return jax.shard_map(
        per_device,
        mesh=split,
        in_specs=(P(shard, "x"), P(shard, None), P(shard, None), P("x", None), P("x", None)),
        out_specs=(P(shard, "x"), P("x", None)),
        check_vma=False,
    )
```

```python
import functools
import math

import jax
import jax.numpy as jnp
from jax import lax
from jax.experimental import pallas as pl
from jax.experimental.pallas import tpu as pltpu
from jax.sharding import Mesh
from jax.sharding import PartitionSpec as P

D = 2048
BLOCK = 128
PLACES = 16
GROUP = 8
CORES = 2
LANES = 128
SHARD = ("y", "z", "half", "core")
VMEM = 48 * 1024 * 1024
INTERPRET = False
STEPS = 2
HBM = pltpu.HBM
f32 = jnp.float32
bf16 = jnp.bfloat16
i16 = jnp.int16
i32 = jnp.int32
LEVELS = 32512.0
STEPS_PER_OCTAVE = 64.0
NT = (((1,), (1,)), ((), ()))
TN = (((0,), (0,)), ((), ()))


def exchange(parts, axis):
    return lax.all_to_all(parts, axis, split_axis=0, concat_axis=0, tiled=True)


def spread(part, axis, count):
    return exchange(jnp.broadcast_to(part[None], (count,) + part.shape), axis)


def hbm(shape, dtype):
    return jax.ShapeDtypeStruct(shape, dtype) if INTERPRET else pltpu.HBM(shape, dtype)


def pinned(value):
    return value if INTERPRET else pltpu.with_memory_space_constraint(value, HBM)


def params(**more):
    return pltpu.CompilerParams(vmem_limit_bytes=VMEM, **more)


def table_kernel(halves, listed_ref, owned_ref, high_ref, low_ref):
    rows = listed_ref.shape[0]
    row = lax.broadcasted_iota(i32, (rows, LANES), 0)
    lane = lax.broadcasted_iota(i32, (rows, LANES), 1)
    lower = (row > lane).astype(bf16)
    own_mark = (row + 1).astype(f32)
    before = jnp.zeros((1, LANES), f32)
    high = jnp.zeros((LANES, LANES), f32)
    low = jnp.zeros((LANES, LANES), f32)
    for slot in range(listed_ref.shape[1]):
        listed = listed_ref[:, slot : slot + 1]
        shard = lax.shift_right_logical(listed, 7)
        plane = shard // (4 * halves)
        half = lax.shift_right_logical(shard, 2) - plane * halves
        shard = (plane * 2 + (lax.shift_right_logical(shard, 1) & 1)) * (2 * halves) + half * 2 + (shard & 1)
        match = lane == shard
        ones = jnp.where(match, 1.0, 0.0)
        counted = jnp.dot(lower, ones.astype(bf16), preferred_element_type=f32) + before
        before = before + jnp.sum(ones, axis=0, keepdims=True)
        rank = jnp.sum(jnp.where(match, counted, 0.0), axis=1, keepdims=True).astype(i32)
        left = jnp.where(lane == lax.shift_right_logical(shard, 3), 1.0, 0.0).astype(bf16)
        here = lane == (shard & (GROUP - 1)) * PLACES + rank
        source = ((listed & (BLOCK - 1)) * 2 + owned_ref[:, slot : slot + 1]).astype(f32)
        high += lax.dot_general(left, jnp.where(here, own_mark, 0.0).astype(bf16), TN, preferred_element_type=f32)
        low += lax.dot_general(left, jnp.where(here, source, 0.0).astype(bf16), TN, preferred_element_type=f32)
    high_ref[...] = high[: high_ref.shape[0]]
    low_ref[...] = low[: low_ref.shape[0]]


def build_table(neighbours, owned, shards, halves):
    return pl.pallas_call(
        functools.partial(table_kernel, halves),
        out_shape=[jax.ShapeDtypeStruct((shards // GROUP, LANES), f32)] * 2,
        compiler_params=params(),
        interpret=INTERPRET,
        name="slot_table",
    )(neighbours, owned)


def similar_kernel(groups, all_ref, own_ref, src_ref, at_ref, got_ref, sims_ref):
    shards = own_ref.shape[0] // BLOCK
    kinds = 2 * shards
    slots = kinds * PLACES
    row = lax.broadcasted_iota(i32, (BLOCK, slots), 0)
    for group in range(groups):
        parts = []
        for one in range(group * GROUP, (group + 1) * GROUP):
            pick = jnp.where(row == src_ref[one : one + 1, :], 1.0, 0.0).astype(bf16)
            block = all_ref[one * BLOCK : (one + 1) * BLOCK, :]
            parts.append(lax.dot_general(pick, block, TN, preferred_element_type=f32).astype(bf16))
        sims = []
        for shard in range(shards):
            chunks = []
            for k in (2 * shard, 2 * shard + 1):
                chunk = jnp.concatenate([part[k * PLACES : (k + 1) * PLACES] for part in parts], axis=0)
                got_ref[k, group * LANES : (group + 1) * LANES, :] = chunk
                chunks.append(chunk)
            own = own_ref[shard * BLOCK : (shard + 1) * BLOCK, :]
            dots = lax.dot_general(own, jnp.concatenate(chunks, axis=0), NT, preferred_element_type=f32)
            for kind in range(2):
                n = group * kinds + 2 * shard + kind
                here = row[:, :LANES] == at_ref[n : n + 1, :]
                held = jnp.where(here, dots[:, kind * LANES : (kind + 1) * LANES], 0.0)
                sims.append(jnp.sum(held, axis=0, keepdims=True))
        sims_ref[group * kinds : (group + 1) * kinds, :] = jnp.concatenate(sims, axis=0)


def similar_parts(everything, own, source, at, steps=STEPS):
    width = own.shape[1]
    groups = everything.shape[0] // BLOCK // GROUP
    per = max(groups // steps, 1)
    kinds = 2 * own.shape[0] // BLOCK
    return pl.pallas_call(
        functools.partial(similar_kernel, per),
        grid=(groups // per,),
        in_specs=[
            pl.BlockSpec((per * GROUP * BLOCK, width), lambda i: (i, 0)),
            pl.BlockSpec(own.shape, lambda i: (0, 0)),
            pl.BlockSpec((per * GROUP, kinds * PLACES), lambda i: (i, 0)),
            pl.BlockSpec((per * kinds, LANES), lambda i: (i, 0)),
        ],
        out_specs=[
            pl.BlockSpec((kinds, per * LANES, width), lambda i: (0, i, 0)),
            pl.BlockSpec((per * kinds, LANES), lambda i: (i, 0)),
        ],
        out_shape=[
            hbm((kinds, groups * LANES, width), bf16),
            jax.ShapeDtypeStruct((groups * kinds, LANES), f32),
        ],
        compiler_params=params(),
        interpret=INTERPRET,
        name="similar_parts",
    )(pinned(everything), own, source, at)


def sum_kernel(got_ref, sims_ref, at_ref, sum_ref, held_ref, sems):
    shards = sum_ref.shape[0]
    copies = []
    for shard in range(shards):
        pair = slice(2 * shard, 2 * shard + 2)
        copies.append(pltpu.make_async_copy(got_ref.at[pair], held_ref.at[pair], sems.at[shard]))
        copies[-1].start()
    row = lax.broadcasted_iota(i32, (BLOCK, LANES), 0)
    similar = jnp.sum(sims_ref[:, : at_ref.shape[0], :], axis=0) / D
    weight = similar * similar * similar
    high = weight.astype(bf16).astype(f32)
    low = weight - high
    groups = at_ref.shape[0] // (2 * shards)
    for shard in range(shards):
        left_high, left_low = [], []
        for k in (2 * shard, 2 * shard + 1):
            for group in range(groups):
                n = group * 2 * shards + k
                here = row == at_ref[n : n + 1, :]
                left_high.append(jnp.where(here, high[n : n + 1], 0.0).astype(bf16))
                left_low.append(jnp.where(here, low[n : n + 1], 0.0).astype(bf16))
        copies[shard].wait()
        right = jnp.concatenate([held_ref[2 * shard], held_ref[2 * shard + 1]], axis=0)
        total = jnp.dot(jnp.concatenate(left_high, axis=1), right, preferred_element_type=f32)
        total += jnp.dot(jnp.concatenate(left_low, axis=1), right, preferred_element_type=f32)
        peak = jnp.maximum(jnp.max(jnp.abs(total), axis=1, keepdims=True), 1e-30)
        level = jnp.floor(jnp.log2(peak) * STEPS_PER_OCTAVE) + 1.0
        scale = LEVELS / jnp.exp2(level / STEPS_PER_OCTAVE)
        sum_ref[shard, :BLOCK, :] = jnp.floor(total * scale + 0.5).astype(i32).astype(i16)
        level = jnp.broadcast_to(level, (BLOCK, LANES)).T[:PLACES].astype(i32).astype(i16)
        sum_ref[shard, BLOCK:, :] = jnp.concatenate([level] * (total.shape[1] // LANES), axis=1)


def weighted_sums(got, sims, at):
    kinds, slots, width = got.shape
    vmem = pl.BlockSpec(memory_space=pltpu.VMEM)
    return pl.pallas_call(
        sum_kernel,
        in_specs=[pl.BlockSpec(memory_space=HBM), vmem, vmem],
        out_specs=vmem,
        out_shape=jax.ShapeDtypeStruct((kinds // 2, BLOCK + PLACES, width), i16),
        scratch_shapes=[pltpu.VMEM(got.shape, bf16), pltpu.SemaphoreType.DMA((kinds // 2,))],
        compiler_params=params(),
        interpret=INTERPRET,
        name="weighted_sums",
    )(pinned(got), sims, at)


def score_kernel(parts_ref, own_ref, chosen_ref, sum_ref, out_ref):
    total = own_ref[...].astype(f32)
    for part in range(parts_ref.shape[0]):
        level = parts_ref[part, BLOCK:, :LANES].astype(i32).astype(f32)[:1]
        level = jnp.broadcast_to(level, (BLOCK, LANES)).T[:, :1]
        scale = jnp.exp2(level / STEPS_PER_OCTAVE) / LEVELS
        total += parts_ref[part, :BLOCK, :].astype(i32).astype(f32) * scale
    sum_ref[...] = total
    energy = jnp.sum(total * total, axis=1, keepdims=True)
    energy = jnp.broadcast_to(energy, (BLOCK, LANES)).T[:8]
    high = total.astype(bf16)
    low = (total - high.astype(f32)).astype(bf16)
    lanes = out_ref.shape[0]
    quarters = total.shape[1] // LANES
    before = chosen_ref.shape[1] - quarters * PLACES
    scores = jnp.zeros((lanes * PLACES, LANES), f32)
    for quarter in range(quarters):
        at = before + quarter * PLACES
        chosen = jnp.concatenate([chosen_ref[lane, at : at + PLACES, :] for lane in range(lanes)], axis=0).astype(bf16)
        columns = slice(quarter * LANES, (quarter + 1) * LANES)
        scores += lax.dot_general(chosen, high[:, columns], NT, preferred_element_type=f32)
        scores += lax.dot_general(chosen, low[:, columns], NT, preferred_element_type=f32)
    for lane in range(out_ref.shape[0]):
        out_ref[lane, :PLACES, :] = scores[lane * PLACES : (lane + 1) * PLACES]
        out_ref[lane, PLACES:, :] = energy


def score_parts(parts, own, chosen, xs):
    return pl.pallas_call(
        score_kernel,
        out_shape=[
            jax.ShapeDtypeStruct(own.shape, f32),
            jax.ShapeDtypeStruct((xs, PLACES + 8, LANES), f32),
        ],
        compiler_params=params(),
        interpret=INTERPRET,
        name="score_parts",
    )(parts, own, chosen)


def pick_kernel(rows_ref, near_ref, far_ref, out_ref):
    count = near_ref.shape[0]

    def step(i, carry):
        for cand in range(2):
            picked = []
            for one in range(GROUP):
                r = rows_ref[i * (2 * GROUP) + 2 * one + cand]
                place = pl.ds(r & (count - 1), 1)
                picked.append(jnp.where(r < count, near_ref[place, :], far_ref[place, :]))
            at = pl.ds(pl.multiple_of(i * GROUP, GROUP), GROUP)
            out_ref[at, cand * LANES : (cand + 1) * LANES] = jnp.concatenate(picked, axis=0)
        return carry

    lax.fori_loop(0, out_ref.shape[0] // GROUP, step, 0, unroll=4)


def pick_scores(rows, near, far):
    queries = rows.shape[0] // 2
    vmem = pl.BlockSpec(memory_space=pltpu.VMEM)
    return pl.pallas_call(
        pick_kernel,
        in_specs=[pl.BlockSpec(memory_space=pltpu.SMEM), vmem, vmem],
        out_specs=vmem,
        out_shape=jax.ShapeDtypeStruct((queries, 2 * LANES), f32),
        compiler_params=params(),
        interpret=INTERPRET,
        name="pick_scores",
    )(rows, near, far)


def own_and_orders(descriptors, high, low, ys, halves):
    rows, width = descriptors.shape
    shards = 2 * ys
    count = halves * CORES
    groups = count // GROUP
    codes = jnp.concatenate([high.reshape(shards, -1), low.reshape(shards, -1)], axis=1).astype(bf16)
    codes = jnp.pad(codes, ((0, 0), (0, width - codes.shape[1])))
    codes = jnp.broadcast_to(codes[:, None, :], (shards, PLACES, width))
    sent = jnp.concatenate([jnp.broadcast_to(descriptors[None], (shards, rows, width)), codes], axis=1)
    came = exchange(sent, ("y", "half"))
    own = came[:, :rows, :].reshape(shards * rows, width)
    codes = came[:, rows, : 2 * groups * LANES].astype(i32).reshape(shards, 2, groups, LANES)
    ahead_own = codes[:, 0] - 1
    ahead_src = jnp.where(ahead_own >= 0, lax.shift_right_logical(codes[:, 1], 1), -1)
    back = jnp.where(high > 0, (high - 1) * 256 + low, -1).astype(i32)
    back = back.reshape(shards, count, PLACES).transpose(1, 0, 2).reshape(count, 1, shards * PLACES)
    back = exchange(back, ("z", "core")).reshape(count, shards, PLACES)
    held = (back >= 0) & ((back & 1) == 1)
    back_src = jnp.where(held, lax.shift_right_logical(back, 8), -1)
    back_own = jnp.where(held, lax.shift_right_logical(back, 1) & (BLOCK - 1), -1)
    source = jnp.stack([ahead_src.reshape(shards, count, PLACES).transpose(1, 0, 2), back_src], axis=2)
    at = jnp.stack([ahead_own, back_own.transpose(1, 0, 2).reshape(shards, groups, LANES)], axis=1)
    at = at.reshape(2 * shards, groups, LANES).transpose(1, 0, 2).reshape(groups * 2 * shards, LANES)
    return own, source.reshape(count, 2 * shards * PLACES), at


def query_entries(queries, candidates, xs, zs):
    flat = candidates.reshape(-1)
    order = jnp.arange(flat.shape[0], dtype=i32)
    earlier = (flat[:, None] == flat[None, :]) & (order[:, None] > order[None, :])
    rank = jnp.sum(earlier.astype(i32), axis=1)
    here = lax.axis_index(SHARD)
    hits = (flat == here)[None, :] & (rank[None, :] == jnp.arange(PLACES, dtype=i32)[:, None])
    hits = jnp.sum(hits.reshape(PLACES, -1, 2).astype(f32), axis=2).astype(bf16)
    chosen = jnp.dot(hits, queries, preferred_element_type=f32)
    chosen = chosen.reshape(PLACES, xs, -1, LANES).transpose(1, 2, 0, 3).reshape(xs, -1, LANES)
    plane = flat // CORES
    core = flat - plane * CORES
    far = (core != lax.axis_index("core")).astype(i32)
    rows = (far * (GROUP // CORES * zs) + plane) * PLACES + rank
    return chosen, rows


def per_device(descriptors, neighbours, owned, queries, candidates):
    ys, halves, xs = lax.axis_size("y"), lax.axis_size("z"), lax.axis_size("x")
    zs = 2 * halves
    rows, width = descriptors.shape
    everything = lax.all_gather(descriptors, ("z", "core"), axis=0, tiled=True)
    high, low = build_table(neighbours, owned, ys * zs * CORES, halves)
    own, source, at = own_and_orders(descriptors, high, low, ys, halves)
    chosen, score_rows = query_entries(queries, candidates, xs, zs)
    source, at, own, chosen, score_rows = lax.optimization_barrier((source, at, own, chosen, score_rows))
    got, sims = similar_parts(everything, own, source, at)
    sims = jnp.concatenate([jnp.broadcast_to(sims[None], (xs,) + sims.shape), chosen], axis=1)
    sims = exchange(sims, "x")
    parts = exchange(weighted_sums(got, sims, at), ("y", "half"))
    summed, parts = score_parts(parts, descriptors, sims, xs)
    whole = jnp.sum(exchange(parts, "x"), axis=0)
    scale = lax.rsqrt(whole[PLACES] / (xs * width) + 1e-06)
    augmented = (summed * scale[:, None]).astype(bf16)
    mine = whole[:PLACES] * (scale / math.sqrt(xs * width))[None, :]
    near = spread(spread(mine, ("z", "half"), zs), "y", ys).reshape(-1, rows)
    far = lax.ppermute(near, "core", [(0, 1), (1, 0)])
    return augmented, pick_scores(score_rows, near, far)


def solution(mesh):
    shards, lanes = mesh.devices.shape
    ys = GROUP // CORES
    devices = mesh.devices.reshape(ys, shards // GROUP // 2, 2, CORES, lanes)
    return jax.shard_map(
        per_device,
        mesh=Mesh(devices, SHARD + ("x",)),
        in_specs=(P(SHARD, "x"), P(SHARD, None), P(SHARD, None), P("x", None), P("x", None)),
        out_specs=(P(SHARD, "x"), P("x", None)),
        check_vma=False,
    )
```

```python
import functools
import math

import jax
import jax.numpy as jnp
from jax import lax
from jax.experimental import pallas as pl
from jax.experimental.pallas import tpu as pltpu
from jax.sharding import Mesh
from jax.sharding import PartitionSpec as P

D = 2048
BLOCK = 128
PLACES = 16
GROUP = 8
CORES = 2
LANES = 128
SHARD = ("y", "z", "half", "core")
VMEM = 48 * 1024 * 1024
INTERPRET = False
STEPS = 2
HBM = pltpu.HBM
f32 = jnp.float32
bf16 = jnp.bfloat16
i16 = jnp.int16
i32 = jnp.int32
LEVELS = 32512.0
STEPS_PER_OCTAVE = 64.0
NT = (((1,), (1,)), ((), ()))
TN = (((0,), (0,)), ((), ()))


def exchange(parts, axis):
    return lax.all_to_all(parts, axis, split_axis=0, concat_axis=0, tiled=True)


def spread(part, axis, count):
    return exchange(jnp.broadcast_to(part[None], (count,) + part.shape), axis)


def hbm(shape, dtype):
    return jax.ShapeDtypeStruct(shape, dtype) if INTERPRET else pltpu.HBM(shape, dtype)


def pinned(value):
    return value if INTERPRET else pltpu.with_memory_space_constraint(value, HBM)


def params(**more):
    return pltpu.CompilerParams(vmem_limit_bytes=VMEM, **more)


def table_kernel(halves, listed_ref, owned_ref, high_ref, low_ref):
    rows = listed_ref.shape[0]
    row = lax.broadcasted_iota(i32, (rows, LANES), 0)
    lane = lax.broadcasted_iota(i32, (rows, LANES), 1)
    lower = (row > lane).astype(bf16)
    own_mark = (row + 1).astype(f32)
    before = jnp.zeros((1, LANES), f32)
    high = jnp.zeros((LANES, LANES), f32)
    low = jnp.zeros((LANES, LANES), f32)
    for slot in range(listed_ref.shape[1]):
        listed = listed_ref[:, slot : slot + 1]
        shard = lax.shift_right_logical(listed, 7)
        plane = shard // (4 * halves)
        half = lax.shift_right_logical(shard, 2) - plane * halves
        shard = (plane * 2 + (lax.shift_right_logical(shard, 1) & 1)) * (2 * halves) + half * 2 + (shard & 1)
        match = lane == shard
        ones = jnp.where(match, 1.0, 0.0)
        counted = jnp.dot(lower, ones.astype(bf16), preferred_element_type=f32) + before
        before = before + jnp.sum(ones, axis=0, keepdims=True)
        rank = jnp.sum(jnp.where(match, counted, 0.0), axis=1, keepdims=True).astype(i32)
        left = jnp.where(lane == lax.shift_right_logical(shard, 3), 1.0, 0.0).astype(bf16)
        here = lane == (shard & (GROUP - 1)) * PLACES + rank
        source = ((listed & (BLOCK - 1)) * 2 + owned_ref[:, slot : slot + 1]).astype(f32)
        high += lax.dot_general(left, jnp.where(here, own_mark, 0.0).astype(bf16), TN, preferred_element_type=f32)
        low += lax.dot_general(left, jnp.where(here, source, 0.0).astype(bf16), TN, preferred_element_type=f32)
    high_ref[...] = high[: high_ref.shape[0]]
    low_ref[...] = low[: low_ref.shape[0]]


def build_table(neighbours, owned, shards, halves):
    return pl.pallas_call(
        functools.partial(table_kernel, halves),
        out_shape=[jax.ShapeDtypeStruct((shards // GROUP, LANES), f32)] * 2,
        compiler_params=params(),
        interpret=INTERPRET,
        name="slot_table",
    )(neighbours, owned)


def similar_kernel(groups, all_ref, own_ref, src_ref, at_ref, got_ref, sims_ref):
    shards = own_ref.shape[0] // BLOCK
    kinds = 2 * shards
    slots = kinds * PLACES
    row = lax.broadcasted_iota(i32, (BLOCK, slots), 0)
    for group in range(groups):
        parts = []
        for one in range(group * GROUP, (group + 1) * GROUP):
            pick = jnp.where(row == src_ref[one : one + 1, :], 1.0, 0.0).astype(bf16)
            block = all_ref[one * BLOCK : (one + 1) * BLOCK, :]
            parts.append(lax.dot_general(pick, block, TN, preferred_element_type=f32).astype(bf16))
        sims = []
        for shard in range(shards):
            chunks = []
            for k in (2 * shard, 2 * shard + 1):
                chunk = jnp.concatenate([part[k * PLACES : (k + 1) * PLACES] for part in parts], axis=0)
                got_ref[k, group * LANES : (group + 1) * LANES, :] = chunk
                chunks.append(chunk)
            own = own_ref[shard * BLOCK : (shard + 1) * BLOCK, :]
            dots = lax.dot_general(own, jnp.concatenate(chunks, axis=0), NT, preferred_element_type=f32)
            for kind in range(2):
                n = group * kinds + 2 * shard + kind
                here = row[:, :LANES] == at_ref[n : n + 1, :]
                held = jnp.where(here, dots[:, kind * LANES : (kind + 1) * LANES], 0.0)
                sims.append(jnp.sum(held, axis=0, keepdims=True))
        sims_ref[group * kinds : (group + 1) * kinds, :] = jnp.concatenate(sims, axis=0)


def similar_parts(everything, own, source, at, steps=STEPS):
    width = own.shape[1]
    groups = everything.shape[0] // BLOCK // GROUP
    per = max(groups // steps, 1)
    kinds = 2 * own.shape[0] // BLOCK
    return pl.pallas_call(
        functools.partial(similar_kernel, per),
        grid=(groups // per,),
        in_specs=[
            pl.BlockSpec((per * GROUP * BLOCK, width), lambda i: (i, 0)),
            pl.BlockSpec(own.shape, lambda i: (0, 0)),
            pl.BlockSpec((per * GROUP, kinds * PLACES), lambda i: (i, 0)),
            pl.BlockSpec((per * kinds, LANES), lambda i: (i, 0)),
        ],
        out_specs=[
            pl.BlockSpec((kinds, per * LANES, width), lambda i: (0, i, 0)),
            pl.BlockSpec((per * kinds, LANES), lambda i: (i, 0)),
        ],
        out_shape=[
            hbm((kinds, groups * LANES, width), bf16),
            jax.ShapeDtypeStruct((groups * kinds, LANES), f32),
        ],
        compiler_params=params(),
        interpret=INTERPRET,
        name="similar_parts",
    )(pinned(everything), own, source, at)


def sum_kernel(got_ref, sims_ref, at_ref, sum_ref, held_ref, sems):
    shards = sum_ref.shape[0]
    copies = []
    for shard in range(shards):
        pair = slice(2 * shard, 2 * shard + 2)
        copies.append(pltpu.make_async_copy(got_ref.at[pair], held_ref.at[pair], sems.at[shard]))
        copies[-1].start()
    row = lax.broadcasted_iota(i32, (BLOCK, LANES), 0)
    similar = jnp.sum(sims_ref[:, : at_ref.shape[0], :], axis=0) / D
    weight = similar * similar * similar
    high = weight.astype(bf16).astype(f32)
    low = weight - high
    groups = at_ref.shape[0] // (2 * shards)
    for shard in range(shards):
        left_high, left_low = [], []
        for k in (2 * shard, 2 * shard + 1):
            for group in range(groups):
                n = group * 2 * shards + k
                here = row == at_ref[n : n + 1, :]
                left_high.append(jnp.where(here, high[n : n + 1], 0.0).astype(bf16))
                left_low.append(jnp.where(here, low[n : n + 1], 0.0).astype(bf16))
        copies[shard].wait()
        right = jnp.concatenate([held_ref[2 * shard], held_ref[2 * shard + 1]], axis=0)
        total = jnp.dot(jnp.concatenate(left_high, axis=1), right, preferred_element_type=f32)
        total += jnp.dot(jnp.concatenate(left_low, axis=1), right, preferred_element_type=f32)
        peak = jnp.maximum(jnp.max(jnp.abs(total), axis=1, keepdims=True), 1e-30)
        level = jnp.floor(jnp.log2(peak) * STEPS_PER_OCTAVE) + 1.0
        scale = LEVELS / jnp.exp2(level / STEPS_PER_OCTAVE)
        sum_ref[shard, :BLOCK, :] = jnp.floor(total * scale + 0.5).astype(i32).astype(i16)
        level = jnp.broadcast_to(level, (BLOCK, LANES)).T[:PLACES].astype(i32).astype(i16)
        sum_ref[shard, BLOCK:, :] = jnp.concatenate([level] * (total.shape[1] // LANES), axis=1)


def weighted_sums(got, sims, at):
    kinds, slots, width = got.shape
    vmem = pl.BlockSpec(memory_space=pltpu.VMEM)
    return pl.pallas_call(
        sum_kernel,
        in_specs=[pl.BlockSpec(memory_space=HBM), vmem, vmem],
        out_specs=vmem,
        out_shape=jax.ShapeDtypeStruct((kinds // 2, BLOCK + PLACES, width), i16),
        scratch_shapes=[pltpu.VMEM(got.shape, bf16), pltpu.SemaphoreType.DMA((kinds // 2,))],
        compiler_params=params(),
        interpret=INTERPRET,
        name="weighted_sums",
    )(pinned(got), sims, at)


def score_kernel(parts_ref, own_ref, chosen_ref, sum_ref, out_ref):
    total = own_ref[...].astype(f32)
    for part in range(parts_ref.shape[0]):
        level = parts_ref[part, BLOCK:, :LANES].astype(i32).astype(f32)[:1]
        level = jnp.broadcast_to(level, (BLOCK, LANES)).T[:, :1]
        scale = jnp.exp2(level / STEPS_PER_OCTAVE) / LEVELS
        total += parts_ref[part, :BLOCK, :].astype(i32).astype(f32) * scale
    sum_ref[...] = total
    energy = jnp.sum(total * total, axis=1, keepdims=True)
    energy = jnp.broadcast_to(energy, (BLOCK, LANES)).T[:8]
    high = total.astype(bf16)
    low = (total - high.astype(f32)).astype(bf16)
    lanes = out_ref.shape[0]
    quarters = total.shape[1] // LANES
    before = chosen_ref.shape[1] - quarters * PLACES
    scores = jnp.zeros((lanes * PLACES, LANES), f32)
    for quarter in range(quarters):
        at = before + quarter * PLACES
        chosen = jnp.concatenate([chosen_ref[lane, at : at + PLACES, :] for lane in range(lanes)], axis=0).astype(bf16)
        columns = slice(quarter * LANES, (quarter + 1) * LANES)
        scores += lax.dot_general(chosen, high[:, columns], NT, preferred_element_type=f32)
        scores += lax.dot_general(chosen, low[:, columns], NT, preferred_element_type=f32)
    for lane in range(out_ref.shape[0]):
        out_ref[lane, :PLACES, :] = scores[lane * PLACES : (lane + 1) * PLACES]
        out_ref[lane, PLACES:, :] = energy


def score_parts(parts, own, chosen, xs):
    return pl.pallas_call(
        score_kernel,
        out_shape=[
            jax.ShapeDtypeStruct(own.shape, f32),
            jax.ShapeDtypeStruct((xs, PLACES + 8, LANES), f32),
        ],
        compiler_params=params(),
        interpret=INTERPRET,
        name="score_parts",
    )(parts, own, chosen)


def pick_kernel(rows_ref, near_ref, far_ref, out_ref):
    count = near_ref.shape[0]

    def step(i, carry):
        for cand in range(2):
            picked = []
            for one in range(GROUP):
                r = rows_ref[i * (2 * GROUP) + 2 * one + cand]
                place = pl.ds(r & (count - 1), 1)
                picked.append(jnp.where(r < count, near_ref[place, :], far_ref[place, :]))
            at = pl.ds(pl.multiple_of(i * GROUP, GROUP), GROUP)
            out_ref[at, cand * LANES : (cand + 1) * LANES] = jnp.concatenate(picked, axis=0)
        return carry

    lax.fori_loop(0, out_ref.shape[0] // GROUP, step, 0, unroll=4)


def pick_scores(rows, near, far):
    queries = rows.shape[0] // 2
    vmem = pl.BlockSpec(memory_space=pltpu.VMEM)
    return pl.pallas_call(
        pick_kernel,
        in_specs=[pl.BlockSpec(memory_space=pltpu.SMEM), vmem, vmem],
        out_specs=vmem,
        out_shape=jax.ShapeDtypeStruct((queries, 2 * LANES), f32),
        compiler_params=params(),
        interpret=INTERPRET,
        name="pick_scores",
    )(rows, near, far)


def slot_orders(high, low, ys, halves):
    shards = 2 * ys
    count = halves * CORES
    groups = count // GROUP
    codes = jnp.concatenate([high.reshape(shards, -1), low.reshape(shards, -1)], axis=1)
    codes = exchange(codes.astype(i32).reshape(shards, 2 * groups, LANES), ("y", "half"))
    codes = codes.reshape(shards, 2, groups, LANES)
    ahead_own = codes[:, 0] - 1
    ahead_src = jnp.where(ahead_own >= 0, lax.shift_right_logical(codes[:, 1], 1), -1)
    back = jnp.where(high > 0, (high - 1) * 256 + low, -1).astype(i32)
    back = back.reshape(shards, count, PLACES).transpose(1, 0, 2).reshape(count, 1, shards * PLACES)
    back = exchange(back, ("z", "core")).reshape(count, shards, PLACES)
    held = (back >= 0) & ((back & 1) == 1)
    back_src = jnp.where(held, lax.shift_right_logical(back, 8), -1)
    back_own = jnp.where(held, lax.shift_right_logical(back, 1) & (BLOCK - 1), -1)
    source = jnp.stack([ahead_src.reshape(shards, count, PLACES).transpose(1, 0, 2), back_src], axis=2)
    at = jnp.stack([ahead_own, back_own.transpose(1, 0, 2).reshape(shards, groups, LANES)], axis=1)
    at = at.reshape(2 * shards, groups, LANES).transpose(1, 0, 2).reshape(groups * 2 * shards, LANES)
    return source.reshape(count, 2 * shards * PLACES), at


def query_entries(queries, candidates, xs, zs):
    flat = candidates.reshape(-1)
    order = jnp.arange(flat.shape[0], dtype=i32)
    earlier = (flat[:, None] == flat[None, :]) & (order[:, None] > order[None, :])
    rank = jnp.sum(earlier.astype(i32), axis=1)
    here = lax.axis_index(SHARD)
    hits = (flat == here)[None, :] & (rank[None, :] == jnp.arange(PLACES, dtype=i32)[:, None])
    hits = jnp.sum(hits.reshape(PLACES, -1, 2).astype(f32), axis=2).astype(bf16)
    chosen = jnp.dot(hits, queries, preferred_element_type=f32)
    chosen = chosen.reshape(PLACES, xs, -1, LANES).transpose(1, 2, 0, 3).reshape(xs, -1, LANES)
    plane = flat // CORES
    core = flat - plane * CORES
    far = (core != lax.axis_index("core")).astype(i32)
    rows = (far * (GROUP // CORES * zs) + plane) * PLACES + rank
    return chosen, rows


def per_device(descriptors, neighbours, owned, queries, candidates):
    ys, halves, xs = lax.axis_size("y"), lax.axis_size("z"), lax.axis_size("x")
    zs = 2 * halves
    rows, width = descriptors.shape
    everything = lax.all_gather(descriptors, ("z", "core"), axis=0, tiled=True)
    near = spread(descriptors, "y", ys)
    far = lax.ppermute(near, "half", [(0, 1), (1, 0)])
    first = lax.axis_index("half") == 0
    own = jnp.stack([jnp.where(first, near, far), jnp.where(first, far, near)], axis=1)
    own = own.reshape(2 * ys * rows, width)
    high, low = build_table(neighbours, owned, ys * zs * CORES, halves)
    source, at = slot_orders(high, low, ys, halves)
    chosen, score_rows = query_entries(queries, candidates, xs, zs)
    source, at, own, chosen, score_rows = lax.optimization_barrier((source, at, own, chosen, score_rows))
    got, sims = similar_parts(everything, own, source, at)
    sims = jnp.concatenate([jnp.broadcast_to(sims[None], (xs,) + sims.shape), chosen], axis=1)
    sims = exchange(sims, "x")
    parts = exchange(weighted_sums(got, sims, at), ("y", "half"))
    summed, parts = score_parts(parts, descriptors, sims, xs)
    whole = jnp.sum(exchange(parts, "x"), axis=0)
    scale = lax.rsqrt(whole[PLACES] / (xs * width) + 1e-06)
    augmented = (summed * scale[:, None]).astype(bf16)
    mine = whole[:PLACES] * (scale / math.sqrt(xs * width))[None, :]
    near = spread(spread(mine, ("z", "half"), zs), "y", ys).reshape(-1, rows)
    far = lax.ppermute(near, "core", [(0, 1), (1, 0)])
    return augmented, pick_scores(score_rows, near, far)


def solution(mesh):
    shards, lanes = mesh.devices.shape
    ys = GROUP // CORES
    devices = mesh.devices.reshape(ys, shards // GROUP // 2, 2, CORES, lanes)
    return jax.shard_map(
        per_device,
        mesh=Mesh(devices, SHARD + ("x",)),
        in_specs=(P(SHARD, "x"), P(SHARD, None), P(SHARD, None), P("x", None), P("x", None)),
        out_specs=(P(SHARD, "x"), P("x", None)),
        check_vma=False,
    )
```

```python
import functools
import math

import jax
import jax.numpy as jnp
from jax import lax
from jax.experimental import pallas as pl
from jax.experimental.pallas import tpu as pltpu
from jax.sharding import Mesh
from jax.sharding import PartitionSpec as P

D = 2048
BLOCK = 128
PLACES = 16
GROUP = 8
CORES = 2
LANES = 128
SHARD = ("y", "z", "half", "core")
VMEM = 48 * 1024 * 1024
INTERPRET = False
SPLIT = 1
LEAVE = 2
JOIN = 4
HBM = pltpu.HBM
f32 = jnp.float32
bf16 = jnp.bfloat16
i16 = jnp.int16
i32 = jnp.int32
LEVELS = 32512.0
STEPS_PER_OCTAVE = 64.0
NT = (((1,), (1,)), ((), ()))
TN = (((0,), (0,)), ((), ()))


def exchange(parts, axis):
    return lax.all_to_all(parts, axis, split_axis=0, concat_axis=0, tiled=True)


def spread(part, axis, count):
    return exchange(jnp.broadcast_to(part[None], (count,) + part.shape), axis)


def hbm(shape, dtype):
    return jax.ShapeDtypeStruct(shape, dtype) if INTERPRET else pltpu.HBM(shape, dtype)


def pinned(value):
    return value if INTERPRET else pltpu.with_memory_space_constraint(value, HBM)


def params(**more):
    return pltpu.CompilerParams(vmem_limit_bytes=VMEM, **more)


def table_kernel(halves, listed_ref, owned_ref, high_ref, low_ref):
    rows = listed_ref.shape[0]
    row = lax.broadcasted_iota(i32, (rows, LANES), 0)
    lane = lax.broadcasted_iota(i32, (rows, LANES), 1)
    lower = (row > lane).astype(bf16)
    own_mark = (row + 1).astype(f32)
    before = jnp.zeros((1, LANES), f32)
    high = jnp.zeros((LANES, LANES), f32)
    low = jnp.zeros((LANES, LANES), f32)
    for slot in range(listed_ref.shape[1]):
        listed = listed_ref[:, slot : slot + 1]
        shard = lax.shift_right_logical(listed, 7)
        plane = shard // (4 * halves)
        half = lax.shift_right_logical(shard, 2) - plane * halves
        shard = (plane * 2 + (lax.shift_right_logical(shard, 1) & 1)) * (2 * halves) + half * 2 + (shard & 1)
        match = lane == shard
        ones = jnp.where(match, 1.0, 0.0)
        counted = jnp.dot(lower, ones.astype(bf16), preferred_element_type=f32) + before
        before = before + jnp.sum(ones, axis=0, keepdims=True)
        rank = jnp.sum(jnp.where(match, counted, 0.0), axis=1, keepdims=True).astype(i32)
        left = jnp.where(lane == lax.shift_right_logical(shard, 3), 1.0, 0.0).astype(bf16)
        here = lane == (shard & (GROUP - 1)) * PLACES + rank
        source = ((listed & (BLOCK - 1)) * 2 + owned_ref[:, slot : slot + 1]).astype(f32)
        high += lax.dot_general(left, jnp.where(here, own_mark, 0.0).astype(bf16), TN, preferred_element_type=f32)
        low += lax.dot_general(left, jnp.where(here, source, 0.0).astype(bf16), TN, preferred_element_type=f32)
    high_ref[...] = high[: high_ref.shape[0]]
    low_ref[...] = low[: low_ref.shape[0]]


def build_table(neighbours, owned, shards, halves):
    return pl.pallas_call(
        functools.partial(table_kernel, halves),
        out_shape=[jax.ShapeDtypeStruct((shards // GROUP, LANES), f32)] * 2,
        compiler_params=params(),
        interpret=INTERPRET,
        name="slot_table",
    )(neighbours, owned)


def similar_kernel(all_ref, own_ref, src_ref, at_ref, got_ref, sims_ref, held_ref, out_ref, in_sems, out_sems):
    shards = own_ref.shape[0] // BLOCK
    kinds = 2 * shards
    slots = kinds * PLACES
    groups = src_ref.shape[0] // GROUP
    arrivals, departures = [], []
    for part in range(groups * SPLIT):
        rows = pl.ds(part * (GROUP // SPLIT) * BLOCK, GROUP // SPLIT * BLOCK)
        arrivals.append(pltpu.make_async_copy(all_ref.at[rows], held_ref.at[rows], in_sems.at[part]))
        arrivals[-1].start()
    row = lax.broadcasted_iota(i32, (BLOCK, slots), 0)
    for group in range(groups):
        parts = []
        for one in range(group * GROUP, (group + 1) * GROUP):
            pick = jnp.where(row == src_ref[one : one + 1, :], 1.0, 0.0).astype(bf16)
            if one % (GROUP // SPLIT) == 0:
                arrivals[one // (GROUP // SPLIT)].wait()
            block = held_ref[one * BLOCK : (one + 1) * BLOCK, :]
            parts.append(lax.dot_general(pick, block, TN, preferred_element_type=f32).astype(bf16))
        sims = []
        for shard in range(shards):
            chunks = []
            for k in (2 * shard, 2 * shard + 1):
                chunk = jnp.concatenate([part[k * PLACES : (k + 1) * PLACES] for part in parts], axis=0)
                out_ref[group, k] = chunk
                chunks.append(chunk)
            own = own_ref[shard * BLOCK : (shard + 1) * BLOCK, :]
            dots = lax.dot_general(own, jnp.concatenate(chunks, axis=0), NT, preferred_element_type=f32)
            for kind in range(2):
                n = group * kinds + 2 * shard + kind
                here = row[:, :LANES] == at_ref[n : n + 1, :]
                held = jnp.where(here, dots[:, kind * LANES : (kind + 1) * LANES], 0.0)
                sims.append(jnp.sum(held, axis=0, keepdims=True))
            if (shard + 1) % LEAVE == 0:
                some = pl.ds(2 * (shard + 1 - LEAVE), 2 * LEAVE)
                sem = out_sems.at[len(departures)]
                departures.append(pltpu.make_async_copy(out_ref.at[group, some], got_ref.at[group, some], sem))
                departures[-1].start()
        sims_ref[group * kinds : (group + 1) * kinds, :] = jnp.concatenate(sims, axis=0)
    for departure in departures:
        departure.wait()


def similar_parts(everything, own, source, at):
    width = own.shape[1]
    groups = everything.shape[0] // BLOCK // GROUP
    kinds = 2 * own.shape[0] // BLOCK
    vmem = pl.BlockSpec(memory_space=pltpu.VMEM)
    outside = pl.BlockSpec(memory_space=HBM)
    shape = (groups, kinds, LANES, width)
    return pl.pallas_call(
        similar_kernel,
        in_specs=[outside, vmem, vmem, vmem],
        out_specs=[outside, vmem],
        out_shape=[hbm(shape, bf16), jax.ShapeDtypeStruct((groups * kinds, LANES), f32)],
        scratch_shapes=[
            pltpu.VMEM(everything.shape, bf16),
            pltpu.VMEM(shape, bf16),
            pltpu.SemaphoreType.DMA((groups * SPLIT,)),
            pltpu.SemaphoreType.DMA((groups * kinds // 2 // LEAVE,)),
        ],
        compiler_params=params(),
        interpret=INTERPRET,
        name="similar_parts",
    )(pinned(everything), own, source, at)


def sum_kernel(got_ref, sims_ref, at_ref, sum_ref, held_ref, sems):
    shards = sum_ref.shape[0]
    copies = []
    for some in range(shards // JOIN):
        kinds = pl.ds(2 * JOIN * some, 2 * JOIN)
        copies.append(pltpu.make_async_copy(got_ref.at[:, kinds], held_ref.at[:, kinds], sems.at[some]))
        copies[-1].start()
    row = lax.broadcasted_iota(i32, (BLOCK, LANES), 0)
    similar = jnp.sum(sims_ref[:, : at_ref.shape[0], :], axis=0) / D
    weight = similar * similar * similar
    high = weight.astype(bf16).astype(f32)
    low = weight - high
    groups = at_ref.shape[0] // (2 * shards)
    for shard in range(shards):
        left_high, left_low = [], []
        for k in (2 * shard, 2 * shard + 1):
            for group in range(groups):
                n = group * 2 * shards + k
                here = row == at_ref[n : n + 1, :]
                left_high.append(jnp.where(here, high[n : n + 1], 0.0).astype(bf16))
                left_low.append(jnp.where(here, low[n : n + 1], 0.0).astype(bf16))
        if shard % JOIN == 0:
            copies[shard // JOIN].wait()
        pair = (2 * shard, 2 * shard + 1)
        right = jnp.concatenate([held_ref[group, k] for k in pair for group in range(groups)], axis=0)
        total = jnp.dot(jnp.concatenate(left_high, axis=1), right, preferred_element_type=f32)
        total += jnp.dot(jnp.concatenate(left_low, axis=1), right, preferred_element_type=f32)
        peak = jnp.maximum(jnp.max(jnp.abs(total), axis=1, keepdims=True), 1e-30)
        level = jnp.floor(jnp.log2(peak) * STEPS_PER_OCTAVE) + 1.0
        scale = LEVELS / jnp.exp2(level / STEPS_PER_OCTAVE)
        sum_ref[shard, :BLOCK, :] = jnp.floor(total * scale + 0.5).astype(i32).astype(i16)
        level = jnp.broadcast_to(level, (BLOCK, LANES)).T[:PLACES].astype(i32).astype(i16)
        sum_ref[shard, BLOCK:, :] = jnp.concatenate([level] * (total.shape[1] // LANES), axis=1)


def weighted_sums(got, sims, at):
    kinds, width = got.shape[1], got.shape[3]
    vmem = pl.BlockSpec(memory_space=pltpu.VMEM)
    return pl.pallas_call(
        sum_kernel,
        in_specs=[pl.BlockSpec(memory_space=HBM), vmem, vmem],
        out_specs=vmem,
        out_shape=jax.ShapeDtypeStruct((kinds // 2, BLOCK + PLACES, width), i16),
        scratch_shapes=[pltpu.VMEM(got.shape, bf16), pltpu.SemaphoreType.DMA((kinds // 2 // JOIN,))],
        compiler_params=params(),
        interpret=INTERPRET,
        name="weighted_sums",
    )(pinned(got), sims, at)


def score_kernel(parts_ref, own_ref, chosen_ref, sum_ref, out_ref):
    total = own_ref[...].astype(f32)
    for part in range(parts_ref.shape[0]):
        level = parts_ref[part, BLOCK:, :LANES].astype(i32).astype(f32)[:1]
        level = jnp.broadcast_to(level, (BLOCK, LANES)).T[:, :1]
        scale = jnp.exp2(level / STEPS_PER_OCTAVE) / LEVELS
        total += parts_ref[part, :BLOCK, :].astype(i32).astype(f32) * scale
    sum_ref[...] = total
    energy = jnp.sum(total * total, axis=1, keepdims=True)
    energy = jnp.broadcast_to(energy, (BLOCK, LANES)).T[:8]
    high = total.astype(bf16)
    low = (total - high.astype(f32)).astype(bf16)
    lanes = chosen_ref.shape[0]
    quarters = total.shape[1] // LANES
    before = chosen_ref.shape[1] - quarters * PLACES
    scores = jnp.zeros((lanes * PLACES, LANES), f32)
    for quarter in range(quarters):
        at = before + quarter * PLACES
        chosen = jnp.concatenate([chosen_ref[lane, at : at + PLACES, :] for lane in range(lanes)], axis=0).astype(bf16)
        columns = slice(quarter * LANES, (quarter + 1) * LANES)
        scores += lax.dot_general(chosen, high[:, columns], NT, preferred_element_type=f32)
        scores += lax.dot_general(chosen, low[:, columns], NT, preferred_element_type=f32)
    for place in range(out_ref.shape[0]):
        lane = place % lanes
        out_ref[place, :PLACES, :] = scores[lane * PLACES : (lane + 1) * PLACES]
        out_ref[place, PLACES:, :] = energy


def score_parts(parts, own, chosen, places):
    return pl.pallas_call(
        score_kernel,
        out_shape=[
            jax.ShapeDtypeStruct(own.shape, f32),
            jax.ShapeDtypeStruct((places, PLACES + 8, LANES), f32),
        ],
        compiler_params=params(),
        interpret=INTERPRET,
        name="score_parts",
    )(parts, own, chosen)


def finish_kernel(depth, parts_ref, out_ref, scale_ref):
    ys = scale_ref.shape[0]
    lanes = parts_ref.shape[0] // ys
    scores = []
    for y in range(ys):
        whole = parts_ref[y * lanes]
        for lane in range(1, lanes):
            whole += parts_ref[y * lanes + lane]
        scale = lax.rsqrt(whole[PLACES:] / depth + 1e-06)
        scale_ref[y] = scale
        scores.append(whole[:PLACES] * (scale[:1] / math.sqrt(depth)))
    scores = jnp.concatenate(scores, axis=0)
    peak = jnp.max(jnp.max(jnp.abs(scores), axis=0, keepdims=True), axis=1, keepdims=True)
    level = jnp.floor(jnp.log2(jnp.maximum(peak, 1e-30)) * STEPS_PER_OCTAVE) + 1.0
    level = jnp.broadcast_to(level, (PLACES, LANES))
    count = scores.shape[0]
    scores = scores * (LEVELS / jnp.exp2(level[:1] / STEPS_PER_OCTAVE))
    out_ref[:count, :] = jnp.floor(scores + 0.5).astype(i32).astype(i16)
    out_ref[count:, :] = level.astype(i32).astype(i16)


def finish_scores(parts, ys, depth):
    return pl.pallas_call(
        functools.partial(finish_kernel, depth),
        out_shape=[
            jax.ShapeDtypeStruct(((ys + 1) * PLACES, LANES), i16),
            jax.ShapeDtypeStruct((ys, 8, LANES), f32),
        ],
        compiler_params=params(),
        interpret=INTERPRET,
        name="finish_scores",
    )(parts)


def pick_kernel(rows_ref, near_ref, far_ref, out_ref, table_ref):
    planes, held, _ = near_ref.shape
    count = held - PLACES
    for side, ref in enumerate((near_ref, far_ref)):
        for plane in range(planes):
            level = ref[plane, count:, :].astype(i32).astype(f32)[:1]
            scores = ref[plane, :count, :].astype(i32).astype(f32) * (jnp.exp2(level / STEPS_PER_OCTAVE) / LEVELS)
            table_ref[(side * planes + plane) * count : (side * planes + plane + 1) * count, :] = scores

    def step(i, carry):
        for cand in range(2):
            picked = []
            for one in range(GROUP):
                r = rows_ref[i * (2 * GROUP) + 2 * one + cand]
                picked.append(table_ref[pl.ds(r, 1), :])
            at = pl.ds(pl.multiple_of(i * GROUP, GROUP), GROUP)
            out_ref[at, cand * LANES : (cand + 1) * LANES] = jnp.concatenate(picked, axis=0)
        return carry

    lax.fori_loop(0, out_ref.shape[0] // GROUP, step, 0, unroll=8)


def pick_scores(rows, near, far):
    queries = rows.shape[0] // 2
    vmem = pl.BlockSpec(memory_space=pltpu.VMEM)
    planes, held, _ = near.shape
    return pl.pallas_call(
        pick_kernel,
        in_specs=[pl.BlockSpec(memory_space=pltpu.SMEM), vmem, vmem],
        out_specs=vmem,
        out_shape=jax.ShapeDtypeStruct((queries, 2 * LANES), f32),
        scratch_shapes=[pltpu.VMEM((2 * planes * (held - PLACES), LANES), f32)],
        compiler_params=params(),
        interpret=INTERPRET,
        name="pick_scores",
    )(rows, near, far)


def slot_orders(high, low, ys, halves):
    shards = 2 * ys
    count = halves * CORES
    groups = count // GROUP
    codes = jnp.concatenate([high.reshape(shards, -1), low.reshape(shards, -1)], axis=1)
    codes = exchange(codes.astype(i32).reshape(shards, 2 * groups, LANES), ("y", "half"))
    codes = codes.reshape(shards, 2, groups, LANES)
    ahead_own = codes[:, 0] - 1
    ahead_src = jnp.where(ahead_own >= 0, lax.shift_right_logical(codes[:, 1], 1), -1)
    back = jnp.where(high > 0, (high - 1) * 256 + low, -1).astype(i32)
    back = back.reshape(shards, count, PLACES).transpose(1, 0, 2).reshape(count, 1, shards * PLACES)
    back = exchange(back, ("z", "core")).reshape(count, shards, PLACES)
    held = (back >= 0) & ((back & 1) == 1)
    back_src = jnp.where(held, lax.shift_right_logical(back, 8), -1)
    back_own = jnp.where(held, lax.shift_right_logical(back, 1) & (BLOCK - 1), -1)
    source = jnp.stack([ahead_src.reshape(shards, count, PLACES).transpose(1, 0, 2), back_src], axis=2)
    at = jnp.stack([ahead_own, back_own.transpose(1, 0, 2).reshape(shards, groups, LANES)], axis=1)
    at = at.reshape(2 * shards, groups, LANES).transpose(1, 0, 2).reshape(groups * 2 * shards, LANES)
    return source.reshape(count, 2 * shards * PLACES), at


def query_entries(queries, candidates, xs, ys, zs):
    flat = candidates.reshape(-1)
    order = jnp.arange(flat.shape[0], dtype=i32)
    earlier = (flat[:, None] == flat[None, :]) & (order[:, None] > order[None, :])
    rank = jnp.sum(earlier.astype(i32), axis=1)
    here = lax.axis_index(SHARD)
    hits = (flat == here)[None, :] & (rank[None, :] == jnp.arange(PLACES, dtype=i32)[:, None])
    hits = jnp.sum(hits.reshape(PLACES, -1, 2).astype(f32), axis=2).astype(bf16)
    chosen = jnp.dot(hits, queries, preferred_element_type=f32)
    chosen = chosen.reshape(PLACES, xs, -1, LANES).transpose(1, 2, 0, 3).reshape(xs, -1, LANES)
    plane = flat // CORES
    core = flat - plane * CORES
    far = (core != lax.axis_index("core")).astype(i32)
    y = plane // zs
    rows = ((far * zs + plane - y * zs) * ys + y) * PLACES + rank
    return chosen, rows


def per_device(descriptors, neighbours, owned, queries, candidates):
    ys, halves, xs = lax.axis_size("y"), lax.axis_size("z"), lax.axis_size("x")
    zs = 2 * halves
    rows, width = descriptors.shape
    everything = lax.all_gather(descriptors, ("z", "core"), axis=0, tiled=True)
    near = spread(descriptors, "y", ys)
    far = lax.ppermute(near, "half", [(0, 1), (1, 0)])
    first = lax.axis_index("half") == 0
    own = jnp.stack([jnp.where(first, near, far), jnp.where(first, far, near)], axis=1)
    own = own.reshape(2 * ys * rows, width)
    high, low = build_table(neighbours, owned, ys * zs * CORES, halves)
    source, at = slot_orders(high, low, ys, halves)
    chosen, score_rows = query_entries(queries, candidates, xs, ys, zs)
    source, at, own, chosen, score_rows = lax.optimization_barrier((source, at, own, chosen, score_rows))
    got, sims = similar_parts(everything, own, source, at)
    sims = jnp.concatenate([jnp.broadcast_to(sims[None], (xs,) + sims.shape), chosen], axis=1)
    sims = exchange(sims, "x")
    parts = exchange(weighted_sums(got, sims, at), ("y", "half"))
    summed, parts = score_parts(parts, descriptors, sims, ys * xs)
    mine, scales = finish_scores(exchange(parts, ("y", "x")), ys, xs * width)
    scale = lax.dynamic_index_in_dim(scales, lax.axis_index("y"), 0, keepdims=False)[0]
    augmented = (summed * scale[:, None]).astype(bf16)
    near = spread(mine, ("z", "half"), zs)
    far = lax.ppermute(near, "core", [(0, 1), (1, 0)])
    return augmented, pick_scores(score_rows, near, far)


def solution(mesh):
    shards, lanes = mesh.devices.shape
    ys = GROUP // CORES
    devices = mesh.devices.reshape(ys, shards // GROUP // 2, 2, CORES, lanes)
    return jax.shard_map(
        per_device,
        mesh=Mesh(devices, SHARD + ("x",)),
        in_specs=(P(SHARD, "x"), P(SHARD, None), P(SHARD, None), P("x", None), P("x", None)),
        out_specs=(P(SHARD, "x"), P("x", None)),
        check_vma=False,
    )
```

```python
import functools
import math

import jax
import jax.numpy as jnp
from jax import lax
from jax.experimental import pallas as pl
from jax.experimental.pallas import tpu as pltpu
from jax.sharding import Mesh
from jax.sharding import PartitionSpec as P

D = 2048
BLOCK = 128
PLACES = 16
GROUP = 8
CORES = 2
LANES = 128
SHARD = ("y", "z", "half", "core")
VMEM = 48 * 1024 * 1024
INTERPRET = False
SPLIT = 1
LEAVE = 2
JOIN = 4
HBM = pltpu.HBM
f32 = jnp.float32
bf16 = jnp.bfloat16
i16 = jnp.int16
i32 = jnp.int32
LEVELS = 32512.0
STEPS_PER_OCTAVE = 64.0
NT = (((1,), (1,)), ((), ()))
TN = (((0,), (0,)), ((), ()))


def exchange(parts, axis):
    return lax.all_to_all(parts, axis, split_axis=0, concat_axis=0, tiled=True)


def spread(part, axis, count):
    return exchange(jnp.broadcast_to(part[None], (count,) + part.shape), axis)


def hbm(shape, dtype):
    return jax.ShapeDtypeStruct(shape, dtype) if INTERPRET else pltpu.HBM(shape, dtype)


def pinned(value):
    return value if INTERPRET else pltpu.with_memory_space_constraint(value, HBM)


def params(**more):
    return pltpu.CompilerParams(vmem_limit_bytes=VMEM, **more)


def table_kernel(halves, listed_ref, owned_ref, high_ref, low_ref):
    rows = listed_ref.shape[0]
    row = lax.broadcasted_iota(i32, (rows, LANES), 0)
    lane = lax.broadcasted_iota(i32, (rows, LANES), 1)
    lower = (row > lane).astype(bf16)
    own_mark = (row + 1).astype(f32)
    before = jnp.zeros((1, LANES), f32)
    high = jnp.zeros((LANES, LANES), f32)
    low = jnp.zeros((LANES, LANES), f32)
    for slot in range(listed_ref.shape[1]):
        listed = listed_ref[:, slot : slot + 1]
        shard = lax.shift_right_logical(listed, 7)
        plane = shard // (4 * halves)
        half = lax.shift_right_logical(shard, 2) - plane * halves
        shard = (plane * 2 + (lax.shift_right_logical(shard, 1) & 1)) * (2 * halves) + half * 2 + (shard & 1)
        match = lane == shard
        ones = jnp.where(match, 1.0, 0.0)
        counted = jnp.dot(lower, ones.astype(bf16), preferred_element_type=f32) + before
        before = before + jnp.sum(ones, axis=0, keepdims=True)
        rank = jnp.sum(jnp.where(match, counted, 0.0), axis=1, keepdims=True).astype(i32)
        left = jnp.where(lane == lax.shift_right_logical(shard, 3), 1.0, 0.0).astype(bf16)
        here = lane == (shard & (GROUP - 1)) * PLACES + rank
        source = ((listed & (BLOCK - 1)) * 2 + owned_ref[:, slot : slot + 1]).astype(f32)
        high += lax.dot_general(left, jnp.where(here, own_mark, 0.0).astype(bf16), TN, preferred_element_type=f32)
        low += lax.dot_general(left, jnp.where(here, source, 0.0).astype(bf16), TN, preferred_element_type=f32)
    high_ref[...] = high[: high_ref.shape[0]]
    low_ref[...] = low[: low_ref.shape[0]]


def build_table(neighbours, owned, shards, halves):
    return pl.pallas_call(
        functools.partial(table_kernel, halves),
        out_shape=[jax.ShapeDtypeStruct((shards // GROUP, LANES), f32)] * 2,
        compiler_params=params(),
        interpret=INTERPRET,
        name="slot_table",
    )(neighbours, owned)


def similar_kernel(all_ref, own_ref, src_ref, at_ref, got_ref, sims_ref, held_ref, out_ref, in_sems, out_sems):
    shards = own_ref.shape[0] // BLOCK
    kinds = 2 * shards
    slots = kinds * PLACES
    groups = src_ref.shape[0] // GROUP
    arrivals, departures = [], []
    for part in range(groups * SPLIT):
        rows = pl.ds(part * (GROUP // SPLIT) * BLOCK, GROUP // SPLIT * BLOCK)
        arrivals.append(pltpu.make_async_copy(all_ref.at[rows], held_ref.at[rows], in_sems.at[part]))
        arrivals[-1].start()
    row = lax.broadcasted_iota(i32, (BLOCK, slots), 0)
    for group in range(groups):
        parts = []
        for one in range(group * GROUP, (group + 1) * GROUP):
            pick = jnp.where(row == src_ref[one : one + 1, :], 1.0, 0.0).astype(bf16)
            if one % (GROUP // SPLIT) == 0:
                arrivals[one // (GROUP // SPLIT)].wait()
            block = held_ref[one * BLOCK : (one + 1) * BLOCK, :]
            parts.append(lax.dot_general(pick, block, TN, preferred_element_type=f32).astype(bf16))
        sims = []
        for shard in range(shards):
            chunks = []
            for k in (2 * shard, 2 * shard + 1):
                chunk = jnp.concatenate([part[k * PLACES : (k + 1) * PLACES] for part in parts], axis=0)
                out_ref[group, k] = chunk
                chunks.append(chunk)
            own = own_ref[shard * BLOCK : (shard + 1) * BLOCK, :]
            dots = lax.dot_general(own, jnp.concatenate(chunks, axis=0), NT, preferred_element_type=f32)
            for kind in range(2):
                n = group * kinds + 2 * shard + kind
                here = row[:, :LANES] == at_ref[n : n + 1, :]
                held = jnp.where(here, dots[:, kind * LANES : (kind + 1) * LANES], 0.0)
                sims.append(jnp.sum(held, axis=0, keepdims=True))
            if (shard + 1) % LEAVE == 0:
                some = pl.ds(2 * (shard + 1 - LEAVE), 2 * LEAVE)
                sem = out_sems.at[len(departures)]
                departures.append(pltpu.make_async_copy(out_ref.at[group, some], got_ref.at[group, some], sem))
                departures[-1].start()
        sims_ref[group * kinds : (group + 1) * kinds, :] = jnp.concatenate(sims, axis=0)
    for departure in departures:
        departure.wait()


def similar_parts(everything, own, source, at):
    width = own.shape[1]
    groups = everything.shape[0] // BLOCK // GROUP
    kinds = 2 * own.shape[0] // BLOCK
    vmem = pl.BlockSpec(memory_space=pltpu.VMEM)
    outside = pl.BlockSpec(memory_space=HBM)
    shape = (groups, kinds, LANES, width)
    return pl.pallas_call(
        similar_kernel,
        in_specs=[outside, vmem, vmem, vmem],
        out_specs=[outside, vmem],
        out_shape=[hbm(shape, bf16), jax.ShapeDtypeStruct((groups * kinds, LANES), f32)],
        scratch_shapes=[
            pltpu.VMEM(everything.shape, bf16),
            pltpu.VMEM(shape, bf16),
            pltpu.SemaphoreType.DMA((groups * SPLIT,)),
            pltpu.SemaphoreType.DMA((groups * kinds // 2 // LEAVE,)),
        ],
        compiler_params=params(),
        interpret=INTERPRET,
        name="similar_parts",
    )(pinned(everything), own, source, at)


def sum_kernel(got_ref, sims_ref, at_ref, sum_ref, held_ref, sems):
    shards = sum_ref.shape[0]
    copies = []
    for some in range(shards // JOIN):
        kinds = pl.ds(2 * JOIN * some, 2 * JOIN)
        copies.append(pltpu.make_async_copy(got_ref.at[:, kinds], held_ref.at[:, kinds], sems.at[some]))
        copies[-1].start()
    row = lax.broadcasted_iota(i32, (BLOCK, LANES), 0)
    similar = jnp.sum(sims_ref[:, : at_ref.shape[0], :], axis=0) / D
    weight = similar * similar * similar
    high = weight.astype(bf16).astype(f32)
    low = weight - high
    groups = at_ref.shape[0] // (2 * shards)
    for shard in range(shards):
        left_high, left_low = [], []
        for k in (2 * shard, 2 * shard + 1):
            for group in range(groups):
                n = group * 2 * shards + k
                here = row == at_ref[n : n + 1, :]
                left_high.append(jnp.where(here, high[n : n + 1], 0.0).astype(bf16))
                left_low.append(jnp.where(here, low[n : n + 1], 0.0).astype(bf16))
        if shard % JOIN == 0:
            copies[shard // JOIN].wait()
        pair = (2 * shard, 2 * shard + 1)
        right = jnp.concatenate([held_ref[group, k] for k in pair for group in range(groups)], axis=0)
        total = jnp.dot(jnp.concatenate(left_high, axis=1), right, preferred_element_type=f32)
        total += jnp.dot(jnp.concatenate(left_low, axis=1), right, preferred_element_type=f32)
        peak = jnp.maximum(jnp.max(jnp.abs(total), axis=1, keepdims=True), 1e-30)
        level = jnp.floor(jnp.log2(peak) * STEPS_PER_OCTAVE) + 1.0
        scale = LEVELS / jnp.exp2(level / STEPS_PER_OCTAVE)
        total = jnp.floor(total * scale + 0.5).astype(i32).astype(i16)
        quarters = total.shape[1] // LANES
        for quarter in range(quarters):
            at = slice(quarter * BLOCK, (quarter + 1) * BLOCK)
            sum_ref[shard, at, :] = total[:, quarter * LANES : (quarter + 1) * LANES]
        sum_ref[shard, quarters * BLOCK :, :] = jnp.broadcast_to(level, (BLOCK, LANES)).T[:PLACES].astype(i32).astype(i16)


def weighted_sums(got, sims, at):
    kinds, width = got.shape[1], got.shape[3]
    vmem = pl.BlockSpec(memory_space=pltpu.VMEM)
    return pl.pallas_call(
        sum_kernel,
        in_specs=[pl.BlockSpec(memory_space=HBM), vmem, vmem],
        out_specs=vmem,
        out_shape=jax.ShapeDtypeStruct((kinds // 2, width // LANES * BLOCK + PLACES, LANES), i16),
        scratch_shapes=[pltpu.VMEM(got.shape, bf16), pltpu.SemaphoreType.DMA((kinds // 2 // JOIN,))],
        compiler_params=params(),
        interpret=INTERPRET,
        name="weighted_sums",
    )(pinned(got), sims, at)


def score_kernel(parts_ref, own_ref, chosen_ref, sum_ref, out_ref):
    total = own_ref[...].astype(f32)
    quarters = total.shape[1] // LANES
    for part in range(parts_ref.shape[0]):
        level = parts_ref[part, quarters * BLOCK :, :].astype(i32).astype(f32)[:1]
        level = jnp.broadcast_to(level, (BLOCK, LANES)).T[:, :1]
        scale = jnp.exp2(level / STEPS_PER_OCTAVE) / LEVELS
        pieces = [parts_ref[part, quarter * BLOCK : (quarter + 1) * BLOCK, :] for quarter in range(quarters)]
        total += jnp.concatenate(pieces, axis=1).astype(i32).astype(f32) * scale
    sum_ref[...] = total
    energy = jnp.sum(total * total, axis=1, keepdims=True)
    energy = jnp.broadcast_to(energy, (BLOCK, LANES)).T[:8]
    high = total.astype(bf16)
    low = (total - high.astype(f32)).astype(bf16)
    lanes = chosen_ref.shape[0]
    before = chosen_ref.shape[1] - quarters * PLACES
    scores = jnp.zeros((lanes * PLACES, LANES), f32)
    for quarter in range(quarters):
        at = before + quarter * PLACES
        chosen = jnp.concatenate([chosen_ref[lane, at : at + PLACES, :] for lane in range(lanes)], axis=0).astype(bf16)
        columns = slice(quarter * LANES, (quarter + 1) * LANES)
        scores += lax.dot_general(chosen, high[:, columns], NT, preferred_element_type=f32)
        scores += lax.dot_general(chosen, low[:, columns], NT, preferred_element_type=f32)
    for place in range(out_ref.shape[0]):
        lane = place % lanes
        out_ref[place, :PLACES, :] = scores[lane * PLACES : (lane + 1) * PLACES]
        out_ref[place, PLACES:, :] = energy


def score_parts(parts, own, chosen, places):
    return pl.pallas_call(
        score_kernel,
        out_shape=[
            jax.ShapeDtypeStruct(own.shape, f32),
            jax.ShapeDtypeStruct((places, PLACES + 8, LANES), f32),
        ],
        compiler_params=params(),
        interpret=INTERPRET,
        name="score_parts",
    )(parts, own, chosen)


def finish_kernel(depth, parts_ref, out_ref, scale_ref):
    ys = scale_ref.shape[0]
    lanes = parts_ref.shape[0] // ys
    scores = []
    for y in range(ys):
        whole = parts_ref[y * lanes]
        for lane in range(1, lanes):
            whole += parts_ref[y * lanes + lane]
        scale = lax.rsqrt(whole[PLACES:] / depth + 1e-06)
        scale_ref[y] = scale
        scores.append(whole[:PLACES] * (scale[:1] / math.sqrt(depth)))
    scores = jnp.concatenate(scores, axis=0)
    peak = jnp.max(jnp.max(jnp.abs(scores), axis=0, keepdims=True), axis=1, keepdims=True)
    level = jnp.floor(jnp.log2(jnp.maximum(peak, 1e-30)) * STEPS_PER_OCTAVE) + 1.0
    level = jnp.broadcast_to(level, (PLACES, LANES))
    count = scores.shape[0]
    scores = scores * (LEVELS / jnp.exp2(level[:1] / STEPS_PER_OCTAVE))
    scores = jnp.floor(scores + 0.5).astype(i32).astype(i16)
    level = level.astype(i32).astype(i16)
    for place in range(out_ref.shape[0]):
        out_ref[place, :count, :] = scores
        out_ref[place, count:, :] = level


def finish_scores(parts, ys, zs, depth):
    return pl.pallas_call(
        functools.partial(finish_kernel, depth),
        out_shape=[
            jax.ShapeDtypeStruct((zs, (ys + 1) * PLACES, LANES), i16),
            jax.ShapeDtypeStruct((ys, 8, LANES), f32),
        ],
        compiler_params=params(),
        interpret=INTERPRET,
        name="finish_scores",
    )(parts)


def pick_kernel(rows_ref, near_ref, far_ref, out_ref, table_ref):
    planes, held, _ = near_ref.shape
    count = held - PLACES
    for side, ref in enumerate((near_ref, far_ref)):
        for plane in range(planes):
            level = ref[plane, count:, :].astype(i32).astype(f32)[:1]
            scores = ref[plane, :count, :].astype(i32).astype(f32) * (jnp.exp2(level / STEPS_PER_OCTAVE) / LEVELS)
            table_ref[(side * planes + plane) * count : (side * planes + plane + 1) * count, :] = scores

    def step(i, carry):
        for cand in range(2):
            picked = []
            for one in range(GROUP):
                r = rows_ref[i * (2 * GROUP) + 2 * one + cand]
                picked.append(table_ref[pl.ds(r, 1), :])
            at = pl.ds(pl.multiple_of(i * GROUP, GROUP), GROUP)
            out_ref[at, cand * LANES : (cand + 1) * LANES] = jnp.concatenate(picked, axis=0)
        return carry

    lax.fori_loop(0, out_ref.shape[0] // GROUP, step, 0, unroll=8)


def pick_scores(rows, near, far):
    queries = rows.shape[0] // 2
    vmem = pl.BlockSpec(memory_space=pltpu.VMEM)
    planes, held, _ = near.shape
    return pl.pallas_call(
        pick_kernel,
        in_specs=[pl.BlockSpec(memory_space=pltpu.SMEM), vmem, vmem],
        out_specs=vmem,
        out_shape=jax.ShapeDtypeStruct((queries, 2 * LANES), f32),
        scratch_shapes=[pltpu.VMEM((2 * planes * (held - PLACES), LANES), f32)],
        compiler_params=params(),
        interpret=INTERPRET,
        name="pick_scores",
    )(rows, near, far)


def slot_orders(high, low, ys, halves):
    shards = 2 * ys
    count = halves * CORES
    groups = count // GROUP
    codes = jnp.concatenate([high.reshape(shards, -1), low.reshape(shards, -1)], axis=1)
    codes = exchange(codes.astype(i32).reshape(shards, 2 * groups, LANES), ("y", "half"))
    codes = codes.reshape(shards, 2, groups, LANES)
    ahead_own = codes[:, 0] - 1
    ahead_src = jnp.where(ahead_own >= 0, lax.shift_right_logical(codes[:, 1], 1), -1)
    back = jnp.where(high > 0, (high - 1) * 256 + low, -1).astype(i32)
    back = back.reshape(shards, count, PLACES).transpose(1, 0, 2).reshape(count, 1, shards * PLACES)
    back = exchange(back, ("z", "core")).reshape(count, shards, PLACES)
    held = (back >= 0) & ((back & 1) == 1)
    back_src = jnp.where(held, lax.shift_right_logical(back, 8), -1)
    back_own = jnp.where(held, lax.shift_right_logical(back, 1) & (BLOCK - 1), -1)
    source = jnp.stack([ahead_src.reshape(shards, count, PLACES).transpose(1, 0, 2), back_src], axis=2)
    at = jnp.stack([ahead_own, back_own.transpose(1, 0, 2).reshape(shards, groups, LANES)], axis=1)
    at = at.reshape(2 * shards, groups, LANES).transpose(1, 0, 2).reshape(groups * 2 * shards, LANES)
    return source.reshape(count, 2 * shards * PLACES), at


def query_entries(queries, candidates, xs, ys, zs):
    flat = candidates.reshape(-1)
    order = jnp.arange(flat.shape[0], dtype=i32)
    earlier = (flat[:, None] == flat[None, :]) & (order[:, None] > order[None, :])
    rank = jnp.sum(earlier.astype(i32), axis=1)
    here = lax.axis_index(SHARD)
    hits = (flat == here)[None, :] & (rank[None, :] == jnp.arange(PLACES, dtype=i32)[:, None])
    hits = jnp.sum(hits.reshape(PLACES, -1, 2).astype(f32), axis=2).astype(bf16)
    chosen = jnp.dot(hits, queries, preferred_element_type=f32)
    chosen = chosen.reshape(PLACES, xs, -1, LANES).transpose(1, 2, 0, 3).reshape(xs, -1, LANES)
    plane = flat // CORES
    core = flat - plane * CORES
    far = (core != lax.axis_index("core")).astype(i32)
    y = plane // zs
    rows = ((far * zs + plane - y * zs) * ys + y) * PLACES + rank
    return chosen, rows


def per_device(descriptors, neighbours, owned, queries, candidates):
    ys, halves, xs = lax.axis_size("y"), lax.axis_size("z"), lax.axis_size("x")
    zs = 2 * halves
    rows, width = descriptors.shape
    everything = lax.all_gather(descriptors, ("z", "core"), axis=0, tiled=True)
    near = spread(descriptors, "y", ys)
    far = lax.ppermute(near, "half", [(0, 1), (1, 0)])
    first = lax.axis_index("half") == 0
    own = jnp.stack([jnp.where(first, near, far), jnp.where(first, far, near)], axis=1)
    own = own.reshape(2 * ys * rows, width)
    high, low = build_table(neighbours, owned, ys * zs * CORES, halves)
    source, at = slot_orders(high, low, ys, halves)
    chosen, score_rows = query_entries(queries, candidates, xs, ys, zs)
    source, at, own, chosen, score_rows = lax.optimization_barrier((source, at, own, chosen, score_rows))
    got, sims = similar_parts(everything, own, source, at)
    sims = jnp.concatenate([jnp.broadcast_to(sims[None], (xs,) + sims.shape), chosen], axis=1)
    sims = exchange(sims, "x")
    parts = exchange(weighted_sums(got, sims, at), ("y", "half"))
    summed, parts = score_parts(parts, descriptors, sims, ys * xs)
    mine, scales = finish_scores(exchange(parts, ("y", "x")), ys, zs, xs * width)
    scale = lax.dynamic_index_in_dim(scales, lax.axis_index("y"), 0, keepdims=False)[0]
    augmented = (summed * scale[:, None]).astype(bf16)
    near = exchange(mine, ("z", "half"))
    far = lax.ppermute(near, "core", [(0, 1), (1, 0)])
    return augmented, pick_scores(score_rows, near, far)


def solution(mesh):
    shards, lanes = mesh.devices.shape
    ys = GROUP // CORES
    devices = mesh.devices.reshape(ys, shards // GROUP // 2, 2, CORES, lanes)
    return jax.shard_map(
        per_device,
        mesh=Mesh(devices, SHARD + ("x",)),
        in_specs=(P(SHARD, "x"), P(SHARD, None), P(SHARD, None), P("x", None), P("x", None)),
        out_specs=(P(SHARD, "x"), P("x", None)),
        check_vma=False,
    )
```

```python
import functools
import math

import jax
import jax.numpy as jnp
from jax import lax
from jax.experimental import pallas as pl
from jax.experimental.pallas import tpu as pltpu
from jax.sharding import Mesh
from jax.sharding import PartitionSpec as P

D = 2048
BLOCK = 128
PLACES = 16
GROUP = 8
CORES = 2
LANES = 128
SHARD = ("y", "z", "half", "core")
VMEM = 48 * 1024 * 1024
INTERPRET = False
SPLIT = 1
LEAVE = 2
JOIN = 4
HBM = pltpu.HBM
f32 = jnp.float32
bf16 = jnp.bfloat16
i16 = jnp.int16
i32 = jnp.int32
LEVELS = 32512.0
STEPS_PER_OCTAVE = 64.0
STEPS_PER_OCTAVE_OF_SCORES = 512.0
LOWEST = 54.0
NT = (((1,), (1,)), ((), ()))
TN = (((0,), (0,)), ((), ()))


def exchange(parts, axis):
    return lax.all_to_all(parts, axis, split_axis=0, concat_axis=0, tiled=True)


def spread(part, axis, count):
    return exchange(jnp.broadcast_to(part[None], (count,) + part.shape), axis)


def hbm(shape, dtype):
    return jax.ShapeDtypeStruct(shape, dtype) if INTERPRET else pltpu.HBM(shape, dtype)


def pinned(value):
    return value if INTERPRET else pltpu.with_memory_space_constraint(value, HBM)


def params(**more):
    return pltpu.CompilerParams(vmem_limit_bytes=VMEM, **more)


def table_kernel(halves, listed_ref, owned_ref, high_ref, low_ref):
    rows = listed_ref.shape[0]
    row = lax.broadcasted_iota(i32, (rows, LANES), 0)
    lane = lax.broadcasted_iota(i32, (rows, LANES), 1)
    lower = (row > lane).astype(bf16)
    own_mark = (row + 1).astype(f32)
    before = jnp.zeros((1, LANES), f32)
    high = jnp.zeros((LANES, LANES), f32)
    low = jnp.zeros((LANES, LANES), f32)
    for slot in range(listed_ref.shape[1]):
        listed = listed_ref[:, slot : slot + 1]
        shard = lax.shift_right_logical(listed, 7)
        plane = shard // (4 * halves)
        half = lax.shift_right_logical(shard, 2) - plane * halves
        shard = (plane * 2 + (lax.shift_right_logical(shard, 1) & 1)) * (2 * halves) + half * 2 + (shard & 1)
        match = lane == shard
        ones = jnp.where(match, 1.0, 0.0)
        counted = jnp.dot(lower, ones.astype(bf16), preferred_element_type=f32) + before
        before = before + jnp.sum(ones, axis=0, keepdims=True)
        rank = jnp.sum(jnp.where(match, counted, 0.0), axis=1, keepdims=True).astype(i32)
        left = jnp.where(lane == lax.shift_right_logical(shard, 3), 1.0, 0.0).astype(bf16)
        here = lane == (shard & (GROUP - 1)) * PLACES + rank
        source = ((listed & (BLOCK - 1)) * 2 + owned_ref[:, slot : slot + 1]).astype(f32)
        high += lax.dot_general(left, jnp.where(here, own_mark, 0.0).astype(bf16), TN, preferred_element_type=f32)
        low += lax.dot_general(left, jnp.where(here, source, 0.0).astype(bf16), TN, preferred_element_type=f32)
    high_ref[...] = high[: high_ref.shape[0]]
    low_ref[...] = low[: low_ref.shape[0]]


def build_table(neighbours, owned, shards, halves):
    return pl.pallas_call(
        functools.partial(table_kernel, halves),
        out_shape=[jax.ShapeDtypeStruct((shards // GROUP, LANES), f32)] * 2,
        compiler_params=params(),
        interpret=INTERPRET,
        name="slot_table",
    )(neighbours, owned)


def similar_kernel(all_ref, own_ref, src_ref, at_ref, got_ref, sims_ref, held_ref, out_ref, in_sems, out_sems):
    shards = own_ref.shape[0] // BLOCK
    kinds = 2 * shards
    slots = kinds * PLACES
    groups = src_ref.shape[0] // GROUP
    arrivals, departures = [], []
    for part in range(groups * SPLIT):
        rows = pl.ds(part * (GROUP // SPLIT) * BLOCK, GROUP // SPLIT * BLOCK)
        arrivals.append(pltpu.make_async_copy(all_ref.at[rows], held_ref.at[rows], in_sems.at[part]))
        arrivals[-1].start()
    row = lax.broadcasted_iota(i32, (BLOCK, slots), 0)
    for group in range(groups):
        parts = []
        for one in range(group * GROUP, (group + 1) * GROUP):
            pick = jnp.where(row == src_ref[one : one + 1, :], 1.0, 0.0).astype(bf16)
            if one % (GROUP // SPLIT) == 0:
                arrivals[one // (GROUP // SPLIT)].wait()
            block = held_ref[one * BLOCK : (one + 1) * BLOCK, :]
            parts.append(lax.dot_general(pick, block, TN, preferred_element_type=f32).astype(bf16))
        sims = []
        for shard in range(shards):
            chunks = []
            for k in (2 * shard, 2 * shard + 1):
                chunk = jnp.concatenate([part[k * PLACES : (k + 1) * PLACES] for part in parts], axis=0)
                out_ref[group, k] = chunk
                chunks.append(chunk)
            own = own_ref[shard * BLOCK : (shard + 1) * BLOCK, :]
            dots = lax.dot_general(own, jnp.concatenate(chunks, axis=0), NT, preferred_element_type=f32)
            for kind in range(2):
                n = group * kinds + 2 * shard + kind
                here = row[:, :LANES] == at_ref[n : n + 1, :]
                held = jnp.where(here, dots[:, kind * LANES : (kind + 1) * LANES], 0.0)
                sims.append(jnp.sum(held, axis=0, keepdims=True))
            if (shard + 1) % LEAVE == 0:
                some = pl.ds(2 * (shard + 1 - LEAVE), 2 * LEAVE)
                sem = out_sems.at[len(departures)]
                departures.append(pltpu.make_async_copy(out_ref.at[group, some], got_ref.at[group, some], sem))
                departures[-1].start()
        sims_ref[group * kinds : (group + 1) * kinds, :] = jnp.concatenate(sims, axis=0)
    for departure in departures:
        departure.wait()


def similar_parts(everything, own, source, at):
    width = own.shape[1]
    groups = everything.shape[0] // BLOCK // GROUP
    kinds = 2 * own.shape[0] // BLOCK
    vmem = pl.BlockSpec(memory_space=pltpu.VMEM)
    outside = pl.BlockSpec(memory_space=HBM)
    shape = (groups, kinds, LANES, width)
    return pl.pallas_call(
        similar_kernel,
        in_specs=[outside, vmem, vmem, vmem],
        out_specs=[outside, vmem],
        out_shape=[hbm(shape, bf16), jax.ShapeDtypeStruct((groups * kinds, LANES), f32)],
        scratch_shapes=[
            pltpu.VMEM(everything.shape, bf16),
            pltpu.VMEM(shape, bf16),
            pltpu.SemaphoreType.DMA((groups * SPLIT,)),
            pltpu.SemaphoreType.DMA((groups * kinds // 2 // LEAVE,)),
        ],
        compiler_params=params(),
        interpret=INTERPRET,
        name="similar_parts",
    )(pinned(everything), own, source, at)


def sum_kernel(got_ref, sims_ref, at_ref, sum_ref, held_ref, sems):
    shards = sum_ref.shape[0]
    copies = []
    for some in range(shards // JOIN):
        kinds = pl.ds(2 * JOIN * some, 2 * JOIN)
        copies.append(pltpu.make_async_copy(got_ref.at[:, kinds], held_ref.at[:, kinds], sems.at[some]))
        copies[-1].start()
    row = lax.broadcasted_iota(i32, (BLOCK, LANES), 0)
    similar = jnp.sum(sims_ref[:, : at_ref.shape[0], :], axis=0) / D
    weight = similar * similar * similar
    high = weight.astype(bf16).astype(f32)
    low = weight - high
    groups = at_ref.shape[0] // (2 * shards)
    for shard in range(shards):
        left_high, left_low = [], []
        for k in (2 * shard, 2 * shard + 1):
            for group in range(groups):
                n = group * 2 * shards + k
                here = row == at_ref[n : n + 1, :]
                left_high.append(jnp.where(here, high[n : n + 1], 0.0).astype(bf16))
                left_low.append(jnp.where(here, low[n : n + 1], 0.0).astype(bf16))
        if shard % JOIN == 0:
            copies[shard // JOIN].wait()
        pair = (2 * shard, 2 * shard + 1)
        right = jnp.concatenate([held_ref[group, k] for k in pair for group in range(groups)], axis=0)
        total = jnp.dot(jnp.concatenate(left_high, axis=1), right, preferred_element_type=f32)
        total += jnp.dot(jnp.concatenate(left_low, axis=1), right, preferred_element_type=f32)
        peak = jnp.maximum(jnp.max(jnp.abs(total), axis=1, keepdims=True), 1e-30)
        level = jnp.floor(jnp.log2(peak) * STEPS_PER_OCTAVE) + 1.0
        scale = LEVELS / jnp.exp2(level / STEPS_PER_OCTAVE)
        total = jnp.floor(total * scale + 0.5).astype(i32).astype(i16)
        quarters = total.shape[1] // LANES
        for quarter in range(quarters):
            at = slice(quarter * BLOCK, (quarter + 1) * BLOCK)
            sum_ref[shard, at, :] = total[:, quarter * LANES : (quarter + 1) * LANES]
        sum_ref[shard, quarters * BLOCK :, :] = jnp.broadcast_to(level, (BLOCK, LANES)).T[:PLACES].astype(i32).astype(i16)


def weighted_sums(got, sims, at):
    kinds, width = got.shape[1], got.shape[3]
    vmem = pl.BlockSpec(memory_space=pltpu.VMEM)
    return pl.pallas_call(
        sum_kernel,
        in_specs=[pl.BlockSpec(memory_space=HBM), vmem, vmem],
        out_specs=vmem,
        out_shape=jax.ShapeDtypeStruct((kinds // 2, width // LANES * BLOCK + PLACES, LANES), i16),
        scratch_shapes=[pltpu.VMEM(got.shape, bf16), pltpu.SemaphoreType.DMA((kinds // 2 // JOIN,))],
        compiler_params=params(),
        interpret=INTERPRET,
        name="weighted_sums",
    )(pinned(got), sims, at)


def score_kernel(parts_ref, own_ref, chosen_ref, sum_ref, out_ref):
    total = own_ref[...].astype(f32)
    quarters = total.shape[1] // LANES
    for part in range(parts_ref.shape[0]):
        level = parts_ref[part, quarters * BLOCK :, :].astype(i32).astype(f32)[:1]
        level = jnp.broadcast_to(level, (BLOCK, LANES)).T[:, :1]
        scale = jnp.exp2(level / STEPS_PER_OCTAVE) / LEVELS
        pieces = [parts_ref[part, quarter * BLOCK : (quarter + 1) * BLOCK, :] for quarter in range(quarters)]
        total += jnp.concatenate(pieces, axis=1).astype(i32).astype(f32) * scale
    sum_ref[...] = total
    energy = jnp.sum(total * total, axis=1, keepdims=True)
    energy = jnp.broadcast_to(energy, (BLOCK, LANES)).T[:8]
    high = total.astype(bf16)
    low = (total - high.astype(f32)).astype(bf16)
    lanes = chosen_ref.shape[0]
    before = chosen_ref.shape[1] - quarters * PLACES
    scores = jnp.zeros((lanes * PLACES, LANES), f32)
    for quarter in range(quarters):
        at = before + quarter * PLACES
        chosen = jnp.concatenate([chosen_ref[lane, at : at + PLACES, :] for lane in range(lanes)], axis=0).astype(bf16)
        columns = slice(quarter * LANES, (quarter + 1) * LANES)
        scores += lax.dot_general(chosen, high[:, columns], NT, preferred_element_type=f32)
        scores += lax.dot_general(chosen, low[:, columns], NT, preferred_element_type=f32)
    for place in range(out_ref.shape[0]):
        lane = place % lanes
        out_ref[place, :PLACES, :] = scores[lane * PLACES : (lane + 1) * PLACES]
        out_ref[place, PLACES:, :] = energy


def score_parts(parts, own, chosen, places):
    return pl.pallas_call(
        score_kernel,
        out_shape=[
            jax.ShapeDtypeStruct(own.shape, f32),
            jax.ShapeDtypeStruct((places, PLACES + 8, LANES), f32),
        ],
        compiler_params=params(),
        interpret=INTERPRET,
        name="score_parts",
    )(parts, own, chosen)


def finish_kernel(depth, parts_ref, out_ref, scale_ref):
    ys = scale_ref.shape[0]
    lanes = parts_ref.shape[0] // ys
    scores = []
    for y in range(ys):
        whole = parts_ref[y * lanes]
        for lane in range(1, lanes):
            whole += parts_ref[y * lanes + lane]
        scale = lax.rsqrt(whole[PLACES:] / depth + 1e-06)
        scale_ref[y] = scale
        scores.append(whole[:PLACES] * (scale[:1] / math.sqrt(depth)))
    scores = jnp.concatenate(scores, axis=0)
    size = jnp.abs(scores)
    code = jnp.floor((jnp.log2(jnp.maximum(size, 2.0**-LOWEST)) + LOWEST) * STEPS_PER_OCTAVE_OF_SCORES + 1.5)
    code = jnp.where(size < 2.0**-LOWEST, 0.0, jnp.minimum(code, 32767.0))
    code = jnp.where(scores < 0.0, -code, code).astype(i32).astype(i16)
    for place in range(out_ref.shape[0]):
        out_ref[place] = code


def finish_scores(parts, ys, zs, depth):
    return pl.pallas_call(
        functools.partial(finish_kernel, depth),
        out_shape=[
            jax.ShapeDtypeStruct((zs, ys * PLACES, LANES), i16),
            jax.ShapeDtypeStruct((ys, 8, LANES), f32),
        ],
        compiler_params=params(),
        interpret=INTERPRET,
        name="finish_scores",
    )(parts)


def pick_kernel(rows_ref, near_ref, far_ref, out_ref, table_ref):
    planes, count, _ = near_ref.shape
    for side, ref in enumerate((near_ref, far_ref)):
        for plane in range(planes):
            code = ref[plane].astype(i32).astype(f32)
            size = jnp.exp2((jnp.abs(code) - 1.0) / STEPS_PER_OCTAVE_OF_SCORES - LOWEST)
            at = (side * planes + plane) * count
            scores = jnp.where(code < 0.0, -size, size)
            table_ref[at : at + count, :] = jnp.where(code == 0.0, 0.0, scores)

    def step(i, carry):
        for cand in range(2):
            picked = []
            for one in range(GROUP):
                r = rows_ref[i * (2 * GROUP) + 2 * one + cand]
                picked.append(table_ref[pl.ds(r, 1), :])
            at = pl.ds(pl.multiple_of(i * GROUP, GROUP), GROUP)
            out_ref[at, cand * LANES : (cand + 1) * LANES] = jnp.concatenate(picked, axis=0)
        return carry

    lax.fori_loop(0, out_ref.shape[0] // GROUP, step, 0, unroll=8)


def pick_scores(rows, near, far):
    queries = rows.shape[0] // 2
    vmem = pl.BlockSpec(memory_space=pltpu.VMEM)
    planes, count, _ = near.shape
    return pl.pallas_call(
        pick_kernel,
        in_specs=[pl.BlockSpec(memory_space=pltpu.SMEM), vmem, vmem],
        out_specs=vmem,
        out_shape=jax.ShapeDtypeStruct((queries, 2 * LANES), f32),
        scratch_shapes=[pltpu.VMEM((2 * planes * count, LANES), f32)],
        compiler_params=params(),
        interpret=INTERPRET,
        name="pick_scores",
    )(rows, near, far)


def slot_orders(high, low, ys, halves):
    shards = 2 * ys
    count = halves * CORES
    groups = count // GROUP
    codes = jnp.concatenate([high.reshape(shards, -1), low.reshape(shards, -1)], axis=1)
    codes = exchange(codes.astype(i32).reshape(shards, 2 * groups, LANES), ("y", "half"))
    codes = codes.reshape(shards, 2, groups, LANES)
    ahead_own = codes[:, 0] - 1
    ahead_src = jnp.where(ahead_own >= 0, lax.shift_right_logical(codes[:, 1], 1), -1)
    back = jnp.where(high > 0, (high - 1) * 256 + low, -1).astype(i32)
    back = back.reshape(shards, count, PLACES).transpose(1, 0, 2).reshape(count, 1, shards * PLACES)
    back = exchange(back, ("z", "core")).reshape(count, shards, PLACES)
    held = (back >= 0) & ((back & 1) == 1)
    back_src = jnp.where(held, lax.shift_right_logical(back, 8), -1)
    back_own = jnp.where(held, lax.shift_right_logical(back, 1) & (BLOCK - 1), -1)
    source = jnp.stack([ahead_src.reshape(shards, count, PLACES).transpose(1, 0, 2), back_src], axis=2)
    at = jnp.stack([ahead_own, back_own.transpose(1, 0, 2).reshape(shards, groups, LANES)], axis=1)
    at = at.reshape(2 * shards, groups, LANES).transpose(1, 0, 2).reshape(groups * 2 * shards, LANES)
    return source.reshape(count, 2 * shards * PLACES), at


def query_entries(queries, candidates, xs, ys, zs):
    flat = candidates.reshape(-1)
    order = jnp.arange(flat.shape[0], dtype=i32)
    earlier = (flat[:, None] == flat[None, :]) & (order[:, None] > order[None, :])
    rank = jnp.sum(earlier.astype(i32), axis=1)
    here = lax.axis_index(SHARD)
    hits = (flat == here)[None, :] & (rank[None, :] == jnp.arange(PLACES, dtype=i32)[:, None])
    hits = jnp.sum(hits.reshape(PLACES, -1, 2).astype(f32), axis=2).astype(bf16)
    chosen = jnp.dot(hits, queries, preferred_element_type=f32)
    chosen = chosen.reshape(PLACES, xs, -1, LANES).transpose(1, 2, 0, 3).reshape(xs, -1, LANES)
    plane = flat // CORES
    core = flat - plane * CORES
    far = (core != lax.axis_index("core")).astype(i32)
    y = plane // zs
    rows = ((far * zs + plane - y * zs) * ys + y) * PLACES + rank
    return chosen, rows


def per_device(descriptors, neighbours, owned, queries, candidates):
    ys, halves, xs = lax.axis_size("y"), lax.axis_size("z"), lax.axis_size("x")
    zs = 2 * halves
    rows, width = descriptors.shape
    everything = lax.all_gather(descriptors, ("z", "core"), axis=0, tiled=True)
    near = spread(descriptors, "y", ys)
    far = lax.ppermute(near, "half", [(0, 1), (1, 0)])
    first = lax.axis_index("half") == 0
    own = jnp.stack([jnp.where(first, near, far), jnp.where(first, far, near)], axis=1)
    own = own.reshape(2 * ys * rows, width)
    high, low = build_table(neighbours, owned, ys * zs * CORES, halves)
    source, at = slot_orders(high, low, ys, halves)
    chosen, score_rows = query_entries(queries, candidates, xs, ys, zs)
    source, at, own, chosen, score_rows = lax.optimization_barrier((source, at, own, chosen, score_rows))
    got, sims = similar_parts(everything, own, source, at)
    sims = jnp.concatenate([jnp.broadcast_to(sims[None], (xs,) + sims.shape), chosen], axis=1)
    sims = exchange(sims, "x")
    parts = exchange(weighted_sums(got, sims, at), ("y", "half"))
    summed, parts = score_parts(parts, descriptors, sims, ys * xs)
    mine, scales = finish_scores(exchange(parts, ("y", "x")), ys, zs, xs * width)
    scale = lax.dynamic_index_in_dim(scales, lax.axis_index("y"), 0, keepdims=False)[0]
    augmented = (summed * scale[:, None]).astype(bf16)
    near = exchange(mine, ("z", "half"))
    far = lax.ppermute(near, "core", [(0, 1), (1, 0)])
    return augmented, pick_scores(score_rows, near, far)


def solution(mesh):
    shards, lanes = mesh.devices.shape
    ys = GROUP // CORES
    devices = mesh.devices.reshape(ys, shards // GROUP // 2, 2, CORES, lanes)
    return jax.shard_map(
        per_device,
        mesh=Mesh(devices, SHARD + ("x",)),
        in_specs=(P(SHARD, "x"), P(SHARD, None), P(SHARD, None), P("x", None), P("x", None)),
        out_specs=(P(SHARD, "x"), P("x", None)),
        check_vma=False,
    )
```

```python
import functools
import math

import jax
import jax.numpy as jnp
from jax import lax
from jax.experimental import pallas as pl
from jax.experimental.pallas import tpu as pltpu
from jax.sharding import Mesh
from jax.sharding import PartitionSpec as P

D = 2048
BLOCK = 128
PLACES = 16
GROUP = 8
CORES = 2
LANES = 128
SHARD = ("y", "z", "half", "core")
VMEM = 48 * 1024 * 1024
INTERPRET = False
SPLIT = 1
LEAVE = 2
JOIN = 4
HBM = pltpu.HBM
f32 = jnp.float32
bf16 = jnp.bfloat16
i16 = jnp.int16
i32 = jnp.int32
LEVELS = 32512.0
STEPS_PER_OCTAVE = 64.0
STEPS_PER_OCTAVE_OF_SCORES = 512.0
LOWEST = 54.0
NT = (((1,), (1,)), ((), ()))
TN = (((0,), (0,)), ((), ()))


def exchange(parts, axis):
    return lax.all_to_all(parts, axis, split_axis=0, concat_axis=0, tiled=True)


def spread(part, axis, count):
    return exchange(jnp.broadcast_to(part[None], (count,) + part.shape), axis)


def hbm(shape, dtype):
    return jax.ShapeDtypeStruct(shape, dtype) if INTERPRET else pltpu.HBM(shape, dtype)


def pinned(value):
    return value if INTERPRET else pltpu.with_memory_space_constraint(value, HBM)


def params(**more):
    return pltpu.CompilerParams(vmem_limit_bytes=VMEM, **more)


def table_kernel(halves, listed_ref, owned_ref, high_ref, low_ref):
    rows = listed_ref.shape[0]
    row = lax.broadcasted_iota(i32, (rows, LANES), 0)
    lane = lax.broadcasted_iota(i32, (rows, LANES), 1)
    lower = (row > lane).astype(bf16)
    own_mark = (row + 1).astype(f32)
    before = jnp.zeros((1, LANES), f32)
    high = jnp.zeros((LANES, LANES), f32)
    low = jnp.zeros((LANES, LANES), f32)
    for slot in range(listed_ref.shape[1]):
        listed = listed_ref[:, slot : slot + 1]
        shard = lax.shift_right_logical(listed, 7)
        plane = shard // (4 * halves)
        half = lax.shift_right_logical(shard, 2) - plane * halves
        shard = (plane * 2 + (lax.shift_right_logical(shard, 1) & 1)) * (2 * halves) + half * 2 + (shard & 1)
        match = lane == shard
        ones = jnp.where(match, 1.0, 0.0)
        counted = jnp.dot(lower, ones.astype(bf16), preferred_element_type=f32) + before
        before = before + jnp.sum(ones, axis=0, keepdims=True)
        rank = jnp.sum(jnp.where(match, counted, 0.0), axis=1, keepdims=True).astype(i32)
        left = jnp.where(lane == lax.shift_right_logical(shard, 3), 1.0, 0.0).astype(bf16)
        here = lane == (shard & (GROUP - 1)) * PLACES + rank
        source = ((listed & (BLOCK - 1)) * 2 + owned_ref[:, slot : slot + 1]).astype(f32)
        high += lax.dot_general(left, jnp.where(here, own_mark, 0.0).astype(bf16), TN, preferred_element_type=f32)
        low += lax.dot_general(left, jnp.where(here, source, 0.0).astype(bf16), TN, preferred_element_type=f32)
    high_ref[...] = high[: high_ref.shape[0]]
    low_ref[...] = low[: low_ref.shape[0]]


def build_table(neighbours, owned, shards, halves):
    return pl.pallas_call(
        functools.partial(table_kernel, halves),
        out_shape=[jax.ShapeDtypeStruct((shards // GROUP, LANES), f32)] * 2,
        compiler_params=params(),
        interpret=INTERPRET,
        name="slot_table",
    )(neighbours, owned)


def similar_kernel(all_ref, own_ref, src_ref, at_ref, got_ref, sims_ref, held_ref, out_ref, in_sems, out_sems):
    shards = own_ref.shape[0] // BLOCK
    kinds = 2 * shards
    slots = kinds * PLACES
    groups = src_ref.shape[0] // GROUP
    arrivals, departures = [], []
    for part in range(groups * SPLIT):
        rows = pl.ds(part * (GROUP // SPLIT) * BLOCK, GROUP // SPLIT * BLOCK)
        arrivals.append(pltpu.make_async_copy(all_ref.at[rows], held_ref.at[rows], in_sems.at[part]))
        arrivals[-1].start()
    row = lax.broadcasted_iota(i32, (BLOCK, slots), 0)
    for group in range(groups):
        parts = []
        for one in range(group * GROUP, (group + 1) * GROUP):
            pick = jnp.where(row == src_ref[one : one + 1, :], 1.0, 0.0).astype(bf16)
            if one % (GROUP // SPLIT) == 0:
                arrivals[one // (GROUP // SPLIT)].wait()
            block = held_ref[one * BLOCK : (one + 1) * BLOCK, :]
            parts.append(lax.dot_general(pick, block, TN, preferred_element_type=f32).astype(bf16))
        sims = []
        for shard in range(shards):
            chunks = []
            for k in (2 * shard, 2 * shard + 1):
                chunk = jnp.concatenate([part[k * PLACES : (k + 1) * PLACES] for part in parts], axis=0)
                out_ref[group, k] = chunk
                chunks.append(chunk)
            own = own_ref[shard * BLOCK : (shard + 1) * BLOCK, :]
            dots = lax.dot_general(own, jnp.concatenate(chunks, axis=0), NT, preferred_element_type=f32)
            for kind in range(2):
                n = group * kinds + 2 * shard + kind
                here = row[:, :LANES] == at_ref[n : n + 1, :]
                held = jnp.where(here, dots[:, kind * LANES : (kind + 1) * LANES], 0.0)
                sims.append(jnp.sum(held, axis=0, keepdims=True))
            if (shard + 1) % LEAVE == 0:
                some = pl.ds(2 * (shard + 1 - LEAVE), 2 * LEAVE)
                sem = out_sems.at[len(departures)]
                departures.append(pltpu.make_async_copy(out_ref.at[group, some], got_ref.at[group, some], sem))
                departures[-1].start()
        sims_ref[group * kinds : (group + 1) * kinds, :] = jnp.concatenate(sims, axis=0)
    for departure in departures:
        departure.wait()


def similar_parts(everything, own, source, at):
    width = own.shape[1]
    groups = everything.shape[0] // BLOCK // GROUP
    kinds = 2 * own.shape[0] // BLOCK
    vmem = pl.BlockSpec(memory_space=pltpu.VMEM)
    outside = pl.BlockSpec(memory_space=HBM)
    shape = (groups, kinds, LANES, width)
    return pl.pallas_call(
        similar_kernel,
        in_specs=[outside, vmem, vmem, vmem],
        out_specs=[outside, vmem],
        out_shape=[hbm(shape, bf16), jax.ShapeDtypeStruct((groups * kinds, LANES), f32)],
        scratch_shapes=[
            pltpu.VMEM(everything.shape, bf16),
            pltpu.VMEM(shape, bf16),
            pltpu.SemaphoreType.DMA((groups * SPLIT,)),
            pltpu.SemaphoreType.DMA((groups * kinds // 2 // LEAVE,)),
        ],
        compiler_params=params(),
        interpret=INTERPRET,
        name="similar_parts",
    )(pinned(everything), own, source, at)


def sum_kernel(got_ref, sims_ref, at_ref, sum_ref, held_ref, sems):
    shards = sum_ref.shape[0]
    copies = []
    for some in range(shards // JOIN):
        kinds = pl.ds(2 * JOIN * some, 2 * JOIN)
        copies.append(pltpu.make_async_copy(got_ref.at[:, kinds], held_ref.at[:, kinds], sems.at[some]))
        copies[-1].start()
    row = lax.broadcasted_iota(i32, (BLOCK, LANES), 0)
    similar = jnp.sum(sims_ref[:, : at_ref.shape[0], :], axis=0) / D
    weight = similar * similar * similar
    high = weight.astype(bf16).astype(f32)
    low = weight - high
    groups = at_ref.shape[0] // (2 * shards)
    for shard in range(shards):
        left_high, left_low = [], []
        for k in (2 * shard, 2 * shard + 1):
            for group in range(groups):
                n = group * 2 * shards + k
                here = row == at_ref[n : n + 1, :]
                left_high.append(jnp.where(here, high[n : n + 1], 0.0).astype(bf16))
                left_low.append(jnp.where(here, low[n : n + 1], 0.0).astype(bf16))
        if shard % JOIN == 0:
            copies[shard // JOIN].wait()
        pair = (2 * shard, 2 * shard + 1)
        right = jnp.concatenate([held_ref[group, k] for k in pair for group in range(groups)], axis=0)
        total = jnp.dot(jnp.concatenate(left_high, axis=1), right, preferred_element_type=f32)
        total += jnp.dot(jnp.concatenate(left_low, axis=1), right, preferred_element_type=f32)
        peak = jnp.maximum(jnp.max(jnp.abs(total), axis=1, keepdims=True), 1e-30)
        level = jnp.floor(jnp.log2(peak) * STEPS_PER_OCTAVE) + 1.0
        scale = LEVELS / jnp.exp2(level / STEPS_PER_OCTAVE)
        total = jnp.floor(total * scale + 0.5).astype(i32).astype(i16)
        quarters = total.shape[1] // LANES
        for quarter in range(quarters):
            at = slice(quarter * BLOCK, (quarter + 1) * BLOCK)
            sum_ref[shard, at, :] = total[:, quarter * LANES : (quarter + 1) * LANES]
        sum_ref[shard, quarters * BLOCK :, :] = jnp.broadcast_to(level, (BLOCK, LANES)).T[:PLACES].astype(i32).astype(i16)


def weighted_sums(got, sims, at):
    kinds, width = got.shape[1], got.shape[3]
    vmem = pl.BlockSpec(memory_space=pltpu.VMEM)
    return pl.pallas_call(
        sum_kernel,
        in_specs=[pl.BlockSpec(memory_space=HBM), vmem, vmem],
        out_specs=vmem,
        out_shape=jax.ShapeDtypeStruct((kinds // 2, width // LANES * BLOCK + PLACES, LANES), i16),
        scratch_shapes=[pltpu.VMEM(got.shape, bf16), pltpu.SemaphoreType.DMA((kinds // 2 // JOIN,))],
        compiler_params=params(),
        interpret=INTERPRET,
        name="weighted_sums",
    )(pinned(got), sims, at)


def score_kernel(parts_ref, own_ref, chosen_ref, sum_ref, out_ref):
    total = own_ref[...].astype(f32)
    quarters = total.shape[1] // LANES
    for part in range(parts_ref.shape[0]):
        level = parts_ref[part, quarters * BLOCK :, :].astype(i32).astype(f32)[:1]
        level = jnp.broadcast_to(level, (BLOCK, LANES)).T[:, :1]
        scale = jnp.exp2(level / STEPS_PER_OCTAVE) / LEVELS
        pieces = [parts_ref[part, quarter * BLOCK : (quarter + 1) * BLOCK, :] for quarter in range(quarters)]
        total += jnp.concatenate(pieces, axis=1).astype(i32).astype(f32) * scale
    sum_ref[...] = total
    energy = jnp.sum(total * total, axis=1, keepdims=True)
    energy = jnp.broadcast_to(energy, (BLOCK, LANES)).T[:8]
    high = total.astype(bf16)
    low = (total - high.astype(f32)).astype(bf16)
    lanes = chosen_ref.shape[0]
    before = chosen_ref.shape[1] - quarters * PLACES
    scores = jnp.zeros((lanes * PLACES, LANES), f32)
    for quarter in range(quarters):
        at = before + quarter * PLACES
        chosen = jnp.concatenate([chosen_ref[lane, at : at + PLACES, :] for lane in range(lanes)], axis=0).astype(bf16)
        columns = slice(quarter * LANES, (quarter + 1) * LANES)
        scores += lax.dot_general(chosen, high[:, columns], NT, preferred_element_type=f32)
        scores += lax.dot_general(chosen, low[:, columns], NT, preferred_element_type=f32)
    for place in range(out_ref.shape[0]):
        lane = place % lanes
        out_ref[place, :PLACES, :] = scores[lane * PLACES : (lane + 1) * PLACES]
        out_ref[place, PLACES:, :] = energy


def score_parts(parts, own, chosen, places):
    return pl.pallas_call(
        score_kernel,
        out_shape=[
            jax.ShapeDtypeStruct(own.shape, f32),
            jax.ShapeDtypeStruct((places, PLACES + 8, LANES), f32),
        ],
        compiler_params=params(),
        interpret=INTERPRET,
        name="score_parts",
    )(parts, own, chosen)


def finish_kernel(depth, parts_ref, out_ref, scale_ref):
    ys = scale_ref.shape[0]
    lanes = parts_ref.shape[0] // ys
    scores = []
    for y in range(ys):
        whole = parts_ref[y * lanes]
        for lane in range(1, lanes):
            whole += parts_ref[y * lanes + lane]
        scale = lax.rsqrt(whole[PLACES:] / depth + 1e-06)
        scale_ref[y] = scale
        scores.append(whole[:PLACES] * (scale[:1] / math.sqrt(depth)))
    scores = jnp.concatenate(scores, axis=0)
    size = jnp.abs(scores)
    code = jnp.floor((jnp.log2(jnp.maximum(size, 2.0**-LOWEST)) + LOWEST) * STEPS_PER_OCTAVE_OF_SCORES + 1.5)
    code = jnp.where(size < 2.0**-LOWEST, 0.0, jnp.minimum(code, 32767.0))
    code = jnp.where(scores < 0.0, -code, code).astype(i32).astype(i16)
    for place in range(out_ref.shape[0]):
        out_ref[place] = code


def finish_scores(parts, ys, zs, depth):
    return pl.pallas_call(
        functools.partial(finish_kernel, depth),
        out_shape=[
            jax.ShapeDtypeStruct((zs, ys * PLACES, LANES), i16),
            jax.ShapeDtypeStruct((ys, 8, LANES), f32),
        ],
        compiler_params=params(),
        interpret=INTERPRET,
        name="finish_scores",
    )(parts)


def pick_kernel(rows_ref, near_ref, far_ref, out_ref, table_ref):
    planes, count, _ = near_ref.shape
    for side, ref in enumerate((near_ref, far_ref)):
        for plane in range(planes):
            code = ref[plane].astype(i32).astype(f32)
            size = jnp.exp2((jnp.abs(code) - 1.0) / STEPS_PER_OCTAVE_OF_SCORES - LOWEST)
            at = (side * planes + plane) * count
            scores = jnp.where(code < 0.0, -size, size)
            table_ref[at : at + count, :] = jnp.where(code == 0.0, 0.0, scores)

    def step(i, carry):
        for cand in range(2):
            picked = []
            for one in range(GROUP):
                r = rows_ref[i * (2 * GROUP) + 2 * one + cand]
                picked.append(table_ref[pl.ds(r, 1), :])
            at = pl.ds(pl.multiple_of(i * GROUP, GROUP), GROUP)
            out_ref[at, cand * LANES : (cand + 1) * LANES] = jnp.concatenate(picked, axis=0)
        return carry

    lax.fori_loop(0, out_ref.shape[0] // GROUP, step, 0, unroll=8)


def pick_scores(rows, near, far):
    queries = rows.shape[0] // 2
    vmem = pl.BlockSpec(memory_space=pltpu.VMEM)
    planes, count, _ = near.shape
    return pl.pallas_call(
        pick_kernel,
        in_specs=[pl.BlockSpec(memory_space=pltpu.SMEM), vmem, vmem],
        out_specs=vmem,
        out_shape=jax.ShapeDtypeStruct((queries, 2 * LANES), f32),
        scratch_shapes=[pltpu.VMEM((2 * planes * count, LANES), f32)],
        compiler_params=params(),
        interpret=INTERPRET,
        name="pick_scores",
    )(rows, near, far)


def slot_orders(high, low, ys, halves):
    shards = 2 * ys
    count = halves * CORES
    groups = count // GROUP
    codes = jnp.concatenate([high.reshape(shards, -1), low.reshape(shards, -1)], axis=1)
    codes = exchange(codes.astype(i32).reshape(shards, 2 * groups, LANES), ("y", "half"))
    codes = codes.reshape(shards, 2, groups, LANES)
    ahead_own = codes[:, 0] - 1
    ahead_src = jnp.where(ahead_own >= 0, lax.shift_right_logical(codes[:, 1], 1), -1)
    back = jnp.where(high > 0, (high - 1) * 256 + low, -1).astype(i32)
    back = back.reshape(shards, count, PLACES).transpose(1, 0, 2).reshape(count, 1, shards * PLACES)
    back = exchange(back, ("z", "core")).reshape(count, shards, PLACES)
    held = (back >= 0) & ((back & 1) == 1)
    back_src = jnp.where(held, lax.shift_right_logical(back, 8), -1)
    back_own = jnp.where(held, lax.shift_right_logical(back, 1) & (BLOCK - 1), -1)
    source = jnp.stack([ahead_src.reshape(shards, count, PLACES).transpose(1, 0, 2), back_src], axis=2)
    at = jnp.stack([ahead_own, back_own.transpose(1, 0, 2).reshape(shards, groups, LANES)], axis=1)
    at = at.reshape(2 * shards, groups, LANES).transpose(1, 0, 2).reshape(groups * 2 * shards, LANES)
    return source.reshape(count, 2 * shards * PLACES), at


def query_entries(queries, candidates, xs, ys, zs):
    flat = candidates.reshape(-1)
    order = jnp.arange(flat.shape[0], dtype=i32)
    earlier = (flat[:, None] == flat[None, :]) & (order[:, None] > order[None, :])
    rank = jnp.sum(earlier.astype(i32), axis=1)
    here = lax.axis_index(SHARD)
    hits = (flat == here)[None, :] & (rank[None, :] == jnp.arange(PLACES, dtype=i32)[:, None])
    hits = jnp.sum(hits.reshape(PLACES, -1, 2).astype(f32), axis=2).astype(bf16)
    chosen = jnp.dot(hits, queries, preferred_element_type=f32)
    chosen = chosen.reshape(PLACES, xs, -1, LANES).transpose(1, 2, 0, 3).reshape(xs, -1, LANES)
    plane = flat // CORES
    core = flat - plane * CORES
    far = (core != lax.axis_index("core")).astype(i32)
    y = plane // zs
    rows = ((far * zs + plane - y * zs) * ys + y) * PLACES + rank
    return chosen, rows


def per_device(descriptors, neighbours, owned, queries, candidates):
    ys, halves, xs = lax.axis_size("y"), lax.axis_size("z"), lax.axis_size("x")
    zs = 2 * halves
    rows, width = descriptors.shape
    everything = lax.all_gather(descriptors, ("z", "core"), axis=0, tiled=True)
    other = lax.ppermute(descriptors, "half", [(0, 1), (1, 0)])
    first = lax.axis_index("half") == 0
    pair = jnp.concatenate([jnp.where(first, descriptors, other), jnp.where(first, other, descriptors)], axis=0)
    own = spread(pair, "y", ys).reshape(2 * ys * rows, width)
    high, low = build_table(neighbours, owned, ys * zs * CORES, halves)
    source, at = slot_orders(high, low, ys, halves)
    chosen, score_rows = query_entries(queries, candidates, xs, ys, zs)
    source, at, own, chosen, score_rows = lax.optimization_barrier((source, at, own, chosen, score_rows))
    got, sims = similar_parts(everything, own, source, at)
    sims = jnp.concatenate([jnp.broadcast_to(sims[None], (xs,) + sims.shape), chosen], axis=1)
    sims = exchange(sims, "x")
    parts = exchange(weighted_sums(got, sims, at), ("y", "half"))
    summed, parts = score_parts(parts, descriptors, sims, ys * xs)
    mine, scales = finish_scores(exchange(parts, ("y", "x")), ys, zs, xs * width)
    scale = lax.dynamic_index_in_dim(scales, lax.axis_index("y"), 0, keepdims=False)[0]
    augmented = (summed * scale[:, None]).astype(bf16)
    near = exchange(mine, ("z", "half"))
    far = lax.ppermute(near, "core", [(0, 1), (1, 0)])
    return augmented, pick_scores(score_rows, near, far)


def solution(mesh):
    shards, lanes = mesh.devices.shape
    ys = GROUP // CORES
    devices = mesh.devices.reshape(ys, shards // GROUP // 2, 2, CORES, lanes)
    return jax.shard_map(
        per_device,
        mesh=Mesh(devices, SHARD + ("x",)),
        in_specs=(P(SHARD, "x"), P(SHARD, None), P(SHARD, None), P("x", None), P("x", None)),
        out_specs=(P(SHARD, "x"), P("x", None)),
        check_vma=False,
    )
```

```python
import functools
import math

import jax
import jax.numpy as jnp
from jax import lax
from jax.experimental import pallas as pl
from jax.experimental.pallas import tpu as pltpu
from jax.sharding import Mesh
from jax.sharding import PartitionSpec as P

D = 2048
BLOCK = 128
PLACES = 16
GROUP = 8
CORES = 2
LANES = 128
SHARD = ("y", "z", "half", "core")
VMEM = 48 * 1024 * 1024
INTERPRET = False
SPLIT = 1
LEAVE = 2
JOIN = 4
HBM = pltpu.HBM
f32 = jnp.float32
bf16 = jnp.bfloat16
i16 = jnp.int16
i32 = jnp.int32
LEVELS = 32512.0
STEPS_PER_OCTAVE = 64.0
STEPS_PER_OCTAVE_OF_SCORES = 512.0
LOWEST = 54.0
NT = (((1,), (1,)), ((), ()))
TN = (((0,), (0,)), ((), ()))


def exchange(parts, axis):
    return lax.all_to_all(parts, axis, split_axis=0, concat_axis=0, tiled=True)


def spread(part, axis, count):
    return exchange(jnp.broadcast_to(part[None], (count,) + part.shape), axis)


def hbm(shape, dtype):
    return jax.ShapeDtypeStruct(shape, dtype) if INTERPRET else pltpu.HBM(shape, dtype)


def pinned(value):
    return value if INTERPRET else pltpu.with_memory_space_constraint(value, HBM)


def params(**more):
    return pltpu.CompilerParams(vmem_limit_bytes=VMEM, **more)


def table_kernel(halves, listed_ref, owned_ref, high_ref, low_ref):
    rows = listed_ref.shape[0]
    row = lax.broadcasted_iota(i32, (rows, LANES), 0)
    lane = lax.broadcasted_iota(i32, (rows, LANES), 1)
    lower = (row > lane).astype(bf16)
    own_mark = (row + 1).astype(f32)
    before = jnp.zeros((1, LANES), f32)
    high = jnp.zeros((LANES, LANES), f32)
    low = jnp.zeros((LANES, LANES), f32)
    for slot in range(listed_ref.shape[1]):
        listed = listed_ref[:, slot : slot + 1]
        shard = lax.shift_right_logical(listed, 7)
        plane = shard // (4 * halves)
        half = lax.shift_right_logical(shard, 2) - plane * halves
        shard = (plane * 2 + (lax.shift_right_logical(shard, 1) & 1)) * (2 * halves) + half * 2 + (shard & 1)
        match = lane == shard
        ones = jnp.where(match, 1.0, 0.0)
        counted = jnp.dot(lower, ones.astype(bf16), preferred_element_type=f32) + before
        before = before + jnp.sum(ones, axis=0, keepdims=True)
        rank = jnp.sum(jnp.where(match, counted, 0.0), axis=1, keepdims=True).astype(i32)
        left = jnp.where(lane == lax.shift_right_logical(shard, 3), 1.0, 0.0).astype(bf16)
        here = lane == (shard & (GROUP - 1)) * PLACES + rank
        source = ((listed & (BLOCK - 1)) * 2 + owned_ref[:, slot : slot + 1]).astype(f32)
        high += lax.dot_general(left, jnp.where(here, own_mark, 0.0).astype(bf16), TN, preferred_element_type=f32)
        low += lax.dot_general(left, jnp.where(here, source, 0.0).astype(bf16), TN, preferred_element_type=f32)
    high_ref[...] = high[: high_ref.shape[0]]
    low_ref[...] = low[: low_ref.shape[0]]


def build_table(neighbours, owned, shards, halves):
    return pl.pallas_call(
        functools.partial(table_kernel, halves),
        out_shape=[jax.ShapeDtypeStruct((shards // GROUP, LANES), f32)] * 2,
        compiler_params=params(),
        interpret=INTERPRET,
        name="slot_table",
    )(neighbours, owned)


def similar_kernel(all_ref, own_ref, src_ref, at_ref, got_ref, sims_ref, held_ref, out_ref, in_sems, out_sems):
    shards = 2 * own_ref.shape[0]
    kinds = 2 * shards
    slots = kinds * PLACES
    groups = src_ref.shape[0] // GROUP
    arrivals, departures = [], []
    for part in range(groups * SPLIT):
        rows = pl.ds(part * (GROUP // SPLIT) * BLOCK, GROUP // SPLIT * BLOCK)
        arrivals.append(pltpu.make_async_copy(all_ref.at[rows], held_ref.at[rows], in_sems.at[part]))
        arrivals[-1].start()
    row = lax.broadcasted_iota(i32, (BLOCK, slots), 0)
    for group in range(groups):
        parts = []
        for one in range(group * GROUP, (group + 1) * GROUP):
            pick = jnp.where(row == src_ref[one : one + 1, :], 1.0, 0.0).astype(bf16)
            if one % (GROUP // SPLIT) == 0:
                arrivals[one // (GROUP // SPLIT)].wait()
            block = held_ref[one * BLOCK : (one + 1) * BLOCK, :]
            parts.append(lax.dot_general(pick, block, TN, preferred_element_type=f32).astype(bf16))
        sims = []
        for shard in range(shards):
            chunks = []
            for k in (2 * shard, 2 * shard + 1):
                chunk = jnp.concatenate([part[k * PLACES : (k + 1) * PLACES] for part in parts], axis=0)
                out_ref[group, k] = chunk
                chunks.append(chunk)
            own = own_ref[shard // 2, shard % 2 * BLOCK : (shard % 2 + 1) * BLOCK, :]
            dots = lax.dot_general(own, jnp.concatenate(chunks, axis=0), NT, preferred_element_type=f32)
            for kind in range(2):
                n = group * kinds + 2 * shard + kind
                here = row[:, :LANES] == at_ref[n : n + 1, :]
                held = jnp.where(here, dots[:, kind * LANES : (kind + 1) * LANES], 0.0)
                sims.append(jnp.sum(held, axis=0, keepdims=True))
            if (shard + 1) % LEAVE == 0:
                some = pl.ds(2 * (shard + 1 - LEAVE), 2 * LEAVE)
                sem = out_sems.at[len(departures)]
                departures.append(pltpu.make_async_copy(out_ref.at[group, some], got_ref.at[group, some], sem))
                departures[-1].start()
        sims_ref[group * kinds : (group + 1) * kinds, :] = jnp.concatenate(sims, axis=0)
    for departure in departures:
        departure.wait()


def similar_parts(everything, own, source, at):
    width = own.shape[2]
    groups = everything.shape[0] // BLOCK // GROUP
    kinds = 4 * own.shape[0]
    vmem = pl.BlockSpec(memory_space=pltpu.VMEM)
    outside = pl.BlockSpec(memory_space=HBM)
    shape = (groups, kinds, LANES, width)
    return pl.pallas_call(
        similar_kernel,
        in_specs=[outside, vmem, vmem, vmem],
        out_specs=[outside, vmem],
        out_shape=[hbm(shape, bf16), jax.ShapeDtypeStruct((groups * kinds, LANES), f32)],
        scratch_shapes=[
            pltpu.VMEM(everything.shape, bf16),
            pltpu.VMEM(shape, bf16),
            pltpu.SemaphoreType.DMA((groups * SPLIT,)),
            pltpu.SemaphoreType.DMA((groups * kinds // 2 // LEAVE,)),
        ],
        compiler_params=params(),
        interpret=INTERPRET,
        name="similar_parts",
    )(pinned(everything), own, source, at)


def sum_kernel(got_ref, sims_ref, at_ref, sum_ref, held_ref, sems):
    shards = sum_ref.shape[0]
    copies = []
    for some in range(shards // JOIN):
        kinds = pl.ds(2 * JOIN * some, 2 * JOIN)
        copies.append(pltpu.make_async_copy(got_ref.at[:, kinds], held_ref.at[:, kinds], sems.at[some]))
        copies[-1].start()
    row = lax.broadcasted_iota(i32, (BLOCK, LANES), 0)
    similar = jnp.sum(sims_ref[:, : at_ref.shape[0], :], axis=0) / D
    weight = similar * similar * similar
    high = weight.astype(bf16).astype(f32)
    low = weight - high
    groups = at_ref.shape[0] // (2 * shards)
    for shard in range(shards):
        left_high, left_low = [], []
        for k in (2 * shard, 2 * shard + 1):
            for group in range(groups):
                n = group * 2 * shards + k
                here = row == at_ref[n : n + 1, :]
                left_high.append(jnp.where(here, high[n : n + 1], 0.0).astype(bf16))
                left_low.append(jnp.where(here, low[n : n + 1], 0.0).astype(bf16))
        if shard % JOIN == 0:
            copies[shard // JOIN].wait()
        pair = (2 * shard, 2 * shard + 1)
        right = jnp.concatenate([held_ref[group, k] for k in pair for group in range(groups)], axis=0)
        total = jnp.dot(jnp.concatenate(left_high, axis=1), right, preferred_element_type=f32)
        total += jnp.dot(jnp.concatenate(left_low, axis=1), right, preferred_element_type=f32)
        peak = jnp.maximum(jnp.max(jnp.abs(total), axis=1, keepdims=True), 1e-30)
        level = jnp.floor(jnp.log2(peak) * STEPS_PER_OCTAVE) + 1.0
        scale = LEVELS / jnp.exp2(level / STEPS_PER_OCTAVE)
        total = jnp.floor(total * scale + 0.5).astype(i32).astype(i16)
        quarters = total.shape[1] // LANES
        for quarter in range(quarters):
            at = slice(quarter * BLOCK, (quarter + 1) * BLOCK)
            sum_ref[shard, at, :] = total[:, quarter * LANES : (quarter + 1) * LANES]
        sum_ref[shard, quarters * BLOCK :, :] = jnp.broadcast_to(level, (BLOCK, LANES)).T[:PLACES].astype(i32).astype(i16)


def weighted_sums(got, sims, at):
    kinds, width = got.shape[1], got.shape[3]
    vmem = pl.BlockSpec(memory_space=pltpu.VMEM)
    return pl.pallas_call(
        sum_kernel,
        in_specs=[pl.BlockSpec(memory_space=HBM), vmem, vmem],
        out_specs=vmem,
        out_shape=jax.ShapeDtypeStruct((kinds // 2, width // LANES * BLOCK + PLACES, LANES), i16),
        scratch_shapes=[pltpu.VMEM(got.shape, bf16), pltpu.SemaphoreType.DMA((kinds // 2 // JOIN,))],
        compiler_params=params(),
        interpret=INTERPRET,
        name="weighted_sums",
    )(pinned(got), sims, at)


def score_kernel(parts_ref, own_ref, chosen_ref, sum_ref, out_ref):
    total = own_ref[...].astype(f32)
    quarters = total.shape[1] // LANES
    for part in range(parts_ref.shape[0]):
        level = parts_ref[part, quarters * BLOCK :, :].astype(i32).astype(f32)[:1]
        level = jnp.broadcast_to(level, (BLOCK, LANES)).T[:, :1]
        scale = jnp.exp2(level / STEPS_PER_OCTAVE) / LEVELS
        pieces = [parts_ref[part, quarter * BLOCK : (quarter + 1) * BLOCK, :] for quarter in range(quarters)]
        total += jnp.concatenate(pieces, axis=1).astype(i32).astype(f32) * scale
    sum_ref[...] = total
    energy = jnp.sum(total * total, axis=1, keepdims=True)
    energy = jnp.broadcast_to(energy, (BLOCK, LANES)).T[:8]
    high = total.astype(bf16)
    low = (total - high.astype(f32)).astype(bf16)
    lanes = chosen_ref.shape[0]
    before = chosen_ref.shape[1] - quarters * PLACES
    scores = jnp.zeros((lanes * PLACES, LANES), f32)
    for quarter in range(quarters):
        at = before + quarter * PLACES
        chosen = jnp.concatenate([chosen_ref[lane, at : at + PLACES, :] for lane in range(lanes)], axis=0).astype(bf16)
        columns = slice(quarter * LANES, (quarter + 1) * LANES)
        scores += lax.dot_general(chosen, high[:, columns], NT, preferred_element_type=f32)
        scores += lax.dot_general(chosen, low[:, columns], NT, preferred_element_type=f32)
    for place in range(out_ref.shape[0]):
        lane = place % lanes
        out_ref[place, :PLACES, :] = scores[lane * PLACES : (lane + 1) * PLACES]
        out_ref[place, PLACES:, :] = energy


def score_parts(parts, own, chosen, places):
    return pl.pallas_call(
        score_kernel,
        out_shape=[
            jax.ShapeDtypeStruct(own.shape, f32),
            jax.ShapeDtypeStruct((places, PLACES + 8, LANES), f32),
        ],
        compiler_params=params(),
        interpret=INTERPRET,
        name="score_parts",
    )(parts, own, chosen)


def finish_kernel(depth, parts_ref, out_ref, scale_ref):
    ys = scale_ref.shape[0]
    lanes = parts_ref.shape[0] // ys
    scores = []
    for y in range(ys):
        whole = parts_ref[y * lanes]
        for lane in range(1, lanes):
            whole += parts_ref[y * lanes + lane]
        scale = lax.rsqrt(whole[PLACES:] / depth + 1e-06)
        scale_ref[y] = scale
        scores.append(whole[:PLACES] * (scale[:1] / math.sqrt(depth)))
    scores = jnp.concatenate(scores, axis=0)
    size = jnp.abs(scores)
    code = jnp.floor((jnp.log2(jnp.maximum(size, 2.0**-LOWEST)) + LOWEST) * STEPS_PER_OCTAVE_OF_SCORES + 1.5)
    code = jnp.where(size < 2.0**-LOWEST, 0.0, jnp.minimum(code, 32767.0))
    code = jnp.where(scores < 0.0, -code, code).astype(i32).astype(i16)
    for place in range(out_ref.shape[0]):
        out_ref[place] = code


def finish_scores(parts, ys, zs, depth):
    return pl.pallas_call(
        functools.partial(finish_kernel, depth),
        out_shape=[
            jax.ShapeDtypeStruct((zs, ys * PLACES, LANES), i16),
            jax.ShapeDtypeStruct((ys, 8, LANES), f32),
        ],
        compiler_params=params(),
        interpret=INTERPRET,
        name="finish_scores",
    )(parts)


def pick_kernel(rows_ref, near_ref, far_ref, out_ref, table_ref):
    planes, count, _ = near_ref.shape
    for side, ref in enumerate((near_ref, far_ref)):
        for plane in range(planes):
            code = ref[plane].astype(i32).astype(f32)
            size = jnp.exp2((jnp.abs(code) - 1.0) / STEPS_PER_OCTAVE_OF_SCORES - LOWEST)
            at = (side * planes + plane) * count
            scores = jnp.where(code < 0.0, -size, size)
            table_ref[at : at + count, :] = jnp.where(code == 0.0, 0.0, scores)

    def step(i, carry):
        for cand in range(2):
            picked = []
            for one in range(GROUP):
                r = rows_ref[i * (2 * GROUP) + 2 * one + cand]
                picked.append(table_ref[pl.ds(r, 1), :])
            at = pl.ds(pl.multiple_of(i * GROUP, GROUP), GROUP)
            out_ref[at, cand * LANES : (cand + 1) * LANES] = jnp.concatenate(picked, axis=0)
        return carry

    lax.fori_loop(0, out_ref.shape[0] // GROUP, step, 0, unroll=8)


def pick_scores(rows, near, far):
    queries = rows.shape[0] // 2
    vmem = pl.BlockSpec(memory_space=pltpu.VMEM)
    planes, count, _ = near.shape
    return pl.pallas_call(
        pick_kernel,
        in_specs=[pl.BlockSpec(memory_space=pltpu.SMEM), vmem, vmem],
        out_specs=vmem,
        out_shape=jax.ShapeDtypeStruct((queries, 2 * LANES), f32),
        scratch_shapes=[pltpu.VMEM((2 * planes * count, LANES), f32)],
        compiler_params=params(),
        interpret=INTERPRET,
        name="pick_scores",
    )(rows, near, far)


def own_and_orders(descriptors, high, low, ys, halves):
    rows, width = descriptors.shape
    shards = 2 * ys
    count = halves * CORES
    groups = count // GROUP
    first = lax.axis_index("half") == 0

    def in_order(mine, other, axis):
        return jnp.stack([jnp.where(first, mine, other), jnp.where(first, other, mine)], axis=axis)

    def swap(value):
        return lax.ppermute(value, "half", [(0, 1), (1, 0)])

    pair = in_order(descriptors, swap(descriptors), 0).reshape(2 * rows, width)
    codes = jnp.concatenate([high.reshape(shards, -1), low.reshape(shards, -1)], axis=1).astype(bf16)
    codes = codes.reshape(ys, 2, -1)
    mine = jnp.where(first, codes[:, 0], codes[:, 1])
    other = swap(jnp.where(first, codes[:, 1], codes[:, 0]))
    codes = in_order(mine, other, 1)
    sent = jnp.pad(codes, ((0, 0), (0, PLACES - 2), (0, width - codes.shape[2])))
    sent = jnp.concatenate([jnp.broadcast_to(pair[None], (ys,) + pair.shape), sent], axis=1)
    own = exchange(sent, "y")
    codes = own[:, 2 * rows : 2 * rows + 2, : codes.shape[2]].astype(i32).reshape(shards, 2, groups, LANES)
    ahead_own = codes[:, 0] - 1
    ahead_src = jnp.where(ahead_own >= 0, lax.shift_right_logical(codes[:, 1], 1), -1)
    back = jnp.where(high > 0, (high - 1) * 256 + low, -1).astype(i32)
    back = back.reshape(shards, count, PLACES).transpose(1, 0, 2).reshape(count, 1, shards * PLACES)
    back = exchange(back, ("z", "core")).reshape(count, shards, PLACES)
    held = (back >= 0) & ((back & 1) == 1)
    back_src = jnp.where(held, lax.shift_right_logical(back, 8), -1)
    back_own = jnp.where(held, lax.shift_right_logical(back, 1) & (BLOCK - 1), -1)
    source = jnp.stack([ahead_src.reshape(shards, count, PLACES).transpose(1, 0, 2), back_src], axis=2)
    at = jnp.stack([ahead_own, back_own.transpose(1, 0, 2).reshape(shards, groups, LANES)], axis=1)
    at = at.reshape(2 * shards, groups, LANES).transpose(1, 0, 2).reshape(groups * 2 * shards, LANES)
    return own, source.reshape(count, 2 * shards * PLACES), at


def query_entries(queries, candidates, xs, ys, zs):
    flat = candidates.reshape(-1)
    order = jnp.arange(flat.shape[0], dtype=i32)
    earlier = (flat[:, None] == flat[None, :]) & (order[:, None] > order[None, :])
    rank = jnp.sum(earlier.astype(i32), axis=1)
    here = lax.axis_index(SHARD)
    hits = (flat == here)[None, :] & (rank[None, :] == jnp.arange(PLACES, dtype=i32)[:, None])
    hits = jnp.sum(hits.reshape(PLACES, -1, 2).astype(f32), axis=2).astype(bf16)
    chosen = jnp.dot(hits, queries, preferred_element_type=f32)
    chosen = chosen.reshape(PLACES, xs, -1, LANES).transpose(1, 2, 0, 3).reshape(xs, -1, LANES)
    plane = flat // CORES
    core = flat - plane * CORES
    far = (core != lax.axis_index("core")).astype(i32)
    y = plane // zs
    rows = ((far * zs + plane - y * zs) * ys + y) * PLACES + rank
    return chosen, rows


def per_device(descriptors, neighbours, owned, queries, candidates):
    ys, halves, xs = lax.axis_size("y"), lax.axis_size("z"), lax.axis_size("x")
    zs = 2 * halves
    rows, width = descriptors.shape
    everything = lax.all_gather(descriptors, ("z", "core"), axis=0, tiled=True)
    high, low = build_table(neighbours, owned, ys * zs * CORES, halves)
    own, source, at = own_and_orders(descriptors, high, low, ys, halves)
    chosen, score_rows = query_entries(queries, candidates, xs, ys, zs)
    source, at, own, chosen, score_rows = lax.optimization_barrier((source, at, own, chosen, score_rows))
    got, sims = similar_parts(everything, own, source, at)
    sims = jnp.concatenate([jnp.broadcast_to(sims[None], (xs,) + sims.shape), chosen], axis=1)
    sims = exchange(sims, "x")
    parts = exchange(weighted_sums(got, sims, at), ("y", "half"))
    summed, parts = score_parts(parts, descriptors, sims, ys * xs)
    mine, scales = finish_scores(exchange(parts, ("y", "x")), ys, zs, xs * width)
    scale = lax.dynamic_index_in_dim(scales, lax.axis_index("y"), 0, keepdims=False)[0]
    augmented = (summed * scale[:, None]).astype(bf16)
    near = exchange(mine, ("z", "half"))
    far = lax.ppermute(near, "core", [(0, 1), (1, 0)])
    return augmented, pick_scores(score_rows, near, far)


def solution(mesh):
    shards, lanes = mesh.devices.shape
    ys = GROUP // CORES
    devices = mesh.devices.reshape(ys, shards // GROUP // 2, 2, CORES, lanes)
    return jax.shard_map(
        per_device,
        mesh=Mesh(devices, SHARD + ("x",)),
        in_specs=(P(SHARD, "x"), P(SHARD, None), P(SHARD, None), P("x", None), P("x", None)),
        out_specs=(P(SHARD, "x"), P("x", None)),
        check_vma=False,
    )
```

```python
import functools
import math

import jax
import jax.numpy as jnp
from jax import lax
from jax.experimental import pallas as pl
from jax.experimental.pallas import tpu as pltpu
from jax.sharding import Mesh
from jax.sharding import PartitionSpec as P

D = 2048
BLOCK = 128
PLACES = 16
GROUP = 8
CORES = 2
LANES = 128
SHARD = ("y", "z", "half", "core")
VMEM = 48 * 1024 * 1024
INTERPRET = False
SPLIT = 1
LEAVE = 2
JOIN = 4
HBM = pltpu.HBM
f32 = jnp.float32
bf16 = jnp.bfloat16
i16 = jnp.int16
i32 = jnp.int32
LEVELS = 32512.0
STEPS_PER_OCTAVE = 64.0
STEPS_PER_OCTAVE_OF_SCORES = 512.0
LOWEST = 54.0
NT = (((1,), (1,)), ((), ()))
TN = (((0,), (0,)), ((), ()))


def exchange(parts, axis):
    return lax.all_to_all(parts, axis, split_axis=0, concat_axis=0, tiled=True)


def spread(part, axis, count):
    return exchange(jnp.broadcast_to(part[None], (count,) + part.shape), axis)


def hbm(shape, dtype):
    return jax.ShapeDtypeStruct(shape, dtype) if INTERPRET else pltpu.HBM(shape, dtype)


def pinned(value):
    return value if INTERPRET else pltpu.with_memory_space_constraint(value, HBM)


def params(**more):
    return pltpu.CompilerParams(vmem_limit_bytes=VMEM, **more)


def table_kernel(halves, listed_ref, owned_ref, high_ref, low_ref):
    rows = listed_ref.shape[0]
    row = lax.broadcasted_iota(i32, (rows, LANES), 0)
    lane = lax.broadcasted_iota(i32, (rows, LANES), 1)
    lower = (row > lane).astype(bf16)
    own_mark = (row + 1).astype(f32)
    before = jnp.zeros((1, LANES), f32)
    high = jnp.zeros((LANES, LANES), f32)
    low = jnp.zeros((LANES, LANES), f32)
    for slot in range(listed_ref.shape[1]):
        listed = listed_ref[:, slot : slot + 1]
        shard = lax.shift_right_logical(listed, 7)
        plane = shard // (4 * halves)
        half = lax.shift_right_logical(shard, 2) - plane * halves
        shard = (plane * 2 + (lax.shift_right_logical(shard, 1) & 1)) * (2 * halves) + half * 2 + (shard & 1)
        match = lane == shard
        ones = jnp.where(match, 1.0, 0.0)
        counted = jnp.dot(lower, ones.astype(bf16), preferred_element_type=f32) + before
        before = before + jnp.sum(ones, axis=0, keepdims=True)
        rank = jnp.sum(jnp.where(match, counted, 0.0), axis=1, keepdims=True).astype(i32)
        left = jnp.where(lane == lax.shift_right_logical(shard, 3), 1.0, 0.0).astype(bf16)
        here = lane == (shard & (GROUP - 1)) * PLACES + rank
        source = ((listed & (BLOCK - 1)) * 2 + owned_ref[:, slot : slot + 1]).astype(f32)
        high += lax.dot_general(left, jnp.where(here, own_mark, 0.0).astype(bf16), TN, preferred_element_type=f32)
        low += lax.dot_general(left, jnp.where(here, source, 0.0).astype(bf16), TN, preferred_element_type=f32)
    high_ref[...] = high[: high_ref.shape[0]]
    low_ref[...] = low[: low_ref.shape[0]]


def build_table(neighbours, owned, shards, halves):
    return pl.pallas_call(
        functools.partial(table_kernel, halves),
        out_shape=[jax.ShapeDtypeStruct((shards // GROUP, LANES), f32)] * 2,
        compiler_params=params(),
        interpret=INTERPRET,
        name="slot_table",
    )(neighbours, owned)


def similar_kernel(all_ref, own_ref, src_ref, at_ref, got_ref, sims_ref, held_ref, out_ref, in_sems, out_sems):
    shards = 2 * own_ref.shape[0]
    kinds = 2 * shards
    slots = kinds * PLACES
    groups = src_ref.shape[0] // GROUP
    arrivals, departures = [], []
    for part in range(groups * SPLIT):
        rows = pl.ds(part * (GROUP // SPLIT) * BLOCK, GROUP // SPLIT * BLOCK)
        arrivals.append(pltpu.make_async_copy(all_ref.at[rows], held_ref.at[rows], in_sems.at[part]))
        arrivals[-1].start()
    row = lax.broadcasted_iota(i32, (BLOCK, slots), 0)
    for group in range(groups):
        parts = []
        for one in range(group * GROUP, (group + 1) * GROUP):
            pick = jnp.where(row == src_ref[one : one + 1, :], 1.0, 0.0).astype(bf16)
            if one % (GROUP // SPLIT) == 0:
                arrivals[one // (GROUP // SPLIT)].wait()
            block = held_ref[one * BLOCK : (one + 1) * BLOCK, :]
            parts.append(lax.dot_general(pick, block, TN, preferred_element_type=f32).astype(bf16))
        sims = []
        for shard in range(shards):
            chunks = []
            for k in (2 * shard, 2 * shard + 1):
                chunk = jnp.concatenate([part[k * PLACES : (k + 1) * PLACES] for part in parts], axis=0)
                out_ref[group, k] = chunk
                chunks.append(chunk)
            own = own_ref[shard // 2, shard % 2 * BLOCK : (shard % 2 + 1) * BLOCK, :]
            dots = lax.dot_general(own, jnp.concatenate(chunks, axis=0), NT, preferred_element_type=f32)
            for kind in range(2):
                n = group * kinds + 2 * shard + kind
                here = row[:, :LANES] == at_ref[n : n + 1, :]
                held = jnp.where(here, dots[:, kind * LANES : (kind + 1) * LANES], 0.0)
                sims.append(jnp.sum(held, axis=0, keepdims=True))
            if (shard + 1) % LEAVE == 0:
                some = pl.ds(2 * (shard + 1 - LEAVE), 2 * LEAVE)
                sem = out_sems.at[len(departures)]
                departures.append(pltpu.make_async_copy(out_ref.at[group, some], got_ref.at[group, some], sem))
                departures[-1].start()
        sims_ref[group * kinds : (group + 1) * kinds, :] = jnp.concatenate(sims, axis=0)
    for departure in departures:
        departure.wait()


def similar_parts(everything, own, source, at):
    width = own.shape[2]
    groups = everything.shape[0] // BLOCK // GROUP
    kinds = 4 * own.shape[0]
    vmem = pl.BlockSpec(memory_space=pltpu.VMEM)
    outside = pl.BlockSpec(memory_space=HBM)
    shape = (groups, kinds, LANES, width)
    return pl.pallas_call(
        similar_kernel,
        in_specs=[outside, vmem, vmem, vmem],
        out_specs=[outside, vmem],
        out_shape=[hbm(shape, bf16), jax.ShapeDtypeStruct((groups * kinds, LANES), f32)],
        scratch_shapes=[
            pltpu.VMEM(everything.shape, bf16),
            pltpu.VMEM(shape, bf16),
            pltpu.SemaphoreType.DMA((groups * SPLIT,)),
            pltpu.SemaphoreType.DMA((groups * kinds // 2 // LEAVE,)),
        ],
        compiler_params=params(),
        interpret=INTERPRET,
        name="similar_parts",
    )(pinned(everything), own, source, at)


def sum_kernel(got_ref, sims_ref, at_ref, sum_ref, held_ref, sems):
    shards = sum_ref.shape[0]
    copies = []
    for some in range(shards // JOIN):
        kinds = pl.ds(2 * JOIN * some, 2 * JOIN)
        copies.append(pltpu.make_async_copy(got_ref.at[:, kinds], held_ref.at[:, kinds], sems.at[some]))
        copies[-1].start()
    row = lax.broadcasted_iota(i32, (BLOCK, LANES), 0)
    similar = jnp.sum(sims_ref[:, : at_ref.shape[0], :], axis=0) / D
    weight = similar * similar * similar
    high = weight.astype(bf16).astype(f32)
    low = weight - high
    groups = at_ref.shape[0] // (2 * shards)
    for shard in range(shards):
        left_high, left_low = [], []
        for k in (2 * shard, 2 * shard + 1):
            for group in range(groups):
                n = group * 2 * shards + k
                here = row == at_ref[n : n + 1, :]
                left_high.append(jnp.where(here, high[n : n + 1], 0.0).astype(bf16))
                left_low.append(jnp.where(here, low[n : n + 1], 0.0).astype(bf16))
        if shard % JOIN == 0:
            copies[shard // JOIN].wait()
        pair = (2 * shard, 2 * shard + 1)
        right = jnp.concatenate([held_ref[group, k] for k in pair for group in range(groups)], axis=0)
        total = jnp.dot(jnp.concatenate(left_high, axis=1), right, preferred_element_type=f32)
        total += jnp.dot(jnp.concatenate(left_low, axis=1), right, preferred_element_type=f32)
        peak = jnp.maximum(jnp.max(jnp.abs(total), axis=1, keepdims=True), 1e-30)
        level = jnp.floor(jnp.log2(peak) * STEPS_PER_OCTAVE) + 1.0
        scale = LEVELS / jnp.exp2(level / STEPS_PER_OCTAVE)
        total = jnp.floor(total * scale + 0.5).astype(i32).astype(i16)
        quarters = total.shape[1] // LANES
        for quarter in range(quarters):
            at = slice(quarter * BLOCK, (quarter + 1) * BLOCK)
            sum_ref[shard, at, :] = total[:, quarter * LANES : (quarter + 1) * LANES]
        sum_ref[shard, quarters * BLOCK :, :] = jnp.broadcast_to(level, (BLOCK, LANES)).T[:PLACES].astype(i32).astype(i16)


def weighted_sums(got, sims, at):
    kinds, width = got.shape[1], got.shape[3]
    vmem = pl.BlockSpec(memory_space=pltpu.VMEM)
    return pl.pallas_call(
        sum_kernel,
        in_specs=[pl.BlockSpec(memory_space=HBM), vmem, vmem],
        out_specs=vmem,
        out_shape=jax.ShapeDtypeStruct((kinds // 2, width // LANES * BLOCK + PLACES, LANES), i16),
        scratch_shapes=[pltpu.VMEM(got.shape, bf16), pltpu.SemaphoreType.DMA((kinds // 2 // JOIN,))],
        compiler_params=params(),
        interpret=INTERPRET,
        name="weighted_sums",
    )(pinned(got), sims, at)


def score_kernel(parts_ref, own_ref, chosen_ref, sum_ref, out_ref):
    total = own_ref[...].astype(f32)
    quarters = total.shape[1] // LANES
    for part in range(parts_ref.shape[0]):
        level = parts_ref[part, quarters * BLOCK :, :].astype(i32).astype(f32)[:1]
        level = jnp.broadcast_to(level, (BLOCK, LANES)).T[:, :1]
        scale = jnp.exp2(level / STEPS_PER_OCTAVE) / LEVELS
        pieces = [parts_ref[part, quarter * BLOCK : (quarter + 1) * BLOCK, :] for quarter in range(quarters)]
        total += jnp.concatenate(pieces, axis=1).astype(i32).astype(f32) * scale
    sum_ref[...] = total
    energy = jnp.sum(total * total, axis=1, keepdims=True)
    energy = jnp.broadcast_to(energy, (BLOCK, LANES)).T[:8]
    high = total.astype(bf16)
    low = (total - high.astype(f32)).astype(bf16)
    lanes = chosen_ref.shape[0]
    before = chosen_ref.shape[1] - quarters * PLACES
    scores = jnp.zeros((lanes * PLACES, LANES), f32)
    for quarter in range(quarters):
        at = before + quarter * PLACES
        chosen = jnp.concatenate([chosen_ref[lane, at : at + PLACES, :] for lane in range(lanes)], axis=0).astype(bf16)
        columns = slice(quarter * LANES, (quarter + 1) * LANES)
        scores += lax.dot_general(chosen, high[:, columns], NT, preferred_element_type=f32)
        scores += lax.dot_general(chosen, low[:, columns], NT, preferred_element_type=f32)
    for place in range(out_ref.shape[0]):
        lane = place % lanes
        out_ref[place, :PLACES, :] = scores[lane * PLACES : (lane + 1) * PLACES]
        out_ref[place, PLACES:, :] = energy


def score_parts(parts, own, chosen, places):
    return pl.pallas_call(
        score_kernel,
        out_shape=[
            jax.ShapeDtypeStruct(own.shape, f32),
            jax.ShapeDtypeStruct((places, PLACES + 8, LANES), f32),
        ],
        compiler_params=params(),
        interpret=INTERPRET,
        name="score_parts",
    )(parts, own, chosen)


def finish_kernel(depth, parts_ref, out_ref, scale_ref):
    ys = scale_ref.shape[0]
    lanes = parts_ref.shape[0] // ys
    scores = []
    for y in range(ys):
        whole = parts_ref[y * lanes]
        for lane in range(1, lanes):
            whole += parts_ref[y * lanes + lane]
        scale = lax.rsqrt(whole[PLACES:] / depth + 1e-06)
        scale_ref[y] = scale
        scores.append(whole[:PLACES] * (scale[:1] / math.sqrt(depth)))
    scores = jnp.concatenate(scores, axis=0)
    size = jnp.abs(scores)
    code = jnp.floor((jnp.log2(jnp.maximum(size, 2.0**-LOWEST)) + LOWEST) * STEPS_PER_OCTAVE_OF_SCORES + 1.5)
    code = jnp.where(size < 2.0**-LOWEST, 0.0, jnp.minimum(code, 32767.0))
    code = jnp.where(scores < 0.0, -code, code).astype(i32).astype(i16)
    for place in range(out_ref.shape[0]):
        out_ref[place] = code


def finish_scores(parts, ys, zs, depth):
    return pl.pallas_call(
        functools.partial(finish_kernel, depth),
        out_shape=[
            jax.ShapeDtypeStruct((zs, ys * PLACES, LANES), i16),
            jax.ShapeDtypeStruct((ys, 8, LANES), f32),
        ],
        compiler_params=params(),
        interpret=INTERPRET,
        name="finish_scores",
    )(parts)


def pick_kernel(rows_ref, near_ref, far_ref, out_ref, table_ref):
    planes, count, _ = near_ref.shape
    for side, ref in enumerate((near_ref, far_ref)):
        for plane in range(planes):
            code = ref[plane].astype(i32).astype(f32)
            size = jnp.exp2((jnp.abs(code) - 1.0) / STEPS_PER_OCTAVE_OF_SCORES - LOWEST)
            at = (side * planes + plane) * count
            scores = jnp.where(code < 0.0, -size, size)
            table_ref[at : at + count, :] = jnp.where(code == 0.0, 0.0, scores)

    def step(i, carry):
        for cand in range(2):
            picked = []
            for one in range(GROUP):
                r = rows_ref[i * (2 * GROUP) + 2 * one + cand]
                picked.append(table_ref[pl.ds(r, 1), :])
            at = pl.ds(pl.multiple_of(i * GROUP, GROUP), GROUP)
            out_ref[at, cand * LANES : (cand + 1) * LANES] = jnp.concatenate(picked, axis=0)
        return carry

    lax.fori_loop(0, out_ref.shape[0] // GROUP, step, 0, unroll=8)


def pick_scores(rows, near, far):
    queries = rows.shape[0] // 2
    vmem = pl.BlockSpec(memory_space=pltpu.VMEM)
    planes, count, _ = near.shape
    return pl.pallas_call(
        pick_kernel,
        in_specs=[pl.BlockSpec(memory_space=pltpu.SMEM), vmem, vmem],
        out_specs=vmem,
        out_shape=jax.ShapeDtypeStruct((queries, 2 * LANES), f32),
        scratch_shapes=[pltpu.VMEM((2 * planes * count, LANES), f32)],
        compiler_params=params(),
        interpret=INTERPRET,
        name="pick_scores",
    )(rows, near, far)


def own_and_orders(descriptors, high, low, ys, halves):
    rows, width = descriptors.shape
    shards = 2 * ys
    count = halves * CORES
    groups = count // GROUP
    first = lax.axis_index("half") == 0

    def in_order(mine, other, axis):
        return jnp.stack([jnp.where(first, mine, other), jnp.where(first, other, mine)], axis=axis)

    def swap(value):
        return lax.ppermute(value, "half", [(0, 1), (1, 0)])

    pair = in_order(descriptors, swap(descriptors), 0).reshape(2 * rows, width)
    codes = jnp.concatenate([high.reshape(shards, -1), low.reshape(shards, -1)], axis=1).astype(bf16)
    codes = codes.reshape(ys, 2, -1)
    mine = jnp.where(first, codes[:, 0], codes[:, 1])
    other = swap(jnp.where(first, codes[:, 1], codes[:, 0]))
    codes = in_order(mine, other, 1)
    sent = jnp.pad(codes, ((0, 0), (0, PLACES - 2), (0, width - codes.shape[2])))
    sent = jnp.concatenate([jnp.broadcast_to(pair[None], (ys,) + pair.shape), sent], axis=1)
    own = exchange(sent, "y")
    codes = own[:, 2 * rows : 2 * rows + 2, : codes.shape[2]].astype(i32).reshape(shards, 2, groups, LANES)
    ahead_own = codes[:, 0] - 1
    ahead_src = jnp.where(ahead_own >= 0, lax.shift_right_logical(codes[:, 1], 1), -1)
    back = jnp.where(high > 0, (high - 1) * 256 + low, -1).astype(i32)
    back = back.reshape(shards, count, PLACES).transpose(1, 0, 2).reshape(count, 1, shards * PLACES)
    back = exchange(back, ("z", "core")).reshape(count, shards, PLACES)
    held = (back >= 0) & ((back & 1) == 1)
    back_src = jnp.where(held, lax.shift_right_logical(back, 8), -1)
    back_own = jnp.where(held, lax.shift_right_logical(back, 1) & (BLOCK - 1), -1)
    source = jnp.stack([ahead_src.reshape(shards, count, PLACES).transpose(1, 0, 2), back_src], axis=2)
    at = jnp.stack([ahead_own, back_own.transpose(1, 0, 2).reshape(shards, groups, LANES)], axis=1)
    at = at.reshape(2 * shards, groups, LANES).transpose(1, 0, 2).reshape(groups * 2 * shards, LANES)
    return own, source.reshape(count, 2 * shards * PLACES), at


def query_entries(queries, candidates, xs, ys, zs):
    flat = candidates.reshape(-1)
    order = jnp.arange(flat.shape[0], dtype=i32)
    earlier = (flat[:, None] == flat[None, :]) & (order[:, None] > order[None, :])
    rank = jnp.sum(earlier.astype(i32), axis=1)
    here = lax.axis_index(SHARD)
    hits = (flat == here)[None, :] & (rank[None, :] == jnp.arange(PLACES, dtype=i32)[:, None])
    hits = jnp.sum(hits.reshape(PLACES, -1, 2).astype(f32), axis=2).astype(bf16)
    chosen = jnp.dot(hits, queries, preferred_element_type=f32)
    chosen = chosen.reshape(PLACES, xs, -1, LANES).transpose(1, 2, 0, 3).reshape(xs, -1, LANES).astype(bf16)
    x = lax.axis_index("x")
    came = []
    for step in range(xs):
        piece = lax.dynamic_index_in_dim(chosen, lax.rem(x + step, xs), 0, keepdims=False)
        came.append(lax.ppermute(piece, "x", [(i, (i + step) % xs) for i in range(xs)]) if step else piece)
    came = jnp.stack([came[(xs - 1 - i) % xs] for i in range(2 * xs - 1)], axis=0)
    chosen = lax.dynamic_slice_in_dim(came, xs - 1 - x, xs, 0)
    plane = flat // CORES
    core = flat - plane * CORES
    far = (core != lax.axis_index("core")).astype(i32)
    y = plane // zs
    rows = ((far * zs + plane - y * zs) * ys + y) * PLACES + rank
    return chosen, rows


def per_device(descriptors, neighbours, owned, queries, candidates):
    ys, halves, xs = lax.axis_size("y"), lax.axis_size("z"), lax.axis_size("x")
    zs = 2 * halves
    rows, width = descriptors.shape
    everything = lax.all_gather(descriptors, ("z", "core"), axis=0, tiled=True)
    high, low = build_table(neighbours, owned, ys * zs * CORES, halves)
    own, source, at = own_and_orders(descriptors, high, low, ys, halves)
    chosen, score_rows = query_entries(queries, candidates, xs, ys, zs)
    source, at, own, chosen, score_rows = lax.optimization_barrier((source, at, own, chosen, score_rows))
    got, sims = similar_parts(everything, own, source, at)
    sims = spread(sims, "x", xs)
    parts = exchange(weighted_sums(got, sims, at), ("y", "half"))
    summed, parts = score_parts(parts, descriptors, chosen, ys * xs)
    mine, scales = finish_scores(exchange(parts, ("y", "x")), ys, zs, xs * width)
    scale = lax.dynamic_index_in_dim(scales, lax.axis_index("y"), 0, keepdims=False)[0]
    augmented = (summed * scale[:, None]).astype(bf16)
    near = exchange(mine, ("z", "half"))
    far = lax.ppermute(near, "core", [(0, 1), (1, 0)])
    return augmented, pick_scores(score_rows, near, far)


def solution(mesh):
    shards, lanes = mesh.devices.shape
    ys = GROUP // CORES
    devices = mesh.devices.reshape(ys, shards // GROUP // 2, 2, CORES, lanes)
    return jax.shard_map(
        per_device,
        mesh=Mesh(devices, SHARD + ("x",)),
        in_specs=(P(SHARD, "x"), P(SHARD, None), P(SHARD, None), P("x", None), P("x", None)),
        out_specs=(P(SHARD, "x"), P("x", None)),
        check_vma=False,
    )
```
